32 devices in a mesh: pipe: 2 (over x), expert: 16 (over z, y, core).
Axes of the slice: x: 2, y: 2, z: 4, core: 2. Of those that a mesh axis runs over, the one named last changes fastest.
Arguments:
- state: bfloat16 [16, 2, 128, 2048], P('expert', 'pipe'), may hold values from -24 to 24
- query: bfloat16 [16, 2, 128, 2048], P('expert', 'pipe'), may hold values from -8 to 8
- enc_kv: bfloat16 [16, 64, 2, 2048], P('expert', 'pipe'), may hold values from -4 to 4
- gain: float32 [2048], replicated, may hold values from 0.1 to 1.9
- w_in: bfloat16 [2048, 6144], P(None, 'expert'), may hold values from -0.125 to 0.125
- w_out: bfloat16 [6144, 2048], P('expert'), may hold values from -0.109375 to 0.109375
- expert_id: int32 [16, 2, 128], P('expert', 'pipe'), may hold values from 0 to 1
- slot: int32 [16, 2, 128], P('expert', 'pipe'), may hold values from -1 to 95, as said below
- gate: float32 [16, 2, 128], P('expert', 'pipe'), may hold values from 0.3 to 1
Outputs:
- output: bfloat16 [16, 2, 128, 2048], P('expert', 'pipe')
The draws below stay inside these ranges and needn't reach their ends.
Inputs may be any that keep to these rules, and one draw needn't show every extreme that they name: Within the 128 tokens of one source and sample, the tokens sent to one expert take slots 0, 1, 2, ... in token order until 96 are taken; later ones have slot -1. In every draw some expert is given 96 slotted tokens by every source and sample.
All inputs are finite; a program needn't handle non-finite values.
Results may differ from the reference program's by a relative error of at most 0.0055.
Values may be sent and summed in bfloat16 or wider, within the bound.
No kernel may reach another device: no remote copies, remote signals or barrier semaphores. Data moves between devices by JAX's collectives and lax.ppermute only.
A program may use at most 128 MiB of HBM per device.

```python
import math
import jax
import jax.numpy as jnp
from jax import lax

D = 2048
HEADS = 16
HD = 128
FF = 3072
WSPLIT = 8
TOK_DEV = 128
FF_DEV = 384
SOURCES = 16
SAMPLES = 2
SRC_LEN = 64
EXPERTS = 2
CAP = 96


def draw_state(key, part):
    full_shape = (SOURCES, SAMPLES, TOK_DEV, D)
    row_scale = jnp.exp(jax.random.uniform(jax.random.fold_in(key, 4), (SOURCES, SAMPLES, TOK_DEV, 1), jnp.float32, math.log(0.3), math.log(3.0)))
    column_scale = jnp.exp(jax.random.uniform(jax.random.fold_in(key, 5), (1, 1, 1, D), jnp.float32, math.log(0.3), math.log(3.0)))
    noise = jnp.clip(jax.random.normal(jax.random.fold_in(key, 6), full_shape, jnp.float32), -4.0, 4.0)
    return jnp.clip(noise * row_scale * column_scale, -24.0, 24.0).astype(jnp.bfloat16)


def draw_query(key, part):
    full_shape = (SOURCES, SAMPLES, TOK_DEV, D)
    values_base = 2.0 * jax.random.normal(jax.random.fold_in(key, 1), full_shape, jnp.float32)
    return jnp.clip(values_base, -8.0, 8.0).astype(jnp.bfloat16)


def draw_enc_kv(key, part):
    full_shape = (SOURCES, SRC_LEN, D)
    key_rows = jnp.clip(jax.random.normal(jax.random.fold_in(key, 2), full_shape, jnp.float32), -3.0, 3.0)
    value_rows = jnp.clip(jax.random.normal(jax.random.fold_in(key, 3), full_shape, jnp.float32), -4.0, 4.0)
    return jnp.stack([key_rows, value_rows], axis=2).astype(jnp.bfloat16)


def route_parts(key):
    block_shape = (SOURCES, SAMPLES, TOK_DEV)
    favored = jax.random.randint(jax.random.fold_in(key, 21), (), 0, EXPERTS)
    extra_count = jax.random.randint(jax.random.fold_in(key, 22), (SOURCES, SAMPLES, 1), 1, TOK_DEV // (4 * EXPERTS) + 1)
    scores = jax.random.randint(jax.random.fold_in(key, 23), block_shape, 0, 1048576) * TOK_DEV + jnp.arange(TOK_DEV, dtype=jnp.int32)
    rank_order = jnp.argsort(jnp.argsort(scores, axis=2), axis=2)
    others = jax.random.randint(jax.random.fold_in(key, 24), block_shape, 0, EXPERTS)
    expert_ids = jnp.where(rank_order < CAP + extra_count, favored, others).astype(jnp.int32)
    onehot = (expert_ids[..., None] == jnp.arange(EXPERTS, dtype=jnp.int32)).astype(jnp.int32)
    before = jnp.cumsum(onehot, axis=2) - onehot
    position = jnp.sum(before * onehot, axis=3)
    slot_ids = jnp.where(position < CAP, position, -1).astype(jnp.int32)
    return (expert_ids, slot_ids)


def draw_expert_id(key, part):
    return route_parts(key)[0]


def draw_slot(key, part):
    return route_parts(key)[1]


def steps_of(stream_key, extent, cuts, least, largest):
    level = 1.0
    for axis_at, parts in cuts:
        draws = jax.random.uniform(jax.random.fold_in(jax.random.fold_in(stream_key, 6), axis_at), (parts,), jnp.float32, least / len(cuts), largest / len(cuts))
        level = level * jnp.repeat(jnp.exp(draws), extent[axis_at] // parts).reshape((-1,) + (1,) * (len(extent) - 1 - axis_at))
    return level


def scatter_about(rng, shape, scale, limit, cuts=(), held_as=jnp.bfloat16):
    loudness = steps_of(rng, shape, cuts, -0.22, 0.18) if cuts else 1.0
    values = jax.random.normal(rng, shape, jnp.float32) * scale * loudness
    return jnp.minimum(jnp.maximum(values, -limit), limit).astype(held_as)


def setup_inputs(seed: int = 0) -> dict:
    arg_keys = jax.random.split(jax.random.key(seed), 10)
    return {
        "state": draw_state(jax.random.fold_in(arg_keys[9], 71), 0),
        "query": draw_query(jax.random.fold_in(arg_keys[9], 71), 0),
        "enc_kv": draw_enc_kv(jax.random.fold_in(arg_keys[9], 71), 0),
        "gain": jnp.clip(1.0 + 0.18 * jax.random.normal(arg_keys[3], (D,), jnp.float32), 0.1, 1.9),
        "w_in": scatter_about(arg_keys[4], (D, EXPERTS * FF), D ** -0.5, 0.125, ((1, 16),)),
        "w_out": scatter_about(arg_keys[5], (EXPERTS * FF, D), FF ** -0.5, 0.109375, ((0, 16),)),
        "expert_id": draw_expert_id(jax.random.fold_in(arg_keys[9], 71), 0),
        "slot": draw_slot(jax.random.fold_in(arg_keys[9], 71), 0),
        "gate": jnp.clip(0.3 + 0.7 * jax.random.uniform(arg_keys[8], (SOURCES, SAMPLES, TOK_DEV), jnp.float32) ** steps_of(arg_keys[8], (SOURCES, SAMPLES, TOK_DEV), ((0, 16), (1, 2)), -0.2, 0.2), 0.3, 1.0),
    }


def attend_source(inputs):
    query_block, kv_block = inputs
    samples, tokens, width = query_block.shape
    queries = query_block.astype(jnp.float32).reshape(samples, tokens, HEADS, HD)
    key_rows = kv_block[:, 0].astype(jnp.float32).reshape(-1, HEADS, HD)
    value_rows = kv_block[:, 1].astype(jnp.float32).reshape(-1, HEADS, HD)
    scores = jnp.einsum('pthd,lhd->phtl', queries, key_rows) * (1.0 / math.sqrt(HD))
    best_score = lax.optimization_barrier(jnp.max(scores, axis=3, keepdims=True))
    raised = jnp.exp(scores - best_score)
    denominator = lax.optimization_barrier(jnp.sum(raised, axis=3))
    rounded = lax.optimization_barrier(raised.astype(jnp.bfloat16)).astype(jnp.float32)
    mixed_heads = jnp.einsum('phtl,lhd->pthd', rounded, value_rows)
    mixed_heads = mixed_heads / jnp.transpose(denominator, (0, 2, 1))[..., None]
    return mixed_heads.reshape(samples, tokens, width)

def reference(state, query, enc_kv, gain, w_in, w_out, expert_id, slot, gate):
    attended = lax.map(attend_source, (query, enc_kv))
    hidden_state = state.astype(jnp.float32) + attended
    mean_square = lax.optimization_barrier(jnp.mean(hidden_state * hidden_state, axis=-1, keepdims=True))
    normed = (hidden_state * lax.rsqrt(mean_square + 1e-06) * gain).astype(jnp.bfloat16)
    sources, samples, tokens, width = state.shape
    flat_slot = jnp.where(slot >= 0, expert_id * CAP + slot, -1).astype(jnp.int32)
    slot_ids = jnp.arange(EXPERTS * CAP, dtype=jnp.int32)
    matches = flat_slot[:, :, None, :] == slot_ids[None, None, :, None]
    token_ids = jnp.arange(tokens, dtype=jnp.int32)
    token_of = lax.optimization_barrier(jnp.sum(jnp.where(matches, token_ids, 0), axis=3)).astype(jnp.int32)
    filled = jnp.any(matches, axis=3)
    source_ids = jnp.arange(sources, dtype=jnp.int32)[:, None, None]
    sample_ids = jnp.arange(samples, dtype=jnp.int32)[None, :, None]
    gathered = normed[source_ids, sample_ids, token_of]
    dispatched = jnp.where(filled[..., None], gathered, jnp.zeros((), jnp.bfloat16))
    per_expert = dispatched.reshape(sources, samples, EXPERTS, CAP, width)
    per_expert = jnp.transpose(per_expert, (2, 0, 1, 3, 4)).reshape(EXPERTS, sources * samples * CAP, width)

    def run_expert(inputs):
        expert_index, slot_rows = inputs
        total_out = jnp.zeros(slot_rows.shape, jnp.float32)
        for width_block in range(WSPLIT):
            column = (expert_index * FF + width_block * FF_DEV).astype(jnp.int32)
            in_block = lax.dynamic_slice_in_dim(w_in, column, FF_DEV, 1)
            out_block = lax.dynamic_slice_in_dim(w_out, column, FF_DEV, 0)
            activation = jnp.maximum(jnp.dot(slot_rows, in_block, preferred_element_type=jnp.float32), 0.0).astype(jnp.bfloat16)
            partial_value = jnp.dot(activation, out_block, preferred_element_type=jnp.float32).astype(jnp.bfloat16)
            total_out = total_out + partial_value.astype(jnp.float32)
        return total_out
    expert_out = lax.map(run_expert, (jnp.arange(EXPERTS, dtype=jnp.int32), per_expert))
    expert_out = expert_out.reshape(EXPERTS, sources, samples, CAP, width)
    picked = expert_out[expert_id, source_ids, sample_ids, jnp.maximum(slot, 0)]
    contribution = jnp.where((slot >= 0)[..., None], gate[..., None] * picked, jnp.float32(0.0))
    return (hidden_state + contribution).astype(jnp.bfloat16)
```

```python
import functools
import math

import jax
import jax.numpy as jnp
from jax import lax
from jax.experimental import pallas as pl
from jax.experimental.pallas import tpu as pltpu
from jax.sharding import PartitionSpec as P

HEADS = 16
HD = 128
WSPLIT = 8
EPS = 1e-06
VMEM_LIMIT = 48 * 1024 * 1024

VMEM = pl.BlockSpec(memory_space=pltpu.VMEM)
ANY = pl.BlockSpec(memory_space=pl.ANY)


def params():
    return pltpu.CompilerParams(vmem_limit_bytes=VMEM_LIMIT)


def attend_kernel(pieces, groups, cap, *refs):
    state_ref, query_ref, gain_ref, flat_ref = refs[:4]
    kv_refs = refs[4 : 4 + pieces]
    hidden_ref = refs[4 + pieces]
    packed_refs = refs[5 + pieces :]
    tokens, width = state_ref.shape
    half = width // 2
    local = kv_refs[0].shape[0] // 2
    scale = 1.0 / math.sqrt(HD)
    squares = jnp.zeros((tokens, HD), jnp.float32)
    for head in range(HEADS):
        cols = slice(head * HD, (head + 1) * HD)
        keys = jnp.concatenate([r[:local, cols] for r in kv_refs], axis=0)
        values = jnp.concatenate([r[local:, cols] for r in kv_refs], axis=0)
        scores = (
            lax.dot_general(
                query_ref[:, cols],
                keys,
                (((1,), (1,)), ((), ())),
                preferred_element_type=jnp.float32,
            )
            * scale
        )
        raised = jnp.exp(scores - jnp.max(scores, axis=1, keepdims=True))
        total = jnp.sum(raised, axis=1, keepdims=True)
        mixed = jnp.dot(raised.astype(jnp.bfloat16), values, preferred_element_type=jnp.float32)
        hidden = state_ref[:, cols].astype(jnp.float32) + mixed / total
        hidden_ref[:, cols] = hidden
        squares = squares + hidden * hidden
    mean_square = jnp.sum(squares, axis=1, keepdims=True) * (1.0 / width)
    inverse = lax.rsqrt(mean_square + EPS)
    rows = lax.broadcasted_iota(jnp.int32, (groups * cap, tokens), 0)
    selector = (rows == flat_ref[...]).astype(jnp.float32).astype(jnp.bfloat16)
    step = 512
    for at in range(0, width, step):
        cols = slice(at, at + step)
        normed = (hidden_ref[:, cols] * inverse * gain_ref[:, cols]).astype(jnp.bfloat16)
        packed = jnp.dot(selector, normed, preferred_element_type=jnp.float32).astype(jnp.bfloat16)
        side, inner = divmod(at, half)
        for group in range(groups):
            packed_refs[2 * group + side][:, inner : inner + step] = packed[
                group * cap : (group + 1) * cap
            ]


def attend(state, query, gain, flat, kv_pieces, groups, cap):
    tokens, width = state.shape
    half = width // 2
    outs = [jax.ShapeDtypeStruct((tokens, width), jnp.float32)]
    outs += [jax.ShapeDtypeStruct((cap, half), jnp.bfloat16)] * (2 * groups)
    pieces = len(kv_pieces)
    return pl.pallas_call(
        functools.partial(attend_kernel, pieces, groups, cap),
        out_shape=outs,
        in_specs=[VMEM] * (4 + pieces),
        out_specs=[VMEM] * len(outs),
        compiler_params=params(),
        cost_estimate=pl.CostEstimate(
            flops=4 * tokens * pieces * kv_pieces[0].shape[0] * width,
            bytes_accessed=12 * tokens * width,
            transcendentals=tokens * 64 * HEADS,
        ),
        name="attend",
    )(state, query, gain, flat, *kv_pieces)


def ffn_kernel(*refs):
    blocks = refs[:8]
    weights = refs[8:12]
    own_ref, z0_ref, y1_ref, y0_ref, z1_ref = refs[12:17]
    held = refs[17:21]
    sems = refs[21]
    copies = [
        pltpu.make_async_copy(source, target, sems.at[i])
        for i, (source, target) in enumerate(zip(weights, held))
    ]
    for copy in copies:
        copy.start()
    rows, half = blocks[0].shape
    left = jnp.concatenate([blocks[2 * i][...] for i in range(4)], axis=0)
    right = jnp.concatenate([blocks[2 * i + 1][...] for i in range(4)], axis=0)
    entries = jnp.concatenate([left, right], axis=1)
    activations = []
    for i in range(2):
        copies[i].wait()
        raw = jnp.dot(entries, held[i][...], preferred_element_type=jnp.float32)
        activations.append(jnp.maximum(raw, 0.0).astype(jnp.bfloat16))
    copies[2].wait()
    copies[3].wait()
    step = 512
    for at in range(0, 2 * half, step):
        cols = slice(at, at + step)
        part = jnp.dot(activations[0], held[2][:, cols], preferred_element_type=jnp.float32)
        part = part + jnp.dot(activations[1], held[3][:, cols], preferred_element_type=jnp.float32)
        part = part.astype(jnp.bfloat16)
        own_ref[:, cols] = part[:rows]
        y_part, z_part, d_part = (part[i * rows : (i + 1) * rows] for i in (1, 2, 3))
        side, inner = divmod(at, half)
        cols = slice(inner, inner + step)
        if side == 0:
            y0_ref[:, cols] = y_part
            z0_ref[0, :, cols] = z_part
            z0_ref[1, :, cols] = d_part
        else:
            z1_ref[:, cols] = z_part
            y1_ref[0, :, cols] = y_part
            y1_ref[1, :, cols] = d_part


def ffn(blocks, weights):
    rows, half = blocks[0].shape
    width = 2 * half
    units = weights[0].shape[1]
    one = jax.ShapeDtypeStruct((rows, half), jnp.bfloat16)
    two = jax.ShapeDtypeStruct((2, rows, half), jnp.bfloat16)
    return pl.pallas_call(
        ffn_kernel,
        out_shape=[jax.ShapeDtypeStruct((rows, width), jnp.bfloat16), two, two, one, one],
        in_specs=[VMEM] * 8 + [ANY] * 4,
        out_specs=[VMEM] * 5,
        scratch_shapes=[pltpu.VMEM(w.shape, w.dtype) for w in weights]
        + [pltpu.SemaphoreType.DMA((4,))],
        compiler_params=params(),
        cost_estimate=pl.CostEstimate(
            flops=4 * 4 * rows * width * units * 2,
            bytes_accessed=8 * units * width + 16 * rows * width,
            transcendentals=0,
        ),
        name="expert_ffn",
    )(*blocks, *weights)


def finish_kernel(groups, cap, *refs):
    hidden_ref, gate_ref, flat_ref, own_ref, az_ref, ay_ref, by_ref, bz_ref = refs[:8]
    back_refs = refs[8:-1]
    out_ref = refs[-1]
    tokens, width = hidden_ref.shape
    half = width // 2
    flat = flat_ref[...]

    def picker(group):
        slots = lax.broadcasted_iota(jnp.int32, (tokens, cap), 1) + group * cap
        return (slots == flat).astype(jnp.float32).astype(jnp.bfloat16)

    pickers = [picker(group) for group in range(groups)]
    step = 512
    for at in range(0, width, step):
        side, inner = divmod(at, half)
        whole = slice(at, at + step)
        part = slice(inner, inner + step)
        first, second = (az_ref, by_ref) if side == 0 else (ay_ref, bz_ref)
        added = (
            own_ref[:, whole].astype(jnp.float32)
            + first[0, :, part].astype(jnp.float32)
            + second[:, part].astype(jnp.float32)
        )
        coarse = added.astype(jnp.bfloat16)
        fine = (added - coarse.astype(jnp.float32)).astype(jnp.bfloat16)
        picked = jnp.dot(pickers[0], coarse, preferred_element_type=jnp.float32)
        picked = picked + jnp.dot(pickers[0], fine, preferred_element_type=jnp.float32)
        for group in range(1, groups):
            picked = picked + jnp.dot(
                pickers[group], back_refs[group - 1][:, whole], preferred_element_type=jnp.float32
            )
        out_ref[:, whole] = (hidden_ref[:, whole] + gate_ref[...] * picked).astype(jnp.bfloat16)


def finish(hidden, gate, flat, own, pieces, backs, groups, cap):
    tokens, width = hidden.shape
    operands = [hidden, gate, flat, own, *pieces, *backs]
    return pl.pallas_call(
        functools.partial(finish_kernel, groups, cap),
        out_shape=jax.ShapeDtypeStruct((tokens, width), jnp.bfloat16),
        in_specs=[VMEM] * len(operands),
        out_specs=VMEM,
        compiler_params=params(),
        cost_estimate=pl.CostEstimate(
            flops=4 * tokens * cap * (groups + 1) * width,
            bytes_accessed=16 * tokens * width,
            transcendentals=0,
        ),
        name="finish",
    )(*operands)


def body(state, query, enc_kv, gain, w_in, w_out, expert_id, slot, gate):
    tokens, width = state.shape[2:]
    devices = lax.axis_size("expert")
    pipes = lax.axis_size("pipe")
    groups = devices // WSPLIT
    cap = 3 * tokens // (2 * groups)
    half = width // 2

    def across(value, bit):
        return lax.ppermute(value, "expert", [(i, i ^ bit) for i in range(devices)])

    def groups_on(value, count):
        shift = count * WSPLIT
        return lax.ppermute(value, "expert", [(i, (i + shift) % devices) for i in range(devices)])

    kv = jnp.transpose(enc_kv[0], (1, 0, 2)).reshape(-1, width)
    kv_pieces = [kv]
    for shift in range(1, pipes):
        perm = [(i, (i + shift) % pipes) for i in range(pipes)]
        kv_pieces.append(lax.ppermute(kv, "pipe", perm))
    weights = [w_in, across(w_in, 1), w_out, across(w_out, 1)]

    group = lax.axis_index("expert") // WSPLIT
    offset = (expert_id[0, 0] - group) % groups
    flat = jnp.where(slot[0, 0] >= 0, offset * cap + slot[0, 0], -1)

    hidden, *packed = attend(
        state[0, 0],
        query[0, 0],
        gain.reshape(1, width),
        flat.reshape(1, tokens),
        kv_pieces,
        groups,
        cap,
    )
    near = packed[:2]
    far = [[], []]
    for count in range(1, groups):
        for side in range(2):
            far[side].append(groups_on(packed[2 * count + side], count))
    far = [jnp.concatenate(side, axis=0) if len(side) > 1 else side[0] for side in far]

    def spread(zero, one):
        y0, z0 = across(zero, 2), across(zero, 4)
        y1, z1 = across(one, 2), across(one, 4)
        d0, d1 = across(y0, 4), across(z1, 2)
        return [zero, one, y0, y1, z0, z1, d0, d1]

    def gather_sums(own, z0, y1, y0, z1):
        from_z, from_y = across(z0, 4), across(y1, 2)
        on_y = (y0.astype(jnp.float32) + from_z[1].astype(jnp.float32)).astype(jnp.bfloat16)
        on_z = (z1.astype(jnp.float32) + from_y[1].astype(jnp.float32)).astype(jnp.bfloat16)
        return own, from_z, from_y, across(on_y, 2), across(on_z, 4)

    near_sums = gather_sums(*ffn(spread(*near), weights))
    own, from_z, from_y, last_y, last_z = gather_sums(*ffn(spread(*far), weights))
    own = own.astype(jnp.float32)
    far_sum = jnp.concatenate(
        [
            own[:, :half] + from_z[0].astype(jnp.float32) + last_y.astype(jnp.float32),
            own[:, half:] + from_y[0].astype(jnp.float32) + last_z.astype(jnp.float32),
        ],
        axis=1,
    ).astype(jnp.bfloat16)
    backs = [
        groups_on(far_sum[(count - 1) * cap : count * cap], groups - count)
        for count in range(1, groups)
    ]
    output = finish(
        hidden,
        gate[0, 0].reshape(tokens, 1),
        flat.reshape(tokens, 1),
        near_sums[0],
        near_sums[1:],
        backs,
        groups,
        cap,
    )
    return output.reshape(1, 1, tokens, width)


def solution(mesh):
    return jax.shard_map(
        body,
        mesh=mesh,
        in_specs=(
            P("expert", "pipe", None, None),
            P("expert", "pipe", None, None),
            P("expert", "pipe", None, None),
            P(),
            P(None, "expert"),
            P("expert", None),
            P("expert", "pipe", None),
            P("expert", "pipe", None),
            P("expert", "pipe", None),
        ),
        out_specs=P("expert", "pipe", None, None),
        check_vma=False,
    )
```

```python
import functools
import math

import jax
import jax.numpy as jnp
from jax import lax
from jax.experimental import pallas as pl
from jax.experimental.pallas import tpu as pltpu
from jax.sharding import PartitionSpec as P

HEADS = 16
HD = 128
WSPLIT = 8
EPS = 1e-06
VMEM_LIMIT = 32 * 1024 * 1024

VMEM = pl.BlockSpec(memory_space=pltpu.VMEM)
SMEM = pl.BlockSpec(memory_space=pltpu.SMEM)
ANY = pl.BlockSpec(memory_space=pl.ANY)


def struct(shape, dtype=jnp.bfloat16):
    return jax.ShapeDtypeStruct(shape, dtype)


def call(
    kernel, outs, in_specs, name, flops, moved, out_specs=None, aliases=None
):
    return pl.pallas_call(
        kernel,
        out_shape=outs,
        in_specs=in_specs,
        out_specs=out_specs or jax.tree.map(lambda _: VMEM, outs),
        input_output_aliases=aliases or {},
        compiler_params=pltpu.CompilerParams(vmem_limit_bytes=VMEM_LIMIT),
        cost_estimate=pl.CostEstimate(flops=flops, bytes_accessed=moved, transcendentals=0),
        name=name,
    )


def as_column(row):
    count = row.shape[1]
    down = lax.broadcasted_iota(jnp.int32, (count, count), 0)
    along = lax.broadcasted_iota(jnp.int32, (count, count), 1)
    return jnp.sum(jnp.where(down == along, row, jnp.zeros_like(row)), axis=1, keepdims=True)


def stage_kernel(groups, cap, *refs):
    group_ref, state_in, query_in, gain_in, expert_ref, slot_ref, gate_ref = refs[:7]
    state_out, query_out, gain_out, flat_row, flat_column, gate_column = refs[7:]
    state_out[...] = state_in[...]
    query_out[...] = query_in[...]
    gain_out[...] = gain_in[...]
    offset = expert_ref[...] - group_ref[0]
    offset = jnp.where(offset < 0, offset + groups, offset)
    slot = slot_ref[...]
    flat = jnp.where(slot >= 0, offset * cap + slot, -1)
    flat_row[...] = flat
    flat_column[...] = as_column(flat)
    gate_column[...] = as_column(gate_ref[...])


def stage(group, state, query, gain, expert_id, slot, gate, groups, cap):
    tokens, width = state.shape
    outs = [
        struct((tokens, width)),
        struct((tokens, width)),
        struct((1, width), jnp.float32),
        struct((1, tokens), jnp.int32),
        struct((tokens, 1), jnp.int32),
        struct((tokens, 1), jnp.float32),
    ]
    return call(
        functools.partial(stage_kernel, groups, cap),
        outs,
        [SMEM] + [VMEM] * 6,
        "stage",
        tokens * tokens,
        8 * tokens * width,
    )(group, state, query, gain, expert_id, slot, gate)


def gate_kernel(*refs):
    pass


def after_all(value, others):
    return call(
        gate_kernel,
        struct(value.shape),
        [ANY] * (1 + len(others)),
        "hand_on",
        1,
        1,
        out_specs=ANY,
        aliases={0: 0},
    )(value, *others)


def attend_kernel(pieces, groups, cap, *refs):
    state_ref, query_ref, gain_ref, flat_ref = refs[:4]
    kv_refs = refs[4 : 4 + pieces]
    hidden_ref = refs[-1 - groups]
    packed_refs = refs[-groups:]
    tokens, width = state_ref.shape
    local = kv_refs[0].shape[0] // 2
    scale = 1.0 / math.sqrt(HD)
    squares = jnp.zeros((tokens, HD), jnp.float32)
    for head in range(HEADS):
        cols = slice(head * HD, (head + 1) * HD)
        keys = jnp.concatenate([r[:local, cols] for r in kv_refs], axis=0)
        values = jnp.concatenate([r[local:, cols] for r in kv_refs], axis=0)
        scores = (
            lax.dot_general(
                query_ref[:, cols],
                keys,
                (((1,), (1,)), ((), ())),
                preferred_element_type=jnp.float32,
            )
            * scale
        )
        raised = jnp.exp(scores - jnp.max(scores, axis=1, keepdims=True))
        total = jnp.sum(raised, axis=1, keepdims=True)
        mixed = jnp.dot(raised.astype(jnp.bfloat16), values, preferred_element_type=jnp.float32)
        hidden = state_ref[:, cols].astype(jnp.float32) + mixed / total
        hidden_ref[:, cols] = hidden
        squares = squares + hidden * hidden
    mean_square = jnp.sum(squares, axis=1, keepdims=True) * (1.0 / width)
    inverse = lax.rsqrt(mean_square + EPS)
    rows = lax.broadcasted_iota(jnp.int32, (groups * cap, tokens), 0)
    selector = (rows == flat_ref[...]).astype(jnp.float32).astype(jnp.bfloat16)
    step = 512
    for at in range(0, width, step):
        cols = slice(at, at + step)
        normed = (hidden_ref[:, cols] * inverse * gain_ref[:, cols]).astype(jnp.bfloat16)
        packed = jnp.dot(selector, normed, preferred_element_type=jnp.float32).astype(jnp.bfloat16)
        for group in range(groups):
            packed_refs[group][:, cols] = packed[group * cap : (group + 1) * cap]


def attend(state, query, gain, flat, kv_pieces, groups, cap, after):
    tokens, width = state.shape
    outs = [struct((tokens, width), jnp.float32)] + [struct((cap, width))] * groups
    pieces = len(kv_pieces)
    return call(
        functools.partial(attend_kernel, pieces, groups, cap),
        outs,
        [VMEM] * (4 + pieces) + [ANY] * len(after),
        "attend",
        4 * tokens * pieces * kv_pieces[0].shape[0] * width,
        12 * tokens * width,
    )(state, query, gain, flat, *kv_pieces, *after)


def ffn_kernel(parts, cut, *refs):
    own_in, y_in, z_in = refs[:3]
    d_in = refs[3 : 3 + parts]
    in_a, in_b, out_a, out_b = refs[3 + parts : 7 + parts]
    own_ref, z0_ref, y1_ref, y0_ref, z1_ref = refs[-5:]
    rows, width = own_in.shape
    diagonal = jnp.concatenate([r[...] for r in d_in], axis=1)
    entries = jnp.concatenate([own_in[...], y_in[...], z_in[...], diagonal], axis=0)
    w_in = jnp.concatenate([in_a[...], in_b[...]], axis=1)
    raw = jnp.dot(entries, w_in, preferred_element_type=jnp.float32)
    activation = jnp.maximum(raw, 0.0).astype(jnp.bfloat16)
    step = 512
    for at in range(0, width, step):
        cols = slice(at, at + step)
        w_out = jnp.concatenate([out_a[:, cols], out_b[:, cols]], axis=0)
        part = jnp.dot(activation, w_out, preferred_element_type=jnp.float32)
        part = part.astype(jnp.bfloat16)
        own_ref[:, cols] = part[:rows]
        y_part, z_part, d_part = (part[i * rows : (i + 1) * rows] for i in (1, 2, 3))
        if at < cut:
            y0_ref[:, cols] = y_part
            z0_ref[0, :, cols] = z_part
            z0_ref[1, :, cols] = d_part
        else:
            cols = slice(at - cut, at - cut + step)
            z1_ref[:, cols] = z_part
            y1_ref[0, :, cols] = y_part
            y1_ref[1, :, cols] = d_part


def ffn(blocks, weights, cut, after=()):
    rows, width = blocks[0].shape
    units = weights[0].shape[1]
    rest = width - cut
    outs = [
        struct((rows, width)),
        struct((2, rows, cut)),
        struct((2, rows, rest)),
        struct((rows, cut)),
        struct((rows, rest)),
    ]
    return call(
        functools.partial(ffn_kernel, len(blocks) - 3, cut),
        outs,
        [VMEM] * (len(blocks) + 4) + [ANY] * len(after),
        "expert_ffn",
        4 * 4 * rows * width * units * 2,
        8 * units * width + 16 * rows * width,
    )(*blocks, *weights, *after)


def first_kernel(y0_ref, az_ref, z1_ref, ay_ref, *refs):
    y_ref, z_ref = refs[-2:]
    for own, other, out in ((y0_ref, az_ref, y_ref), (z1_ref, ay_ref, z_ref)):
        out[...] = (own[...].astype(jnp.float32) + other[1].astype(jnp.float32)).astype(jnp.bfloat16)


def first_step(y0, from_z, z1, from_y, after=()):
    return call(
        first_kernel,
        [struct(y0.shape), struct(z1.shape)],
        [VMEM] * 4 + [ANY] * len(after),
        "first_step",
        y0.size + z1.size,
        6 * (y0.size + z1.size),
    )(y0, from_z, z1, from_y, *after)


def total_kernel(cut, *refs):
    own_ref, az_ref, ay_ref, by_ref, bz_ref = refs[:5]
    out_ref = refs[7]
    for first, second, cols in (
        (az_ref, by_ref, slice(0, cut)),
        (ay_ref, bz_ref, slice(cut, out_ref.shape[1])),
    ):
        out_ref[:, cols] = (
            own_ref[:, cols].astype(jnp.float32)
            + first[0].astype(jnp.float32)
            + second[...].astype(jnp.float32)
        ).astype(jnp.bfloat16)


def total(sums, cut, held):
    rows, width = sums[0].shape
    outs = [struct((rows, width))] + [struct(value.shape) for value in held]
    return call(
        functools.partial(total_kernel, cut),
        outs,
        [VMEM] * 5 + [ANY] * len(held),
        "far_total",
        3 * rows * width,
        8 * rows * width,
        out_specs=[VMEM] + [ANY] * len(held),
        aliases={5 + i: 1 + i for i in range(len(held))},
    )(*sums, *held)


def finish_kernel(groups, cap, cut, *refs):
    hidden_ref, gate_ref, flat_ref, own_ref, az_ref, ay_ref, by_ref, bz_ref = refs[:8]
    back_refs = refs[8:-1]
    out_ref = refs[-1]
    tokens, width = hidden_ref.shape
    flat = flat_ref[...]

    def picker(group):
        slots = lax.broadcasted_iota(jnp.int32, (tokens, cap), 1) + group * cap
        return (slots == flat).astype(jnp.float32).astype(jnp.bfloat16)

    pickers = [picker(group) for group in range(groups)]
    step = 512
    for at in range(0, width, step):
        whole = slice(at, at + step)
        inner = at if at < cut else at - cut
        part = slice(inner, inner + step)
        first, second = (az_ref, by_ref) if at < cut else (ay_ref, bz_ref)
        added = (
            own_ref[:, whole].astype(jnp.float32)
            + first[0, :, part].astype(jnp.float32)
            + second[:, part].astype(jnp.float32)
        )
        coarse = added.astype(jnp.bfloat16)
        fine = (added - coarse.astype(jnp.float32)).astype(jnp.bfloat16)
        picked = jnp.dot(pickers[0], coarse, preferred_element_type=jnp.float32)
        picked = picked + jnp.dot(pickers[0], fine, preferred_element_type=jnp.float32)
        for group in range(1, groups):
            picked = picked + jnp.dot(
                pickers[group], back_refs[group - 1][:, whole], preferred_element_type=jnp.float32
            )
        out_ref[:, whole] = (hidden_ref[:, whole] + gate_ref[...] * picked).astype(jnp.bfloat16)


def finish(hidden, gate, flat, sums, backs, groups, cap, cut):
    tokens, width = hidden.shape
    operands = [hidden, gate, flat, *sums, *backs]
    return call(
        functools.partial(finish_kernel, groups, cap, cut),
        struct((tokens, width)),
        [VMEM] * len(operands),
        "finish",
        4 * tokens * cap * (groups + 1) * width,
        16 * tokens * width,
    )(*operands)


def body(state, query, enc_kv, gain, w_in, w_out, expert_id, slot, gate):
    tokens, width = state.shape[2:]
    devices = lax.axis_size("expert")
    pipes = lax.axis_size("pipe")
    groups = devices // WSPLIT
    cap = 3 * tokens // (2 * groups)
    far_cut, near_cut = width // 2, width // 4

    def across(value, bit):
        return lax.ppermute(value, "expert", [(i, i ^ bit) for i in range(devices)])

    def groups_on(value, count):
        shift = count * WSPLIT
        return lax.ppermute(value, "expert", [(i, (i + shift) % devices) for i in range(devices)])

    kv = jnp.transpose(enc_kv[0], (1, 0, 2)).reshape(-1, width)
    kv_pieces = [kv]
    for shift in range(1, pipes):
        perm = [(i, (i + shift) % pipes) for i in range(pipes)]
        kv_pieces.append(lax.ppermute(kv, "pipe", perm))
    weights = [w_in, across(w_in, 1), w_out, across(w_out, 1)]

    group = (lax.axis_index("expert") // WSPLIT).astype(jnp.int32).reshape(1)
    staged = stage(
        group,
        state[0, 0],
        query[0, 0],
        gain.reshape(1, width),
        expert_id[0],
        slot[0],
        gate[0],
        groups,
        cap,
    )
    flat, gates = staged[4:]
    hidden, near, *packed = attend(
        *staged[:4], kv_pieces, groups, cap, after=[weights[1], weights[3]]
    )
    far = [groups_on(block, count) for count, block in enumerate(packed, 1)]
    far = jnp.concatenate(far, axis=0) if len(far) > 1 else far[0]

    near_y, near_z = across(near, 2), across(near, 4)
    near_blocks = [near, near_y, near_z, across(near_z, 2)]
    far = after_all(far, [near_y, near_z])
    far_y, far_z = across(far, 2), across(far, 4)
    far_blocks = [
        far,
        far_y,
        far_z,
        across(far_y[:, :far_cut], 4),
        across(far_z[:, far_cut:], 2),
    ]

    def first_sums(own, z0, y1, y0, z1, after=()):
        from_z, from_y = across(z0, 4), across(y1, 2)
        return own, from_z, from_y, *first_step(y0, from_z, z1, from_y, after)

    def last_sums(own, from_z, from_y, on_y, on_z):
        return own, from_z, from_y, across(on_y, 2), across(on_z, 4)

    far_parts = ffn(far_blocks, weights, far_cut)
    near_parts = ffn(near_blocks, weights, near_cut, after=far_parts[3:])
    far_sum, *held = total(
        last_sums(*first_sums(*far_parts, after=near_parts[3:])), far_cut, near_parts[1:3]
    )
    backs = [
        groups_on(far_sum[(count - 1) * cap : count * cap], groups - count)
        for count in range(1, groups)
    ]
    near_sums = last_sums(*first_sums(near_parts[0], *held, *near_parts[3:]))
    output = finish(hidden, gates, flat, near_sums, backs, groups, cap, near_cut)
    return output.reshape(1, 1, tokens, width)


def solution(mesh):
    return jax.shard_map(
        body,
        mesh=mesh,
        in_specs=(
            P("expert", "pipe", None, None),
            P("expert", "pipe", None, None),
            P("expert", "pipe", None, None),
            P(),
            P(None, "expert"),
            P("expert", None),
            P("expert", "pipe", None),
            P("expert", "pipe", None),
            P("expert", "pipe", None),
        ),
        out_specs=P("expert", "pipe", None, None),
        check_vma=False,
    )
```

```python
import functools
import math

import jax
import jax.numpy as jnp
from jax import lax
from jax.experimental import pallas as pl
from jax.experimental.pallas import tpu as pltpu
from jax.sharding import PartitionSpec as P

HEADS = 16
HD = 128
WSPLIT = 8
EPS = 1e-06
VMEM_LIMIT = 32 * 1024 * 1024

VMEM = pl.BlockSpec(memory_space=pltpu.VMEM)
SMEM = pl.BlockSpec(memory_space=pltpu.SMEM)
ANY = pl.BlockSpec(memory_space=pl.ANY)


def struct(shape, dtype=jnp.bfloat16):
    return jax.ShapeDtypeStruct(shape, dtype)


def call(
    kernel, outs, in_specs, name, flops, moved, out_specs=None, aliases=None
):
    return pl.pallas_call(
        kernel,
        out_shape=outs,
        in_specs=in_specs,
        out_specs=out_specs or jax.tree.map(lambda _: VMEM, outs),
        input_output_aliases=aliases or {},
        compiler_params=pltpu.CompilerParams(vmem_limit_bytes=VMEM_LIMIT),
        cost_estimate=pl.CostEstimate(flops=flops, bytes_accessed=moved, transcendentals=0),
        name=name,
    )


def as_column(row):
    count = row.shape[1]
    down = lax.broadcasted_iota(jnp.int32, (count, count), 0)
    along = lax.broadcasted_iota(jnp.int32, (count, count), 1)
    return jnp.sum(jnp.where(down == along, row, jnp.zeros_like(row)), axis=1, keepdims=True)


def stage_kernel(groups, cap, *refs):
    group_ref, state_in, query_in, gain_in, expert_ref, slot_ref, gate_ref = refs[:7]
    state_out, query_out, gain_out, flat_row, flat_column, gate_column = refs[7:]
    state_out[...] = state_in[...]
    query_out[...] = query_in[...]
    gain_out[...] = gain_in[...]
    offset = expert_ref[...] - group_ref[0]
    offset = jnp.where(offset < 0, offset + groups, offset)
    slot = slot_ref[...]
    flat = jnp.where(slot >= 0, offset * cap + slot, -1)
    flat_row[...] = flat
    flat_column[...] = as_column(flat)
    gate_column[...] = as_column(gate_ref[...])


def stage(group, state, query, gain, expert_id, slot, gate, groups, cap):
    tokens, width = state.shape
    outs = [
        struct((tokens, width)),
        struct((tokens, width)),
        struct((1, width), jnp.float32),
        struct((1, tokens), jnp.int32),
        struct((tokens, 1), jnp.int32),
        struct((tokens, 1), jnp.float32),
    ]
    return call(
        functools.partial(stage_kernel, groups, cap),
        outs,
        [SMEM] + [VMEM] * 6,
        "stage",
        tokens * tokens,
        8 * tokens * width,
    )(group, state, query, gain, expert_id, slot, gate)


def gate_kernel(*refs):
    pass


def after_all(values, others):
    return call(
        gate_kernel,
        [struct(value.shape) for value in values],
        [ANY] * (len(values) + len(others)),
        "hand_on",
        1,
        1,
        out_specs=[ANY] * len(values),
        aliases={i: i for i in range(len(values))},
    )(*values, *others)


def attend_kernel(pieces, groups, cap, first, *refs):
    state_ref, query_ref, gain_ref, flat_ref = refs[:4]
    kv_refs = refs[4 : 4 + pieces]
    hidden_ref, squares_ref = refs[-2 - groups : -groups]
    packed_refs = refs[-groups:]
    tokens, width = hidden_ref.shape
    local = kv_refs[0].shape[0] // 2
    scale = 1.0 / math.sqrt(HD)
    squares = jnp.zeros((tokens, HD), jnp.float32)
    rows = lax.broadcasted_iota(jnp.int32, (groups * cap, tokens), 0)
    selector = (rows == flat_ref[...]).astype(jnp.float32).astype(jnp.bfloat16)
    step = 256
    for at in range(0, width, HD):
        cols = slice(at, at + HD)
        whole = slice(first + at, first + at + HD)
        keys = jnp.concatenate([r[:local, cols] for r in kv_refs], axis=0)
        values = jnp.concatenate([r[local:, cols] for r in kv_refs], axis=0)
        scores = (
            lax.dot_general(
                query_ref[:, whole],
                keys,
                (((1,), (1,)), ((), ())),
                preferred_element_type=jnp.float32,
            )
            * scale
        )
        raised = jnp.exp(scores - jnp.max(scores, axis=1, keepdims=True))
        total = jnp.sum(raised, axis=1, keepdims=True)
        mixed = jnp.dot(raised.astype(jnp.bfloat16), values, preferred_element_type=jnp.float32)
        hidden = state_ref[:, whole].astype(jnp.float32) + mixed / total
        hidden_ref[:, cols] = hidden
        squares = squares + hidden * hidden
        done = at + HD
        if done % step == 0:
            cols = slice(done - step, done)
            gained = hidden_ref[:, cols] * gain_ref[:, first + done - step : first + done]
            packed = jnp.dot(
                selector, gained.astype(jnp.bfloat16), preferred_element_type=jnp.float32
            ).astype(jnp.bfloat16)
            for group in range(groups):
                packed_refs[group][:, cols] = packed[group * cap : (group + 1) * cap]
    squares_ref[...] = squares


def attend(state, query, gain, flat, kv_pieces, groups, cap, first, after=()):
    tokens = state.shape[0]
    width = kv_pieces[0].shape[1]
    outs = [struct((tokens, width), jnp.float32), struct((tokens, HD), jnp.float32)]
    outs += [struct((cap, width))] * groups
    pieces = len(kv_pieces)
    return call(
        functools.partial(attend_kernel, pieces, groups, cap, first),
        outs,
        [VMEM] * (4 + pieces) + [ANY] * len(after),
        "attend",
        4 * tokens * pieces * kv_pieces[0].shape[0] * width,
        12 * tokens * width,
    )(state, query, gain, flat, *kv_pieces, *after)


def ffn_kernel(cut, *refs):
    in_a, in_b, out_a, out_b = refs[8:12]
    own_ref, z0_ref, y1_ref, y0_ref, z1_ref = refs[-5:]
    rows, half = refs[0].shape
    width = 2 * half
    w_in = jnp.concatenate([in_a[...], in_b[...]], axis=1)
    left = jnp.concatenate([r[...] for r in refs[:4]], axis=0)
    right = jnp.concatenate([r[...] for r in refs[4:8]], axis=0)
    entries = jnp.concatenate([left, right], axis=1)
    raw = jnp.dot(entries, w_in, preferred_element_type=jnp.float32)
    activation = jnp.maximum(raw, 0.0).astype(jnp.bfloat16)
    step = 512
    for at in range(0, width, step):
        cols = slice(at, at + step)
        w_out = jnp.concatenate([out_a[:, cols], out_b[:, cols]], axis=0)
        part = jnp.dot(activation, w_out, preferred_element_type=jnp.float32)
        part = part.astype(jnp.bfloat16)
        own_ref[:, cols] = part[:rows]
        y_part, z_part, d_part = (part[i * rows : (i + 1) * rows] for i in (1, 2, 3))
        if at < cut:
            y0_ref[:, cols] = y_part
            z0_ref[0, :, cols] = z_part
            z0_ref[1, :, cols] = d_part
        else:
            cols = slice(at - cut, at - cut + step)
            z1_ref[:, cols] = z_part
            y1_ref[0, :, cols] = y_part
            y1_ref[1, :, cols] = d_part


def ffn(left, right, weights, cut, after=()):
    rows, half = left[0].shape
    width = 2 * half
    units = weights[0].shape[1]
    rest = width - cut
    outs = [
        struct((rows, width)),
        struct((2, rows, cut)),
        struct((2, rows, rest)),
        struct((rows, cut)),
        struct((rows, rest)),
    ]
    return call(
        functools.partial(ffn_kernel, cut),
        outs,
        [VMEM] * 12 + [ANY] * len(after),
        "expert_ffn",
        4 * 4 * rows * width * units * 2,
        8 * units * width + 16 * rows * width,
    )(*left, *right, *weights, *after)


def first_kernel(y0_ref, az_ref, z1_ref, ay_ref, *refs):
    y_ref, z_ref = refs[-2:]
    for own, other, out in ((y0_ref, az_ref, y_ref), (z1_ref, ay_ref, z_ref)):
        out[...] = (own[...].astype(jnp.float32) + other[1].astype(jnp.float32)).astype(jnp.bfloat16)


def first_step(y0, from_z, z1, from_y, after=()):
    return call(
        first_kernel,
        [struct(y0.shape), struct(z1.shape)],
        [VMEM] * 4 + [ANY] * len(after),
        "first_step",
        y0.size + z1.size,
        6 * (y0.size + z1.size),
    )(y0, from_z, z1, from_y, *after)


def total_kernel(cut, *refs):
    own_ref, az_ref, ay_ref, by_ref, bz_ref = refs[:5]
    out_ref = refs[7]
    for first, second, cols in (
        (az_ref, by_ref, slice(0, cut)),
        (ay_ref, bz_ref, slice(cut, out_ref.shape[1])),
    ):
        out_ref[:, cols] = (
            own_ref[:, cols].astype(jnp.float32)
            + first[0].astype(jnp.float32)
            + second[...].astype(jnp.float32)
        ).astype(jnp.bfloat16)


def total(sums, cut, held):
    rows, width = sums[0].shape
    outs = [struct((rows, width))] + [struct(value.shape) for value in held]
    return call(
        functools.partial(total_kernel, cut),
        outs,
        [VMEM] * 5 + [ANY] * len(held),
        "far_total",
        3 * rows * width,
        8 * rows * width,
        out_specs=[VMEM] + [ANY] * len(held),
        aliases={5 + i: 1 + i for i in range(len(held))},
    )(*sums, *held)


def finish_kernel(groups, cap, cut, *refs):
    hidden_refs = refs[:2]
    square_refs = refs[2:4]
    gate_ref, flat_ref, own_ref, az_ref, ay_ref, by_ref, bz_ref = refs[4:11]
    back_refs = refs[11:-1]
    out_ref = refs[-1]
    tokens, width = out_ref.shape
    half = width // 2
    flat = flat_ref[...]
    squares = jnp.sum(square_refs[0][...] + square_refs[1][...], axis=1, keepdims=True)
    factor = gate_ref[...] * lax.rsqrt(squares * (1.0 / width) + EPS)

    def picker(group):
        slots = lax.broadcasted_iota(jnp.int32, (tokens, cap), 1) + group * cap
        return (slots == flat).astype(jnp.float32).astype(jnp.bfloat16)

    pickers = [picker(group) for group in range(groups)]
    step = 512
    for at in range(0, width, step):
        whole = slice(at, at + step)
        inner = at if at < cut else at - cut
        part = slice(inner, inner + step)
        first, second = (az_ref, by_ref) if at < cut else (ay_ref, bz_ref)
        added = (
            own_ref[:, whole].astype(jnp.float32)
            + first[0, :, part].astype(jnp.float32)
            + second[:, part].astype(jnp.float32)
        )
        coarse = added.astype(jnp.bfloat16)
        fine = (added - coarse.astype(jnp.float32)).astype(jnp.bfloat16)
        picked = jnp.dot(pickers[0], coarse, preferred_element_type=jnp.float32)
        picked = picked + jnp.dot(pickers[0], fine, preferred_element_type=jnp.float32)
        for group in range(1, groups):
            picked = picked + jnp.dot(
                pickers[group], back_refs[group - 1][:, whole], preferred_element_type=jnp.float32
            )
        side, inner = divmod(at, half)
        hidden = hidden_refs[side][:, inner : inner + step]
        out_ref[:, whole] = (hidden + factor * picked).astype(jnp.bfloat16)


def finish(hidden, squares, gate, flat, sums, backs, groups, cap, cut):
    tokens = hidden[0].shape[0]
    width = 2 * hidden[0].shape[1]
    operands = [*hidden, *squares, gate, flat, *sums, *backs]
    return call(
        functools.partial(finish_kernel, groups, cap, cut),
        struct((tokens, width)),
        [VMEM] * len(operands),
        "finish",
        4 * tokens * cap * (groups + 1) * width,
        16 * tokens * width,
    )(*operands)


def body(state, query, enc_kv, gain, w_in, w_out, expert_id, slot, gate):
    tokens, width = state.shape[2:]
    devices = lax.axis_size("expert")
    pipes = lax.axis_size("pipe")
    groups = devices // WSPLIT
    cap = 3 * tokens // (2 * groups)
    half = width // 2
    far_cut, near_cut = width // 2, width // 4

    def across(value, bit):
        return lax.ppermute(value, "expert", [(i, i ^ bit) for i in range(devices)])

    def groups_on(value, count):
        shift = count * WSPLIT
        return lax.ppermute(value, "expert", [(i, (i + shift) % devices) for i in range(devices)])

    def cross(blocks):
        return [groups_on(block, count) for count, block in enumerate(blocks, 1)]

    def join(blocks):
        return jnp.concatenate(blocks, axis=0) if len(blocks) > 1 else blocks[0]

    def share(value):
        perms = [[(i, (i + shift) % pipes) for i in range(pipes)] for shift in range(1, pipes)]
        return [value] + [lax.ppermute(value, "pipe", perm) for perm in perms]

    def split(value):
        return jnp.transpose(value, (1, 0, 2)).reshape(-1, half)

    weights = [w_in, across(w_in, 1), w_out, across(w_out, 1)]
    kv_a = share(split(enc_kv[0, :, :, :half]))
    group = (lax.axis_index("expert") // WSPLIT).astype(jnp.int32).reshape(1)
    staged = stage(
        group,
        state[0, 0],
        query[0, 0],
        gain.reshape(1, width),
        expert_id[0],
        slot[0],
        gate[0],
        groups,
        cap,
    )
    kv_b = share(*after_all([split(enc_kv[0, :, :, half:])], [*kv_a[1:], staged[3]]))
    flat, gates = staged[4:]
    hidden_a, squares_a, near_a, *far_a = attend(*staged[:4], kv_a, groups, cap, 0)
    hidden_b, squares_b, near_b, *far_b = attend(
        *staged[:4], kv_b, groups, cap, half, after=[weights[1], weights[3]]
    )

    near_ya, near_za, far_a = across(near_a, 2), across(near_a, 4), cross(far_a)
    far_b = cross(after_all(far_b, [*far_a, near_ya, near_za]))
    (far_a,) = after_all([join(far_a)], [squares_b])
    near_yb, near_zb = across(near_b, 2), across(near_b, 4)
    far_ya, far_za = across(far_a, 2), across(far_a, 4)
    (far_b,) = after_all([join(far_b)], [far_ya, far_za, near_yb, near_zb])
    far_yb, far_zb = across(far_b, 2), across(far_b, 4)
    near_left = [near_a, near_ya, near_za, across(near_za, 2)]
    near_right = [near_b, near_yb, near_zb, across(near_zb, 2)]
    far_left = [far_a, far_ya, far_za, across(far_ya, 4)]
    far_right = [far_b, far_yb, far_zb, across(far_zb, 2)]

    def first_sums(own, z0, y1, y0, z1, after=()):
        from_z, from_y = across(z0, 4), across(y1, 2)
        return own, from_z, from_y, *first_step(y0, from_z, z1, from_y, after)

    def last_sums(own, from_z, from_y, on_y, on_z):
        return own, from_z, from_y, across(on_y, 2), across(on_z, 4)

    far_parts = ffn(far_left, far_right, weights, far_cut)
    near_parts = ffn(near_left, near_right, weights, near_cut, after=far_parts[3:])
    far_sum, *held = total(
        last_sums(*first_sums(*far_parts, after=near_parts[3:])), far_cut, near_parts[1:3]
    )
    backs = [
        groups_on(far_sum[(count - 1) * cap : count * cap], groups - count)
        for count in range(1, groups)
    ]
    near_sums = last_sums(*first_sums(near_parts[0], *held, *near_parts[3:]))
    output = finish([hidden_a, hidden_b], [squares_a, squares_b], gates, flat, near_sums, backs, groups, cap, near_cut)
    return output.reshape(1, 1, tokens, width)


def solution(mesh):
    return jax.shard_map(
        body,
        mesh=mesh,
        in_specs=(
            P("expert", "pipe", None, None),
            P("expert", "pipe", None, None),
            P("expert", "pipe", None, None),
            P(),
            P(None, "expert"),
            P("expert", None),
            P("expert", "pipe", None),
            P("expert", "pipe", None),
            P("expert", "pipe", None),
        ),
        out_specs=P("expert", "pipe", None, None),
        check_vma=False,
    )
```

```python
import functools
import math

import jax
import jax.numpy as jnp
from jax import lax
from jax.experimental import pallas as pl
from jax.experimental.pallas import tpu as pltpu
from jax.sharding import PartitionSpec as P

HEADS = 16
HD = 128
WSPLIT = 8
EPS = 1e-06
VMEM_LIMIT = 32 * 1024 * 1024

VMEM = pl.BlockSpec(memory_space=pltpu.VMEM)
SMEM = pl.BlockSpec(memory_space=pltpu.SMEM)
ANY = pl.BlockSpec(memory_space=pl.ANY)


def struct(shape, dtype=jnp.bfloat16):
    return jax.ShapeDtypeStruct(shape, dtype)


def call(
    kernel, outs, in_specs, name, flops, moved, out_specs=None, aliases=None
):
    return pl.pallas_call(
        kernel,
        out_shape=outs,
        in_specs=in_specs,
        out_specs=out_specs or jax.tree.map(lambda _: VMEM, outs),
        input_output_aliases=aliases or {},
        compiler_params=pltpu.CompilerParams(vmem_limit_bytes=VMEM_LIMIT),
        cost_estimate=pl.CostEstimate(flops=flops, bytes_accessed=moved, transcendentals=0),
        name=name,
    )


def as_column(row):
    count = row.shape[1]
    down = lax.broadcasted_iota(jnp.int32, (count, count), 0)
    along = lax.broadcasted_iota(jnp.int32, (count, count), 1)
    return jnp.sum(jnp.where(down == along, row, jnp.zeros_like(row)), axis=1, keepdims=True)


def stage_kernel(groups, cap, *refs):
    group_ref, state_in, query_in, gain_in, expert_ref, slot_ref, gate_ref = refs[:7]
    state_out, query_out, gain_out, flat_row, flat_column, gate_column = refs[7:]
    state_out[...] = state_in[...]
    query_out[...] = query_in[...]
    gain_out[...] = gain_in[...]
    offset = expert_ref[...] - group_ref[0]
    offset = jnp.where(offset < 0, offset + groups, offset)
    slot = slot_ref[...]
    flat = jnp.where(slot >= 0, offset * cap + slot, -1)
    flat_row[...] = flat
    flat_column[...] = as_column(flat)
    gate_column[...] = as_column(gate_ref[...])


def stage(group, state, query, gain, expert_id, slot, gate, groups, cap):
    tokens, width = state.shape
    outs = [
        struct((tokens, width)),
        struct((tokens, width)),
        struct((1, width), jnp.float32),
        struct((1, tokens), jnp.int32),
        struct((tokens, 1), jnp.int32),
        struct((tokens, 1), jnp.float32),
    ]
    return call(
        functools.partial(stage_kernel, groups, cap),
        outs,
        [SMEM] + [VMEM] * 6,
        "stage",
        tokens * tokens,
        8 * tokens * width,
    )(group, state, query, gain, expert_id, slot, gate)


def gate_kernel(*refs):
    pass


def after_all(values, others):
    return call(
        gate_kernel,
        [struct(value.shape) for value in values],
        [ANY] * (len(values) + len(others)),
        "hand_on",
        1,
        1,
        out_specs=[ANY] * len(values),
        aliases={i: i for i in range(len(values))},
    )(*values, *others)


def attend_kernel(pieces, groups, cap, *refs):
    state_ref, query_ref, gain_ref, flat_ref = refs[:4]
    kv_refs = refs[4 : 4 + pieces]
    hidden_ref = refs[-1 - groups]
    packed_refs = refs[-groups:]
    tokens, width = state_ref.shape
    local = kv_refs[0].shape[0] // 2
    scale = 1.0 / math.sqrt(HD)
    squares = jnp.zeros((tokens, HD), jnp.float32)
    for head in range(HEADS):
        cols = slice(head * HD, (head + 1) * HD)
        keys = jnp.concatenate([r[:local, cols] for r in kv_refs], axis=0)
        values = jnp.concatenate([r[local:, cols] for r in kv_refs], axis=0)
        scores = (
            lax.dot_general(
                query_ref[:, cols],
                keys,
                (((1,), (1,)), ((), ())),
                preferred_element_type=jnp.float32,
            )
            * scale
        )
        raised = jnp.exp(scores - jnp.max(scores, axis=1, keepdims=True))
        total = jnp.sum(raised, axis=1, keepdims=True)
        mixed = jnp.dot(raised.astype(jnp.bfloat16), values, preferred_element_type=jnp.float32)
        hidden = state_ref[:, cols].astype(jnp.float32) + mixed / total
        hidden_ref[:, cols] = hidden
        squares = squares + hidden * hidden
    mean_square = jnp.sum(squares, axis=1, keepdims=True) * (1.0 / width)
    inverse = lax.rsqrt(mean_square + EPS)
    rows = lax.broadcasted_iota(jnp.int32, (groups * cap, tokens), 0)
    selector = (rows == flat_ref[...]).astype(jnp.float32).astype(jnp.bfloat16)
    step = 512
    for at in range(0, width, step):
        cols = slice(at, at + step)
        normed = (hidden_ref[:, cols] * inverse * gain_ref[:, cols]).astype(jnp.bfloat16)
        packed = jnp.dot(selector, normed, preferred_element_type=jnp.float32).astype(jnp.bfloat16)
        for group in range(groups):
            packed_refs[group][:, cols] = packed[group * cap : (group + 1) * cap]


def attend(state, query, gain, flat, kv_pieces, groups, cap, after):
    tokens, width = state.shape
    outs = [struct((tokens, width), jnp.float32)] + [struct((cap, width))] * groups
    pieces = len(kv_pieces)
    return call(
        functools.partial(attend_kernel, pieces, groups, cap),
        outs,
        [VMEM] * (4 + pieces) + [ANY] * len(after),
        "attend",
        4 * tokens * pieces * kv_pieces[0].shape[0] * width,
        12 * tokens * width,
    )(state, query, gain, flat, *kv_pieces, *after)


def ffn_kernel(rows_ref, in_a, in_b, out_a, out_b, out_ref):
    w_in = jnp.concatenate([in_a[...], in_b[...]], axis=1)
    raw = jnp.dot(rows_ref[...], w_in, preferred_element_type=jnp.float32)
    activation = jnp.maximum(raw, 0.0).astype(jnp.bfloat16)
    step = 512
    for at in range(0, out_ref.shape[1], step):
        cols = slice(at, at + step)
        w_out = jnp.concatenate([out_a[:, cols], out_b[:, cols]], axis=0)
        part = jnp.dot(activation, w_out, preferred_element_type=jnp.float32)
        out_ref[:, cols] = part.astype(jnp.bfloat16)


def ffn(rows, weights):
    count, width = rows.shape
    units = weights[0].shape[1]
    return call(
        ffn_kernel,
        struct((count, width)),
        [VMEM] * 5,
        "expert_ffn",
        4 * count * width * units * 2,
        8 * units * width + 4 * count * width,
    )(rows, *weights)


def finish_kernel(groups, cap, *refs):
    hidden_ref, gate_ref, flat_ref = refs[:3]
    sum_refs = refs[3:-1]
    out_ref = refs[-1]
    tokens, width = hidden_ref.shape
    flat = flat_ref[...]
    step = 512
    for at in range(0, width, step):
        cols = slice(at, at + step)
        picked = jnp.zeros((tokens, step), jnp.float32)
        for group in range(groups):
            slots = lax.broadcasted_iota(jnp.int32, (tokens, cap), 1) + group * cap
            picker = (slots == flat).astype(jnp.float32).astype(jnp.bfloat16)
            picked = picked + jnp.dot(
                picker, sum_refs[group][:, cols], preferred_element_type=jnp.float32
            )
        out_ref[:, cols] = (hidden_ref[:, cols] + gate_ref[...] * picked).astype(jnp.bfloat16)


def finish(hidden, gate, flat, sums, groups, cap):
    tokens, width = hidden.shape
    operands = [hidden, gate, flat, *sums]
    return call(
        functools.partial(finish_kernel, groups, cap),
        struct((tokens, width)),
        [VMEM] * len(operands),
        "finish",
        4 * tokens * cap * groups * width,
        16 * tokens * width,
    )(*operands)


def body(state, query, enc_kv, gain, w_in, w_out, expert_id, slot, gate):
    tokens, width = state.shape[2:]
    devices = lax.axis_size("expert")
    pipes = lax.axis_size("pipe")
    groups = devices // WSPLIT
    cap = 3 * tokens // (2 * groups)

    def across(value, bit):
        return lax.ppermute(value, "expert", [(i, i ^ bit) for i in range(devices)])

    def groups_on(value, count):
        shift = count * WSPLIT
        return lax.ppermute(value, "expert", [(i, (i + shift) % devices) for i in range(devices)])

    kv = jnp.transpose(enc_kv[0], (1, 0, 2)).reshape(-1, width)
    kv_pieces = [kv]
    for shift in range(1, pipes):
        perm = [(i, (i + shift) % pipes) for i in range(pipes)]
        kv_pieces.append(lax.ppermute(kv, "pipe", perm))
    weights = [w_in, across(w_in, 1), w_out, across(w_out, 1)]

    group = (lax.axis_index("expert") // WSPLIT).astype(jnp.int32).reshape(1)
    staged = stage(
        group,
        state[0, 0],
        query[0, 0],
        gain.reshape(1, width),
        expert_id[0],
        slot[0],
        gate[0],
        groups,
        cap,
    )
    flat, gates = staged[4:]
    hidden, near, *packed = attend(
        *staged[:4], kv_pieces, groups, cap, after=[weights[1], weights[3]]
    )
    far = [groups_on(block, count) for count, block in enumerate(packed, 1)]
    far = jnp.concatenate(far, axis=0) if len(far) > 1 else far[0]

    squares = [
        [base + core + 2 * chip for chip in range(WSPLIT // 2)]
        for base in range(0, devices, WSPLIT)
        for core in range(2)
    ]

    def spread(rows):
        return lax.all_gather(rows, "expert", axis_index_groups=squares, axis=0, tiled=True)

    def experts(spread):
        partial_value = ffn(spread, weights)
        return lax.psum_scatter(
            partial_value,
            "expert",
            scatter_dimension=0,
            axis_index_groups=squares,
            tiled=True,
        )

    near = spread(near)
    far = spread(*after_all([far], [near]))
    near_sum, far_sum = experts(near), experts(far)
    backs = [
        groups_on(far_sum[(count - 1) * cap : count * cap], groups - count)
        for count in range(1, groups)
    ]
    output = finish(hidden, gates, flat, [near_sum, *backs], groups, cap)
    return output.reshape(1, 1, tokens, width)


def solution(mesh):
    return jax.shard_map(
        body,
        mesh=mesh,
        in_specs=(
            P("expert", "pipe", None, None),
            P("expert", "pipe", None, None),
            P("expert", "pipe", None, None),
            P(),
            P(None, "expert"),
            P("expert", None),
            P("expert", "pipe", None),
            P("expert", "pipe", None),
            P("expert", "pipe", None),
        ),
        out_specs=P("expert", "pipe", None, None),
        check_vma=False,
    )
```

```python
import functools
import math

import jax
import jax.numpy as jnp
from jax import lax
from jax.experimental import pallas as pl
from jax.experimental.pallas import tpu as pltpu
from jax.sharding import PartitionSpec as P

HEADS = 16
HD = 128
WSPLIT = 8
EPS = 1e-06
RETURN_WEIGHT = 40_000_000_000
VMEM_LIMIT = 32 * 1024 * 1024

VMEM = pl.BlockSpec(memory_space=pltpu.VMEM)
SMEM = pl.BlockSpec(memory_space=pltpu.SMEM)
ANY = pl.BlockSpec(memory_space=pl.ANY)


def struct(shape, dtype=jnp.bfloat16):
    return jax.ShapeDtypeStruct(shape, dtype)


def call(
    kernel, outs, in_specs, name, flops, moved, out_specs=None, aliases=None
):
    return pl.pallas_call(
        kernel,
        out_shape=outs,
        in_specs=in_specs,
        out_specs=out_specs or jax.tree.map(lambda _: VMEM, outs),
        input_output_aliases=aliases or {},
        compiler_params=pltpu.CompilerParams(vmem_limit_bytes=VMEM_LIMIT),
        cost_estimate=pl.CostEstimate(flops=flops, bytes_accessed=moved, transcendentals=0),
        name=name,
    )


def as_column(row):
    count = row.shape[1]
    down = lax.broadcasted_iota(jnp.int32, (count, count), 0)
    along = lax.broadcasted_iota(jnp.int32, (count, count), 1)
    return jnp.sum(jnp.where(down == along, row, jnp.zeros_like(row)), axis=1, keepdims=True)


def stage_kernel(groups, cap, *refs):
    group_ref, state_in, query_in, gain_in, expert_ref, slot_ref, gate_ref = refs[:7]
    state_out, query_out, gain_out, flat_row, flat_column, gate_column = refs[7:]
    state_out[...] = state_in[...]
    query_out[...] = query_in[...]
    gain_out[...] = gain_in[...]
    offset = expert_ref[...] - group_ref[0]
    offset = jnp.where(offset < 0, offset + groups, offset)
    slot = slot_ref[...]
    flat = jnp.where(slot >= 0, offset * cap + slot, -1)
    flat_row[...] = flat
    flat_column[...] = as_column(flat)
    gate_column[...] = as_column(gate_ref[...])


def stage(group, state, query, gain, expert_id, slot, gate, groups, cap):
    tokens, width = state.shape
    outs = [
        struct((tokens, width)),
        struct((tokens, width)),
        struct((1, width), jnp.float32),
        struct((1, tokens), jnp.int32),
        struct((tokens, 1), jnp.int32),
        struct((tokens, 1), jnp.float32),
    ]
    return call(
        functools.partial(stage_kernel, groups, cap),
        outs,
        [SMEM] + [VMEM] * 6,
        "stage",
        tokens * tokens,
        8 * tokens * width,
    )(group, state, query, gain, expert_id, slot, gate)


def gate_kernel(*refs):
    pass


def after_all(values, others=(), weight=1):
    return call(
        gate_kernel,
        [struct(value.shape) for value in values],
        [ANY] * (len(values) + len(others)),
        "hand_on",
        weight,
        1,
        out_specs=[ANY] * len(values),
        aliases={i: i for i in range(len(values))},
    )(*values, *others)


def attend_kernel(pieces, groups, cap, *refs):
    state_ref, query_ref, gain_ref, flat_ref = refs[:4]
    kv_refs = refs[4 : 4 + pieces]
    hidden_ref = refs[-1 - groups]
    packed_refs = refs[-groups:]
    tokens, width = state_ref.shape
    local = kv_refs[0].shape[0] // 2
    scale = 1.0 / math.sqrt(HD)
    squares = jnp.zeros((tokens, HD), jnp.float32)
    for head in range(HEADS):
        cols = slice(head * HD, (head + 1) * HD)
        keys = jnp.concatenate([r[:local, cols] for r in kv_refs], axis=0)
        values = jnp.concatenate([r[local:, cols] for r in kv_refs], axis=0)
        scores = (
            lax.dot_general(
                query_ref[:, cols],
                keys,
                (((1,), (1,)), ((), ())),
                preferred_element_type=jnp.float32,
            )
            * scale
        )
        raised = jnp.exp(scores - jnp.max(scores, axis=1, keepdims=True))
        total = jnp.sum(raised, axis=1, keepdims=True)
        mixed = jnp.dot(raised.astype(jnp.bfloat16), values, preferred_element_type=jnp.float32)
        hidden = state_ref[:, cols].astype(jnp.float32) + mixed / total
        hidden_ref[:, cols] = hidden
        squares = squares + hidden * hidden
    mean_square = jnp.sum(squares, axis=1, keepdims=True) * (1.0 / width)
    inverse = lax.rsqrt(mean_square + EPS)
    rows = lax.broadcasted_iota(jnp.int32, (groups * cap, tokens), 0)
    selector = (rows == flat_ref[...]).astype(jnp.float32).astype(jnp.bfloat16)
    step = 512
    for at in range(0, width, step):
        cols = slice(at, at + step)
        normed = (hidden_ref[:, cols] * inverse * gain_ref[:, cols]).astype(jnp.bfloat16)
        packed = jnp.dot(selector, normed, preferred_element_type=jnp.float32).astype(jnp.bfloat16)
        for group in range(groups):
            packed_refs[group][:, cols] = packed[group * cap : (group + 1) * cap]


def attend(state, query, gain, flat, kv_pieces, groups, cap, after):
    tokens, width = state.shape
    outs = [struct((tokens, width), jnp.float32)] + [struct((cap, width))] * groups
    pieces = len(kv_pieces)
    return call(
        functools.partial(attend_kernel, pieces, groups, cap),
        outs,
        [VMEM] * (4 + pieces) + [ANY] * len(after),
        "attend",
        4 * tokens * pieces * kv_pieces[0].shape[0] * width,
        12 * tokens * width,
    )(state, query, gain, flat, *kv_pieces, *after)


def ffn_kernel(cut, *refs):
    own_in, y_in, z_in, d_left, d_right = refs[:5]
    in_a, in_b, out_a, out_b = refs[5:9]
    own_ref, z0_ref, y1y_ref, y1d_ref, y0_ref, z1_ref = refs[-6:]
    rows, width = own_in.shape
    diagonal = jnp.concatenate([d_left[...], d_right[...]], axis=1)
    entries = jnp.concatenate([own_in[...], y_in[...], z_in[...], diagonal], axis=0)
    w_in = jnp.concatenate([in_a[...], in_b[...]], axis=1)
    raw = jnp.dot(entries, w_in, preferred_element_type=jnp.float32)
    activation = jnp.maximum(raw, 0.0).astype(jnp.bfloat16)
    step = 512
    for at in range(0, width, step):
        cols = slice(at, at + step)
        w_out = jnp.concatenate([out_a[:, cols], out_b[:, cols]], axis=0)
        part = jnp.dot(activation, w_out, preferred_element_type=jnp.float32)
        part = part.astype(jnp.bfloat16)
        own_ref[:, cols] = part[:rows]
        y_part, z_part, d_part = (part[i * rows : (i + 1) * rows] for i in (1, 2, 3))
        if at < cut:
            y0_ref[:, cols] = y_part
            z0_ref[0, :, cols] = z_part
            z0_ref[1, :, cols] = d_part
        else:
            cols = slice(at - cut, at - cut + step)
            z1_ref[:, cols] = z_part
            y1y_ref[:, cols] = y_part
            y1d_ref[:, cols] = d_part


def ffn(blocks, weights, cut, after=()):
    rows, width = blocks[0].shape
    units = weights[0].shape[1]
    rest = width - cut
    outs = [struct((rows, width)), struct((2, rows, cut))]
    outs += [struct((rows, size)) for size in (rest, rest, cut, rest)]
    return call(
        functools.partial(ffn_kernel, cut),
        outs,
        [VMEM] * 9 + [ANY] * len(after),
        "expert_ffn",
        4 * 4 * rows * width * units * 2,
        8 * units * width + 16 * rows * width,
    )(*blocks, *weights, *after)


def first_kernel(y0_ref, az_ref, z1_ref, ayd_ref, *refs):
    y_ref, z_ref = refs[-2:]
    for own, other, out in ((y0_ref, az_ref.at[1], y_ref), (z1_ref, ayd_ref, z_ref)):
        out[...] = (own[...].astype(jnp.float32) + other[...].astype(jnp.float32)).astype(
            jnp.bfloat16
        )


def first_step(y0, from_z, z1, from_y, after=()):
    return call(
        first_kernel,
        [struct(y0.shape), struct(z1.shape)],
        [VMEM] * 4 + [ANY] * len(after),
        "first_step",
        y0.size + z1.size,
        6 * (y0.size + z1.size),
    )(y0, from_z, z1, from_y, *after)


def total_kernel(cut, held, *refs):
    own_ref, az_ref, ayy_ref, by_ref, bz_ref = refs[:5]
    out_ref = refs[5 + held]
    for first, second, cols in (
        (az_ref.at[0], by_ref, slice(0, cut)),
        (ayy_ref, bz_ref, slice(cut, out_ref.shape[1])),
    ):
        out_ref[:, cols] = (
            own_ref[:, cols].astype(jnp.float32)
            + first[...].astype(jnp.float32)
            + second[...].astype(jnp.float32)
        ).astype(jnp.bfloat16)


def total(sums, cut, held):
    held = list(held)
    rows, width = sums[0].shape
    outs = [struct((rows, width))] + [struct(value.shape) for value in held]
    return call(
        functools.partial(total_kernel, cut, len(held)),
        outs,
        [VMEM] * 5 + [ANY] * len(held),
        "far_total",
        3 * rows * width,
        8 * rows * width,
        out_specs=[VMEM] + [ANY] * len(held),
        aliases={5 + i: 1 + i for i in range(len(held))},
    )(*sums, *held)


def finish_kernel(groups, cap, cut, *refs):
    hidden_ref, gate_ref, flat_ref, own_ref, az_ref, ayy_ref, by_ref, bz_ref = refs[:8]
    back_refs = refs[8:-1]
    out_ref = refs[-1]
    tokens, width = hidden_ref.shape
    flat = flat_ref[...]

    def picker(group):
        slots = lax.broadcasted_iota(jnp.int32, (tokens, cap), 1) + group * cap
        return (slots == flat).astype(jnp.float32).astype(jnp.bfloat16)

    pickers = [picker(group) for group in range(groups)]
    step = 512
    for at in range(0, width, step):
        whole = slice(at, at + step)
        inner = at if at < cut else at - cut
        part = slice(inner, inner + step)
        first, second = (az_ref.at[0], by_ref) if at < cut else (ayy_ref, bz_ref)
        added = (
            own_ref[:, whole].astype(jnp.float32)
            + first[:, part].astype(jnp.float32)
            + second[:, part].astype(jnp.float32)
        )
        coarse = added.astype(jnp.bfloat16)
        fine = (added - coarse.astype(jnp.float32)).astype(jnp.bfloat16)
        picked = jnp.dot(pickers[0], coarse, preferred_element_type=jnp.float32)
        picked = picked + jnp.dot(pickers[0], fine, preferred_element_type=jnp.float32)
        for group in range(1, groups):
            picked = picked + jnp.dot(
                pickers[group], back_refs[group - 1][:, whole], preferred_element_type=jnp.float32
            )
        out_ref[:, whole] = (hidden_ref[:, whole] + gate_ref[...] * picked).astype(jnp.bfloat16)


def finish(hidden, gate, flat, sums, backs, groups, cap, cut):
    tokens, width = hidden.shape
    operands = [hidden, gate, flat, *sums, *backs]
    return call(
        functools.partial(finish_kernel, groups, cap, cut),
        struct((tokens, width)),
        [VMEM] * len(operands),
        "finish",
        4 * tokens * cap * (groups + 1) * width,
        16 * tokens * width,
    )(*operands)


def body(state, query, enc_kv, gain, w_in, w_out, expert_id, slot, gate):
    tokens, width = state.shape[2:]
    devices = lax.axis_size("expert")
    pipes = lax.axis_size("pipe")
    groups = devices // WSPLIT
    cap = 3 * tokens // (2 * groups)
    half = width // 2
    far_cut, near_cut = width // 2, width // 4

    def across(value, bit):
        return lax.ppermute(value, "expert", [(i, i ^ bit) for i in range(devices)])

    def groups_on(value, count):
        shift = count * WSPLIT
        return lax.ppermute(value, "expert", [(i, (i + shift) % devices) for i in range(devices)])

    kv = jnp.transpose(enc_kv[0], (1, 0, 2)).reshape(-1, width)
    kv_pieces = [kv]
    for shift in range(1, pipes):
        perm = [(i, (i + shift) % pipes) for i in range(pipes)]
        kv_pieces.append(lax.ppermute(kv, "pipe", perm))
    weights = [w_in, across(w_in, 1), w_out, across(w_out, 1)]

    group = (lax.axis_index("expert") // WSPLIT).astype(jnp.int32).reshape(1)
    staged = stage(
        group,
        state[0, 0],
        query[0, 0],
        gain.reshape(1, width),
        expert_id[0],
        slot[0],
        gate[0],
        groups,
        cap,
    )
    flat, gates = staged[4:]
    hidden, near, *packed = attend(
        *staged[:4], kv_pieces, groups, cap, after=[weights[1], weights[3]]
    )
    far = [groups_on(block, count) for count, block in enumerate(packed, 1)]
    far = jnp.concatenate(far, axis=0) if len(far) > 1 else far[0]

    near_y, near_z = across(near, 2), across(near, 4)
    (far,) = after_all([far], [near_y, near_z])
    far_y, far_z = across(far, 2), across(far, 4)

    def blocks(own, y, z):
        return [own, y, z, across(y[:, :half], 4), across(z[:, half:], 2)]

    def first_sums(own, z0, y1y, y1d, y0, z1, after=()):
        from_z, from_yy, from_yd = across(z0, 4), across(y1y, 2), across(y1d, 2)
        return own, from_z, from_yy, *first_step(y0, from_z, z1, from_yd, after)

    def last_sums(own, from_z, from_y, on_y, on_z):
        return own, from_z, from_y, across(on_y, 2), across(on_z, 4)

    far_parts = ffn(blocks(far, far_y, far_z), weights, far_cut)
    near_parts = ffn(blocks(near, near_y, near_z), weights, near_cut, after=far_parts[4:])
    far_sum, *held = total(
        last_sums(*first_sums(*far_parts, after=near_parts[4:])), far_cut, near_parts[1:4]
    )
    backs = [
        groups_on(far_sum[(count - 1) * cap : count * cap], groups - count)
        for count in range(1, groups)
    ]
    backs = after_all(backs, weight=RETURN_WEIGHT)
    near_sums = last_sums(*first_sums(near_parts[0], *held, *near_parts[4:]))
    output = finish(hidden, gates, flat, near_sums, backs, groups, cap, near_cut)
    return output.reshape(1, 1, tokens, width)


def solution(mesh):
    return jax.shard_map(
        body,
        mesh=mesh,
        in_specs=(
            P("expert", "pipe", None, None),
            P("expert", "pipe", None, None),
            P("expert", "pipe", None, None),
            P(),
            P(None, "expert"),
            P("expert", None),
            P("expert", "pipe", None),
            P("expert", "pipe", None),
            P("expert", "pipe", None),
        ),
        out_specs=P("expert", "pipe", None, None),
        check_vma=False,
    )
```

```python
import functools
import math

import jax
import jax.numpy as jnp
from jax import lax
from jax.experimental import pallas as pl
from jax.experimental.pallas import tpu as pltpu
from jax.sharding import PartitionSpec as P

HEADS = 16
HD = 128
WSPLIT = 8
EPS = 1e-06
VMEM_LIMIT = 32 * 1024 * 1024

VMEM = pl.BlockSpec(memory_space=pltpu.VMEM)
SMEM = pl.BlockSpec(memory_space=pltpu.SMEM)
ANY = pl.BlockSpec(memory_space=pl.ANY)


def struct(shape, dtype=jnp.bfloat16):
    return jax.ShapeDtypeStruct(shape, dtype)


def call(
    kernel, outs, in_specs, name, flops, moved, out_specs=None, aliases=None
):
    return pl.pallas_call(
        kernel,
        out_shape=outs,
        in_specs=in_specs,
        out_specs=out_specs or jax.tree.map(lambda _: VMEM, outs),
        input_output_aliases=aliases or {},
        compiler_params=pltpu.CompilerParams(vmem_limit_bytes=VMEM_LIMIT),
        cost_estimate=pl.CostEstimate(flops=flops, bytes_accessed=moved, transcendentals=0),
        name=name,
    )


def as_column(row):
    return jnp.transpose(jnp.broadcast_to(row, (8, row.shape[1])))[:, :1]


def stage_kernel(groups, cap, *refs):
    group_ref, state_in, query_in, gain_in, expert_ref, slot_ref, gate_ref = refs[:7]
    state_out, query_out, gain_out, flat_row, flat_column, gate_column = refs[7:]
    state_out[...] = state_in[...]
    query_out[...] = query_in[...]
    gain_out[...] = gain_in[...]
    offset = expert_ref[...] - group_ref[0]
    offset = jnp.where(offset < 0, offset + groups, offset)
    slot = slot_ref[...]
    flat = jnp.where(slot >= 0, offset * cap + slot, -1)
    flat_row[...] = flat
    flat_column[...] = as_column(flat)
    gate_column[...] = as_column(gate_ref[...])


def stage(group, state, query, gain, expert_id, slot, gate, groups, cap):
    tokens, width = state.shape
    outs = [
        struct((tokens, width)),
        struct((tokens, width)),
        struct((1, width), jnp.float32),
        struct((1, tokens), jnp.int32),
        struct((tokens, 1), jnp.int32),
        struct((tokens, 1), jnp.float32),
    ]
    return call(
        functools.partial(stage_kernel, groups, cap),
        outs,
        [SMEM] + [VMEM] * 6,
        "stage",
        tokens * tokens,
        8 * tokens * width,
    )(group, state, query, gain, expert_id, slot, gate)


def gate_kernel(*refs):
    pass


def after_all(values, others):
    return call(
        gate_kernel,
        [struct(value.shape) for value in values],
        [ANY] * (len(values) + len(others)),
        "hand_on",
        1,
        1,
        out_specs=[ANY] * len(values),
        aliases={i: i for i in range(len(values))},
    )(*values, *others)


def attend_kernel(pieces, groups, cap, *refs):
    state_ref, query_ref, gain_ref, flat_ref = refs[:4]
    kv_refs = refs[4 : 4 + pieces]
    hidden_ref = refs[-1 - groups]
    packed_refs = refs[-groups:]
    tokens, width = state_ref.shape
    local = kv_refs[0].shape[0] // 2
    scale = 1.0 / math.sqrt(HD)
    squares = jnp.zeros((tokens, HD), jnp.float32)
    for head in range(HEADS):
        cols = slice(head * HD, (head + 1) * HD)
        keys = jnp.concatenate([r[:local, cols] for r in kv_refs], axis=0)
        values = jnp.concatenate([r[local:, cols] for r in kv_refs], axis=0)
        scores = (
            lax.dot_general(
                keys,
                query_ref[:, cols],
                (((1,), (1,)), ((), ())),
                preferred_element_type=jnp.float32,
            )
            * scale
        )
        raised = jnp.exp(scores - jnp.max(scores, axis=0, keepdims=True))
        total = jnp.sum(raised, axis=0, keepdims=True)
        mixed = lax.dot_general(
            raised.astype(jnp.bfloat16),
            values,
            (((0,), (0,)), ((), ())),
            preferred_element_type=jnp.float32,
        )
        hidden = state_ref[:, cols].astype(jnp.float32) + mixed * as_column(1.0 / total)
        hidden_ref[:, cols] = hidden
        squares = squares + hidden * hidden
    mean_square = jnp.sum(squares, axis=1, keepdims=True) * (1.0 / width)
    inverse = lax.rsqrt(mean_square + EPS)
    rows = lax.broadcasted_iota(jnp.int32, (groups * cap, tokens), 0)
    selector = (rows == flat_ref[...]).astype(jnp.float32).astype(jnp.bfloat16)
    step = 512
    for at in range(0, width, step):
        cols = slice(at, at + step)
        normed = (hidden_ref[:, cols] * inverse * gain_ref[:, cols]).astype(jnp.bfloat16)
        packed = jnp.dot(selector, normed, preferred_element_type=jnp.float32).astype(jnp.bfloat16)
        for group in range(groups):
            packed_refs[group][:, cols] = packed[group * cap : (group + 1) * cap]


def attend(state, query, gain, flat, kv_pieces, groups, cap, after):
    tokens, width = state.shape
    outs = [struct((tokens, width), jnp.float32)] + [struct((cap, width))] * groups
    pieces = len(kv_pieces)
    return call(
        functools.partial(attend_kernel, pieces, groups, cap),
        outs,
        [VMEM] * (4 + pieces) + [ANY] * len(after),
        "attend",
        4 * tokens * pieces * kv_pieces[0].shape[0] * width,
        12 * tokens * width,
    )(state, query, gain, flat, *kv_pieces, *after)


def ffn_kernel(counts, cut, *refs):
    blocks = []
    for count in counts:
        parts, refs = refs[:count], refs[count:]
        blocks.append(jnp.concatenate([r[...] for r in parts], axis=1))
    in_a, in_b, out_a, out_b = refs[:4]
    own_ref, zd_ref, yd_ref, zz_ref, yy_ref, y0_ref, z1_ref = refs[-7:]
    rows, width = blocks[0].shape
    entries = jnp.concatenate(blocks, axis=0)
    w_in = jnp.concatenate([in_a[...], in_b[...]], axis=1)
    raw = jnp.dot(entries, w_in, preferred_element_type=jnp.float32)
    activation = jnp.maximum(raw, 0.0).astype(jnp.bfloat16)
    step = 512
    for at in range(0, width, step):
        cols = slice(at, at + step)
        w_out = jnp.concatenate([out_a[:, cols], out_b[:, cols]], axis=0)
        part = jnp.dot(activation, w_out, preferred_element_type=jnp.float32)
        part = part.astype(jnp.bfloat16)
        own_ref[:, cols] = part[:rows]
        y_part, z_part, d_part = (part[i * rows : (i + 1) * rows] for i in (1, 2, 3))
        if at < cut:
            y0_ref[:, cols] = y_part
            zz_ref[:, cols] = z_part
            zd_ref[:, cols] = d_part
        else:
            cols = slice(at - cut, at - cut + step)
            z1_ref[:, cols] = z_part
            yy_ref[:, cols] = y_part
            yd_ref[:, cols] = d_part


def ffn(blocks, weights, cut, after=()):
    rows = blocks[0][0].shape[0]
    width, units = weights[0].shape
    rest = width - cut
    outs = [struct((rows, size)) for size in (width, cut, rest, cut, rest, cut, rest)]
    counts = [len(parts) for parts in blocks]
    return call(
        functools.partial(ffn_kernel, counts, cut),
        outs,
        [VMEM] * (sum(counts) + 4) + [ANY] * len(after),
        "expert_ffn",
        4 * 4 * rows * width * units * 2,
        8 * units * width + 16 * rows * width,
    )(*sum(blocks, []), *weights, *after)


def first_kernel(y0_ref, zd_ref, z1_ref, yd_ref, y_ref, z_ref):
    for own, other, out in ((y0_ref, zd_ref, y_ref), (z1_ref, yd_ref, z_ref)):
        out[...] = (own[...].astype(jnp.float32) + other[...].astype(jnp.float32)).astype(
            jnp.bfloat16
        )


def first_step(y0, from_zd, z1, from_yd):
    return call(
        first_kernel,
        [struct(y0.shape), struct(z1.shape)],
        [VMEM] * 4,
        "first_step",
        y0.size + z1.size,
        6 * (y0.size + z1.size),
    )(y0, from_zd, z1, from_yd)


def add_up(own_ref, zz_ref, yy_ref, by_ref, bz_ref, cols):
    cut = zz_ref.shape[1]
    whole = slice(*cols)
    if cols[0] < cut:
        first, second, part = zz_ref, by_ref, whole
    else:
        first, second, part = yy_ref, bz_ref, slice(cols[0] - cut, cols[1] - cut)
    return (
        own_ref[:, whole].astype(jnp.float32)
        + first[:, part].astype(jnp.float32)
        + second[:, part].astype(jnp.float32)
    ).astype(jnp.bfloat16)


def total_kernel(held, *refs):
    out_ref = refs[5 + held]
    for at in range(0, out_ref.shape[1], 512):
        out_ref[:, at : at + 512] = add_up(*refs[:5], (at, at + 512))


def total(sums, held):
    rows, width = sums[0].shape
    outs = [struct((rows, width))] + [struct(value.shape) for value in held]
    return call(
        functools.partial(total_kernel, len(held)),
        outs,
        [VMEM] * 5 + [ANY] * len(held),
        "far_total",
        3 * rows * width,
        8 * rows * width,
        out_specs=[VMEM] + [ANY] * len(held),
        aliases={5 + i: 1 + i for i in range(len(held))},
    )(*sums, *held)


def finish_kernel(groups, cap, *refs):
    hidden_ref, gate_ref, flat_ref = refs[:3]
    sums = refs[3:8]
    back_refs = refs[8:-1]
    out_ref = refs[-1]
    tokens, width = hidden_ref.shape
    slots = lax.broadcasted_iota(jnp.int32, (tokens, groups * cap), 1)
    picker = (slots == flat_ref[...]).astype(jnp.float32).astype(jnp.bfloat16)
    step = 512
    for at in range(0, width, step):
        cols = slice(at, at + step)
        near = add_up(*sums, (at, at + step))
        found = jnp.concatenate([near] + [r[:, cols] for r in back_refs], axis=0)
        picked = jnp.dot(picker, found, preferred_element_type=jnp.float32)
        out_ref[:, cols] = (hidden_ref[:, cols] + gate_ref[...] * picked).astype(jnp.bfloat16)


def finish(hidden, gate, flat, sums, backs, groups, cap):
    tokens, width = hidden.shape
    operands = [hidden, gate, flat, *sums, *backs]
    return call(
        functools.partial(finish_kernel, groups, cap),
        struct((tokens, width)),
        [VMEM] * len(operands),
        "finish",
        4 * tokens * cap * groups * width,
        16 * tokens * width,
    )(*operands)


def body(state, query, enc_kv, gain, w_in, w_out, expert_id, slot, gate):
    tokens, width = state.shape[2:]
    devices = lax.axis_size("expert")
    pipes = lax.axis_size("pipe")
    groups = devices // WSPLIT
    cap = 3 * tokens // (2 * groups)
    half = width // 2
    far_cut, near_cut = width // 2, width // 4

    def across(value, bit):
        return lax.ppermute(value, "expert", [(i, i ^ bit) for i in range(devices)])

    def groups_on(value, count):
        shift = count * WSPLIT
        return lax.ppermute(value, "expert", [(i, (i + shift) % devices) for i in range(devices)])

    kv = jnp.transpose(enc_kv[0], (1, 0, 2)).reshape(-1, width)
    kv_pieces = [kv]
    for shift in range(1, pipes):
        perm = [(i, (i + shift) % pipes) for i in range(pipes)]
        kv_pieces.append(lax.ppermute(kv, "pipe", perm))
    weights = [w_in, across(w_in, 1), w_out, across(w_out, 1)]

    group = (lax.axis_index("expert") // WSPLIT).astype(jnp.int32).reshape(1)
    staged = stage(
        group,
        state[0, 0],
        query[0, 0],
        gain.reshape(1, width),
        expert_id[0],
        slot[0],
        gate[0],
        groups,
        cap,
    )
    flat, gates = staged[4:]
    hidden, near, *packed = attend(
        *staged[:4], kv_pieces, groups, cap, after=[weights[1], weights[3]]
    )
    far = [groups_on(block, count) for count, block in enumerate(packed, 1)]
    far = jnp.concatenate(far, axis=0) if len(far) > 1 else far[0]

    near_y, near_z = across(near, 2), across(near, 4)
    near_blocks = [[near], [near_y], [near_z], [across(near_z, 2)]]
    (far,) = after_all([far], [near_y, near_z])
    left, right = far[:, :half], far[:, half:]
    y_left, z_right = across(left, 2), across(right, 4)
    y_right, z_left = across(right, 2), across(left, 4)
    far_blocks = [
        [far],
        [y_left, y_right],
        [z_left, z_right],
        [across(y_left, 4), across(z_right, 2)],
    ]

    far_own, far_zd, far_yd, far_zz, far_yy, far_y0, far_z1 = ffn(far_blocks, weights, far_cut)
    near_own, *near_sent, near_y0, near_z1 = ffn(
        near_blocks, weights, near_cut, after=[far_y0, far_z1]
    )
    from_zd, from_yd = across(far_zd, 4), across(far_yd, 2)
    far_zz, far_yy = after_all([far_zz, far_yy], [near_y0])
    from_zz, from_yy = across(far_zz, 4), across(far_yy, 2)
    on_y, on_z = first_step(far_y0, from_zd, far_z1, from_yd)
    far_sum, *near_sent = total(
        [far_own, from_zz, from_yy, across(on_y, 2), across(on_z, 4)], near_sent
    )
    backs = [
        groups_on(far_sum[(count - 1) * cap : count * cap], groups - count)
        for count in range(1, groups)
    ]
    from_zd, from_yd, from_zz, from_yy = (
        across(value, bit) for value, bit in zip(near_sent, (4, 2, 4, 2))
    )
    on_y, on_z = first_step(near_y0, from_zd, near_z1, from_yd)
    near_sums = [near_own, from_zz, from_yy, across(on_y, 2), across(on_z, 4)]
    output = finish(hidden, gates, flat, near_sums, backs, groups, cap)
    return output.reshape(1, 1, tokens, width)


def solution(mesh):
    return jax.shard_map(
        body,
        mesh=mesh,
        in_specs=(
            P("expert", "pipe", None, None),
            P("expert", "pipe", None, None),
            P("expert", "pipe", None, None),
            P(),
            P(None, "expert"),
            P("expert", None),
            P("expert", "pipe", None),
            P("expert", "pipe", None),
            P("expert", "pipe", None),
        ),
        out_specs=P("expert", "pipe", None, None),
        check_vma=False,
    )
```

```python
import functools
import math

import jax
import jax.numpy as jnp
from jax import lax
from jax.experimental import pallas as pl
from jax.experimental.pallas import tpu as pltpu
from jax.sharding import PartitionSpec as P

HEADS = 16
HD = 128
WSPLIT = 8
EPS = 1e-06
VMEM_LIMIT = 32 * 1024 * 1024

VMEM = pl.BlockSpec(memory_space=pltpu.VMEM)
SMEM = pl.BlockSpec(memory_space=pltpu.SMEM)
ANY = pl.BlockSpec(memory_space=pl.ANY)


def struct(shape, dtype=jnp.bfloat16):
    return jax.ShapeDtypeStruct(shape, dtype)


def call(
    kernel, outs, in_specs, name, flops, moved, out_specs=None, aliases=None
):
    return pl.pallas_call(
        kernel,
        out_shape=outs,
        in_specs=in_specs,
        out_specs=out_specs or jax.tree.map(lambda _: VMEM, outs),
        input_output_aliases=aliases or {},
        compiler_params=pltpu.CompilerParams(vmem_limit_bytes=VMEM_LIMIT),
        cost_estimate=pl.CostEstimate(flops=flops, bytes_accessed=moved, transcendentals=0),
        name=name,
    )


def as_column(row):
    count = row.shape[1]
    down = lax.broadcasted_iota(jnp.int32, (count, count), 0)
    along = lax.broadcasted_iota(jnp.int32, (count, count), 1)
    return jnp.sum(jnp.where(down == along, row, jnp.zeros_like(row)), axis=1, keepdims=True)


def stage_kernel(groups, cap, *refs):
    group_ref, state_in, query_in, gain_in, expert_ref, slot_ref, gate_ref = refs[:7]
    state_out, query_out, gain_out, flat_row, flat_column, gate_column = refs[7:]
    state_out[...] = state_in[...]
    query_out[...] = query_in[...]
    gain_out[...] = gain_in[...]
    offset = expert_ref[...] - group_ref[0]
    offset = jnp.where(offset < 0, offset + groups, offset)
    slot = slot_ref[...]
    flat = jnp.where(slot >= 0, offset * cap + slot, -1)
    flat_row[...] = flat
    flat_column[...] = as_column(flat)
    gate_column[...] = as_column(gate_ref[...])


def stage(group, state, query, gain, expert_id, slot, gate, groups, cap):
    tokens, width = state.shape
    outs = [
        struct((tokens, width)),
        struct((tokens, width)),
        struct((1, width), jnp.float32),
        struct((1, tokens), jnp.int32),
        struct((tokens, 1), jnp.int32),
        struct((tokens, 1), jnp.float32),
    ]
    return call(
        functools.partial(stage_kernel, groups, cap),
        outs,
        [SMEM] + [VMEM] * 6,
        "stage",
        tokens * tokens,
        8 * tokens * width,
    )(group, state, query, gain, expert_id, slot, gate)


def gate_kernel(*refs):
    pass


def after_all(values, others):
    return call(
        gate_kernel,
        [struct(value.shape) for value in values],
        [ANY] * (len(values) + len(others)),
        "hand_on",
        1,
        1,
        out_specs=[ANY] * len(values),
        aliases={i: i for i in range(len(values))},
    )(*values, *others)


def attend_kernel(pieces, groups, cap, *refs):
    state_ref, query_ref, gain_ref, flat_ref = refs[:4]
    kv_refs = refs[4 : 4 + pieces]
    hidden_ref = refs[-1 - groups]
    packed_refs = refs[-groups:]
    tokens, width = state_ref.shape
    local = kv_refs[0].shape[0] // 2
    scale = 1.0 / math.sqrt(HD)
    squares = jnp.zeros((tokens, HD), jnp.float32)
    for head in range(HEADS):
        cols = slice(head * HD, (head + 1) * HD)
        keys = jnp.concatenate([r[:local, cols] for r in kv_refs], axis=0)
        values = jnp.concatenate([r[local:, cols] for r in kv_refs], axis=0)
        scores = (
            lax.dot_general(
                query_ref[:, cols],
                keys,
                (((1,), (1,)), ((), ())),
                preferred_element_type=jnp.float32,
            )
            * scale
        )
        raised = jnp.exp(scores - jnp.max(scores, axis=1, keepdims=True))
        total = jnp.sum(raised, axis=1, keepdims=True)
        mixed = jnp.dot(raised.astype(jnp.bfloat16), values, preferred_element_type=jnp.float32)
        hidden = state_ref[:, cols].astype(jnp.float32) + mixed / total
        hidden_ref[:, cols] = hidden
        squares = squares + hidden * hidden
    mean_square = jnp.sum(squares, axis=1, keepdims=True) * (1.0 / width)
    inverse = lax.rsqrt(mean_square + EPS)
    rows = lax.broadcasted_iota(jnp.int32, (groups * cap, tokens), 0)
    selector = (rows == flat_ref[...]).astype(jnp.float32).astype(jnp.bfloat16)
    step = 512
    for at in range(0, width, step):
        cols = slice(at, at + step)
        normed = (hidden_ref[:, cols] * inverse * gain_ref[:, cols]).astype(jnp.bfloat16)
        packed = jnp.dot(selector, normed, preferred_element_type=jnp.float32).astype(jnp.bfloat16)
        for group in range(groups):
            packed_refs[group][:, cols] = packed[group * cap : (group + 1) * cap]


def attend(state, query, gain, flat, kv_pieces, groups, cap, after):
    tokens, width = state.shape
    outs = [struct((tokens, width), jnp.float32)] + [struct((cap, width))] * groups
    pieces = len(kv_pieces)
    return call(
        functools.partial(attend_kernel, pieces, groups, cap),
        outs,
        [VMEM] * (4 + pieces) + [ANY] * len(after),
        "attend",
        4 * tokens * pieces * kv_pieces[0].shape[0] * width,
        12 * tokens * width,
    )(state, query, gain, flat, *kv_pieces, *after)


def ffn_kernel(counts, cut, *refs):
    blocks = []
    for count in counts:
        parts, refs = refs[:count], refs[count:]
        blocks.append(jnp.concatenate([r[...] for r in parts], axis=1))
    in_a, in_b, out_a, out_b = refs[:4]
    own_ref, zd_ref, yd_ref, zz_ref, yy_ref, y0_ref, z1_ref = refs[-7:]
    rows, width = blocks[0].shape
    entries = jnp.concatenate(blocks, axis=0)
    w_in = jnp.concatenate([in_a[...], in_b[...]], axis=1)
    raw = jnp.dot(entries, w_in, preferred_element_type=jnp.float32)
    activation = jnp.maximum(raw, 0.0).astype(jnp.bfloat16)
    step = 512
    for at in range(0, width, step):
        cols = slice(at, at + step)
        w_out = jnp.concatenate([out_a[:, cols], out_b[:, cols]], axis=0)
        part = jnp.dot(activation, w_out, preferred_element_type=jnp.float32)
        part = part.astype(jnp.bfloat16)
        own_ref[:, cols] = part[:rows]
        y_part, z_part, d_part = (part[i * rows : (i + 1) * rows] for i in (1, 2, 3))
        if at < cut:
            y0_ref[:, cols] = y_part
            zz_ref[:, cols] = z_part
            zd_ref[:, cols] = d_part
        else:
            cols = slice(at - cut, at - cut + step)
            z1_ref[:, cols] = z_part
            yy_ref[:, cols] = y_part
            yd_ref[:, cols] = d_part


def ffn(blocks, weights, cut, after=()):
    rows = blocks[0][0].shape[0]
    width, units = weights[0].shape
    rest = width - cut
    outs = [struct((rows, size)) for size in (width, cut, rest, cut, rest, cut, rest)]
    counts = [len(parts) for parts in blocks]
    return call(
        functools.partial(ffn_kernel, counts, cut),
        outs,
        [VMEM] * (sum(counts) + 4) + [ANY] * len(after),
        "expert_ffn",
        4 * 4 * rows * width * units * 2,
        8 * units * width + 16 * rows * width,
    )(*sum(blocks, []), *weights, *after)


def first_kernel(y0_ref, zd_ref, z1_ref, yd_ref, y_ref, z_ref):
    for own, other, out in ((y0_ref, zd_ref, y_ref), (z1_ref, yd_ref, z_ref)):
        out[...] = (own[...].astype(jnp.float32) + other[...].astype(jnp.float32)).astype(
            jnp.bfloat16
        )


def first_step(y0, from_zd, z1, from_yd):
    return call(
        first_kernel,
        [struct(y0.shape), struct(z1.shape)],
        [VMEM] * 4,
        "first_step",
        y0.size + z1.size,
        6 * (y0.size + z1.size),
    )(y0, from_zd, z1, from_yd)


def add_up(own_ref, zz_ref, yy_ref, by_ref, bz_ref, cols):
    cut = zz_ref.shape[1]
    whole = slice(*cols)
    if cols[0] < cut:
        first, second, part = zz_ref, by_ref, whole
    else:
        first, second, part = yy_ref, bz_ref, slice(cols[0] - cut, cols[1] - cut)
    return (
        own_ref[:, whole].astype(jnp.float32)
        + first[:, part].astype(jnp.float32)
        + second[:, part].astype(jnp.float32)
    ).astype(jnp.bfloat16)


def total_kernel(held, *refs):
    out_ref = refs[5 + held]
    for at in range(0, out_ref.shape[1], 512):
        out_ref[:, at : at + 512] = add_up(*refs[:5], (at, at + 512))


def total(sums, held):
    rows, width = sums[0].shape
    outs = [struct((rows, width))] + [struct(value.shape) for value in held]
    return call(
        functools.partial(total_kernel, len(held)),
        outs,
        [VMEM] * 5 + [ANY] * len(held),
        "far_total",
        3 * rows * width,
        8 * rows * width,
        out_specs=[VMEM] + [ANY] * len(held),
        aliases={5 + i: 1 + i for i in range(len(held))},
    )(*sums, *held)


def finish_kernel(groups, cap, *refs):
    hidden_ref, gate_ref, flat_ref = refs[:3]
    sums = refs[3:8]
    back_refs = refs[8:-1]
    out_ref = refs[-1]
    tokens, width = hidden_ref.shape
    slots = lax.broadcasted_iota(jnp.int32, (tokens, groups * cap), 1)
    picker = (slots == flat_ref[...]).astype(jnp.float32).astype(jnp.bfloat16)
    step = 512
    for at in range(0, width, step):
        cols = slice(at, at + step)
        near = add_up(*sums, (at, at + step))
        found = jnp.concatenate([near] + [r[:, cols] for r in back_refs], axis=0)
        picked = jnp.dot(picker, found, preferred_element_type=jnp.float32)
        out_ref[:, cols] = (hidden_ref[:, cols] + gate_ref[...] * picked).astype(jnp.bfloat16)


def finish(hidden, gate, flat, sums, backs, groups, cap):
    tokens, width = hidden.shape
    operands = [hidden, gate, flat, *sums, *backs]
    return call(
        functools.partial(finish_kernel, groups, cap),
        struct((tokens, width)),
        [VMEM] * len(operands),
        "finish",
        4 * tokens * cap * groups * width,
        16 * tokens * width,
    )(*operands)


def body(state, query, enc_kv, gain, w_in, w_out, expert_id, slot, gate):
    tokens, width = state.shape[2:]
    devices = lax.axis_size("expert")
    pipes = lax.axis_size("pipe")
    groups = devices // WSPLIT
    cap = 3 * tokens // (2 * groups)
    half = width // 2
    far_cut, near_cut = width // 2, width // 4

    def across(value, bit):
        return lax.ppermute(value, "expert", [(i, i ^ bit) for i in range(devices)])

    def groups_on(value, count):
        shift = count * WSPLIT
        return lax.ppermute(value, "expert", [(i, (i + shift) % devices) for i in range(devices)])

    kv = jnp.transpose(enc_kv[0], (1, 0, 2)).reshape(-1, width)
    kv_pieces = [kv]
    for shift in range(1, pipes):
        perm = [(i, (i + shift) % pipes) for i in range(pipes)]
        kv_pieces.append(lax.ppermute(kv, "pipe", perm))
    weights = [w_in, across(w_in, 1), w_out, across(w_out, 1)]

    group = (lax.axis_index("expert") // WSPLIT).astype(jnp.int32).reshape(1)
    staged = stage(
        group,
        state[0, 0],
        query[0, 0],
        gain.reshape(1, width),
        expert_id[0],
        slot[0],
        gate[0],
        groups,
        cap,
    )
    flat, gates = staged[4:]
    hidden, near, *packed = attend(
        *staged[:4], kv_pieces, groups, cap, after=[weights[1], weights[3]]
    )
    far = [groups_on(block, count) for count, block in enumerate(packed, 1)]
    far = jnp.concatenate(far, axis=0) if len(far) > 1 else far[0]

    near_y, near_z = across(near, 2), across(near, 4)
    near_blocks = [[near], [near_y], [near_z], [across(near_z, 2)]]
    (far,) = after_all([far], [near_y, near_z])
    left, right = far[:, :half], far[:, half:]
    y_left, z_right = across(left, 2), across(right, 4)
    y_right, z_left = across(right, 2), across(left, 4)
    far_blocks = [
        [far],
        [y_left, y_right],
        [z_left, z_right],
        [across(y_left, 4), across(z_right, 2)],
    ]

    far_own, far_zd, far_yd, far_zz, far_yy, far_y0, far_z1 = ffn(far_blocks, weights, far_cut)
    near_own, *near_sent, near_y0, near_z1 = ffn(
        near_blocks, weights, near_cut, after=[far_y0, far_z1]
    )
    from_zd, from_yd = across(far_zd, 4), across(far_yd, 2)
    far_zz, far_yy = after_all([far_zz, far_yy], [near_y0])
    from_zz, from_yy = across(far_zz, 4), across(far_yy, 2)
    on_y, on_z = first_step(far_y0, from_zd, far_z1, from_yd)
    far_sum, *near_sent = total(
        [far_own, from_zz, from_yy, across(on_y, 2), across(on_z, 4)], near_sent
    )
    backs = [
        groups_on(far_sum[(count - 1) * cap : count * cap], groups - count)
        for count in range(1, groups)
    ]
    from_zd, from_yd, from_zz, from_yy = (
        across(value, bit) for value, bit in zip(near_sent, (4, 2, 4, 2))
    )
    on_y, on_z = first_step(near_y0, from_zd, near_z1, from_yd)
    near_sums = [near_own, from_zz, from_yy, across(on_y, 2), across(on_z, 4)]
    output = finish(hidden, gates, flat, near_sums, backs, groups, cap)
    return output.reshape(1, 1, tokens, width)


def solution(mesh):
    return jax.shard_map(
        body,
        mesh=mesh,
        in_specs=(
            P("expert", "pipe", None, None),
            P("expert", "pipe", None, None),
            P("expert", "pipe", None, None),
            P(),
            P(None, "expert"),
            P("expert", None),
            P("expert", "pipe", None),
            P("expert", "pipe", None),
            P("expert", "pipe", None),
        ),
        out_specs=P("expert", "pipe", None, None),
        check_vma=False,
    )
```

```python
import functools
import math

import jax
import jax.numpy as jnp
from jax import lax
from jax.experimental import pallas as pl
from jax.experimental.pallas import tpu as pltpu
from jax.sharding import PartitionSpec as P

HEADS = 16
HD = 128
WSPLIT = 8
EPS = 1e-06
FAR_WEIGHT = 3_000_000_000
FAR_STEPS = 4
CROSS_WEIGHT = 1
VMEM_LIMIT = 32 * 1024 * 1024

VMEM = pl.BlockSpec(memory_space=pltpu.VMEM)
SMEM = pl.BlockSpec(memory_space=pltpu.SMEM)
ANY = pl.BlockSpec(memory_space=pl.ANY)


def struct(shape, dtype=jnp.bfloat16):
    return jax.ShapeDtypeStruct(shape, dtype)


def call(
    kernel, outs, in_specs, name, flops, moved, scratch=(), out_specs=None, aliases=None
):
    return pl.pallas_call(
        kernel,
        out_shape=outs,
        in_specs=in_specs,
        out_specs=out_specs or jax.tree.map(lambda _: VMEM, outs),
        scratch_shapes=list(scratch),
        input_output_aliases=aliases or {},
        compiler_params=pltpu.CompilerParams(vmem_limit_bytes=VMEM_LIMIT),
        cost_estimate=pl.CostEstimate(flops=flops, bytes_accessed=moved, transcendentals=0),
        name=name,
    )


def as_column(row):
    count = row.shape[1]
    down = lax.broadcasted_iota(jnp.int32, (count, count), 0)
    along = lax.broadcasted_iota(jnp.int32, (count, count), 1)
    return jnp.sum(jnp.where(down == along, row, jnp.zeros_like(row)), axis=1, keepdims=True)


def stage_kernel(groups, cap, *refs):
    group_ref, state_in, query_in, gain_in, expert_ref, slot_ref, gate_ref = refs[:7]
    state_out, query_out, gain_out, flat_row, flat_column, gate_column = refs[7:]
    state_out[...] = state_in[...]
    query_out[...] = query_in[...]
    gain_out[...] = gain_in[...]
    offset = expert_ref[...] - group_ref[0]
    offset = jnp.where(offset < 0, offset + groups, offset)
    slot = slot_ref[...]
    flat = jnp.where(slot >= 0, offset * cap + slot, -1)
    flat_row[...] = flat
    flat_column[...] = as_column(flat)
    gate_column[...] = as_column(gate_ref[...])


def stage(group, state, query, gain, expert_id, slot, gate, groups, cap):
    tokens, width = state.shape
    outs = [
        struct((tokens, width)),
        struct((tokens, width)),
        struct((1, width), jnp.float32),
        struct((1, tokens), jnp.int32),
        struct((tokens, 1), jnp.int32),
        struct((tokens, 1), jnp.float32),
    ]
    return call(
        functools.partial(stage_kernel, groups, cap),
        outs,
        [SMEM] + [VMEM] * 6,
        "stage",
        tokens * tokens,
        8 * tokens * width,
    )(group, state, query, gain, expert_id, slot, gate)


def gate_kernel(*refs):
    pass


def after_all(values, others, weight=1):
    return call(
        gate_kernel,
        [struct(value.shape) for value in values],
        [ANY] * (len(values) + len(others)),
        "hand_on",
        weight,
        1,
        out_specs=[ANY] * len(values),
        aliases={i: i for i in range(len(values))},
    )(*values, *others)


def attend_kernel(pieces, groups, cap, *refs):
    state_ref, query_ref, gain_ref, flat_ref = refs[:4]
    kv_refs = refs[4 : 4 + pieces]
    hidden_ref = refs[-1 - groups]
    packed_refs = refs[-groups:]
    tokens, width = state_ref.shape
    local = kv_refs[0].shape[0] // 2
    scale = 1.0 / math.sqrt(HD)
    squares = jnp.zeros((tokens, HD), jnp.float32)
    for head in range(HEADS):
        cols = slice(head * HD, (head + 1) * HD)
        keys = jnp.concatenate([r[:local, cols] for r in kv_refs], axis=0)
        values = jnp.concatenate([r[local:, cols] for r in kv_refs], axis=0)
        scores = (
            lax.dot_general(
                query_ref[:, cols],
                keys,
                (((1,), (1,)), ((), ())),
                preferred_element_type=jnp.float32,
            )
            * scale
        )
        raised = jnp.exp(scores - jnp.max(scores, axis=1, keepdims=True))
        total = jnp.sum(raised, axis=1, keepdims=True)
        mixed = jnp.dot(raised.astype(jnp.bfloat16), values, preferred_element_type=jnp.float32)
        hidden = state_ref[:, cols].astype(jnp.float32) + mixed / total
        hidden_ref[:, cols] = hidden
        squares = squares + hidden * hidden
    mean_square = jnp.sum(squares, axis=1, keepdims=True) * (1.0 / width)
    inverse = lax.rsqrt(mean_square + EPS)
    rows = lax.broadcasted_iota(jnp.int32, (groups * cap, tokens), 0)
    selector = (rows == flat_ref[...]).astype(jnp.float32).astype(jnp.bfloat16)
    step = 512
    for at in range(0, width, step):
        cols = slice(at, at + step)
        normed = (hidden_ref[:, cols] * inverse * gain_ref[:, cols]).astype(jnp.bfloat16)
        packed = jnp.dot(selector, normed, preferred_element_type=jnp.float32).astype(jnp.bfloat16)
        for group in range(groups):
            packed_refs[group][:, cols] = packed[group * cap : (group + 1) * cap]


def attend(state, query, gain, flat, kv_pieces, groups, cap, after):
    tokens, width = state.shape
    outs = [struct((tokens, width), jnp.float32)] + [struct((cap, width))] * groups
    pieces = len(kv_pieces)
    return call(
        functools.partial(attend_kernel, pieces, groups, cap),
        outs,
        [VMEM] * (4 + pieces) + [ANY] * len(after),
        "attend",
        4 * tokens * pieces * kv_pieces[0].shape[0] * width,
        12 * tokens * width,
    )(state, query, gain, flat, *kv_pieces, *after)


def place(pipes, shift, pipe, size):
    at = pipe - shift
    at = jnp.where(at < 0, at + pipes, at)
    return pl.multiple_of(at * size, size)


def up_kernel(pipes, *refs):
    pipe = refs[0][0]
    own_in, z_in, w_own, w_pair = refs[1:5]
    y_parts = refs[5 : 5 + pipes]
    pair_parts = refs[5 + pipes : 5 + 2 * pipes]
    out_ref, entries = refs[-2:]
    rows, width = own_in.shape
    units = w_own.shape[1]
    entries[:rows] = own_in[...]
    entries[rows:] = z_in[...]
    weights = jnp.concatenate([w_own[...], w_pair[...]], axis=1)
    raw = jnp.dot(entries[...], weights, preferred_element_type=jnp.float32)
    out_ref[:, : 2 * units] = jnp.maximum(raw, 0.0).astype(jnp.bfloat16)
    depth = width // pipes
    raw = jnp.zeros_like(raw)
    for shift in range(pipes):
        part = entries[:, pl.ds(place(pipes, shift, pipe, depth), depth)]
        weights = jnp.concatenate([y_parts[shift][...], pair_parts[shift][...]], axis=1)
        raw = raw + jnp.dot(part, weights, preferred_element_type=jnp.float32)
    out_ref[:, 2 * units :] = jnp.maximum(raw, 0.0).astype(jnp.bfloat16)


def up(pipe, own, z, w_in, y_parts, pair_parts, after=()):
    rows, width = own.shape
    units = w_in[0].shape[1]
    pipes = len(y_parts)
    return call(
        functools.partial(up_kernel, pipes),
        struct((2 * rows, 4 * units)),
        [SMEM] + [VMEM] * (4 + 2 * pipes) + [ANY] * len(after),
        "expert_up",
        16 * rows * width * units,
        8 * units * width,
        scratch=[pltpu.VMEM((2 * rows, width), jnp.bfloat16)],
    )(pipe, own, z, *w_in, *y_parts, *pair_parts, *after)


def down_kernel(pipes, *refs):
    pipe = refs[0][0]
    act_ref, w_own, w_pair = refs[1:4]
    y_parts, refs = refs[4 : 4 + pipes], refs[4 + pipes :]
    pair_parts, refs = refs[:pipes], refs[pipes:]
    y_rest, pair_rest = refs[:2]
    own_ref, z_ref, held = refs[-3:]
    rows, width = own_ref.shape
    units = w_own.shape[0]
    size = y_parts[0].shape[0]
    for shift in range(pipes):
        at = place(pipes, shift, pipe, size)
        held[pl.ds(at, size)] = y_parts[shift][...]
        held[pl.ds(pl.multiple_of(units + at, size), size)] = pair_parts[shift][...]
    held[pipes * size : units] = y_rest[...]
    held[units + pipes * size :] = pair_rest[...]
    step = 512
    for at in range(0, width, step):
        cols = slice(at, at + step)
        weights = jnp.concatenate([w_own[:, cols], w_pair[:, cols], held[:, cols]], axis=0)
        part = jnp.dot(act_ref[...], weights, preferred_element_type=jnp.float32)
        part = part.astype(jnp.bfloat16)
        own_ref[:, cols] = part[:rows]
        z_ref[:, cols] = part[rows:]


def down(pipe, act, w_out, y_parts, pair_parts, rests, after=()):
    rows = act.shape[0] // 2
    units, width = w_out[0].shape
    pipes = len(y_parts)
    return call(
        functools.partial(down_kernel, pipes),
        [struct((rows, width))] * 2,
        [SMEM] + [VMEM] * (5 + 2 * pipes) + [ANY] * len(after),
        "expert_down",
        16 * rows * width * units,
        8 * units * width,
        scratch=[pltpu.VMEM((2 * units, width), jnp.bfloat16)],
    )(pipe, act, *w_out, *y_parts, *pair_parts, *rests, *after)


def total_kernel(held, own_ref, z_ref, *refs):
    refs[held][...] = (own_ref[...].astype(jnp.float32) + z_ref[...].astype(jnp.float32)).astype(
        jnp.bfloat16
    )


def total(own, z, held):
    outs = [struct(own.shape)] + [struct(value.shape) for value in held]
    return call(
        functools.partial(total_kernel, len(held)),
        outs,
        [VMEM] * 2 + [ANY] * len(held),
        "far_total",
        own.size,
        6 * own.size,
        out_specs=[VMEM] + [ANY] * len(held),
        aliases={2 + i: 1 + i for i in range(len(held))},
    )(own, z, *held)


def finish_kernel(groups, cap, *refs):
    hidden_ref, gate_ref, flat_ref = refs[:3]
    own_ref, z_ref = refs[3:5]
    back_refs = refs[5:-1]
    out_ref = refs[-1]
    tokens, width = hidden_ref.shape
    slots = lax.broadcasted_iota(jnp.int32, (tokens, groups * cap), 1)
    picker = (slots == flat_ref[...]).astype(jnp.float32).astype(jnp.bfloat16)
    step = 512
    for at in range(0, width, step):
        cols = slice(at, at + step)
        near = (own_ref[:, cols].astype(jnp.float32) + z_ref[:, cols].astype(jnp.float32)).astype(
            jnp.bfloat16
        )
        found = jnp.concatenate([near] + [r[:, cols] for r in back_refs], axis=0)
        picked = jnp.dot(picker, found, preferred_element_type=jnp.float32)
        out_ref[:, cols] = (hidden_ref[:, cols] + gate_ref[...] * picked).astype(jnp.bfloat16)


def finish(hidden, gate, flat, sums, backs, groups, cap):
    tokens, width = hidden.shape
    operands = [hidden, gate, flat, *sums, *backs]
    return call(
        functools.partial(finish_kernel, groups, cap),
        struct((tokens, width)),
        [VMEM] * len(operands),
        "finish",
        4 * tokens * cap * groups * width,
        16 * tokens * width,
    )(*operands)


def body(state, query, enc_kv, gain, w_in, w_out, expert_id, slot, gate):
    tokens, width = state.shape[2:]
    devices = lax.axis_size("expert")
    pipes = lax.axis_size("pipe")
    groups = devices // WSPLIT
    cap = 3 * tokens // (2 * groups)

    def across(value, bit):
        return lax.ppermute(value, "expert", [(i, i ^ bit) for i in range(devices)])

    def groups_on(value, count):
        shift = count * WSPLIT
        return lax.ppermute(value, "expert", [(i, (i + shift) % devices) for i in range(devices)])

    kv = jnp.transpose(enc_kv[0], (1, 0, 2)).reshape(-1, width)
    kv_pieces = [kv]
    for shift in range(1, pipes):
        perm = [(i, (i + shift) % pipes) for i in range(pipes)]
        kv_pieces.append(lax.ppermute(kv, "pipe", perm))
    def along(value):
        perms = [[(i, (i + shift) % pipes) for i in range(pipes)] for shift in range(1, pipes)]
        return [value] + [lax.ppermute(value, "pipe", perm) for perm in perms]

    def paired(parts):
        return [across(value, 1) for value in parts]

    pipe = lax.axis_index("pipe").astype(jnp.int32)
    w_in_pair, w_out_pair = across(w_in, 1), across(w_out, 1)
    units = w_in.shape[1]
    depth, size = width // pipes, units // 2 // pipes // 16 * 16
    in_part = lax.dynamic_slice_in_dim(w_in, pipe * depth, depth, 0)
    out_part = lax.dynamic_slice_in_dim(w_out, pipe * size, size, 0)
    out_rest = w_out[pipes * size :]
    pipe = pipe.reshape(1)
    in_y = across(in_part, 2)

    group = (lax.axis_index("expert") // WSPLIT).astype(jnp.int32).reshape(1)
    staged = stage(
        group,
        state[0, 0],
        query[0, 0],
        gain.reshape(1, width),
        expert_id[0],
        slot[0],
        gate[0],
        groups,
        cap,
    )
    flat, gates = staged[4:]
    hidden, near, *packed = attend(
        *staged[:4], kv_pieces, groups, cap, after=[w_in_pair, w_out_pair]
    )
    far = [groups_on(block, count) for count, block in enumerate(packed, 1)]
    far = jnp.concatenate(far, axis=0) if len(far) > 1 else far[0]

    (in_y,) = after_all([in_y], [near])
    out_part, out_rest = after_all([out_part, out_rest], [in_y])
    in_y = after_all(along(in_y), [])
    in_pair = paired(in_y)
    out_y = across(out_part, 2)
    out_y = after_all(along(out_y), [])
    out_pair = paired(out_y)
    rest_y = across(out_rest, 2)
    rests = [rest_y, across(rest_y, 1)]

    near_z = across(near, 4)
    (far,) = after_all([far], [near_z], CROSS_WEIGHT)
    far_z = across(far, 4)
    for _ in range(FAR_STEPS):
        (far_z,) = after_all([far_z], [], FAR_WEIGHT)

    def experts_up(own, z, after=()):
        return up(pipe, own, z, [w_in, w_in_pair], in_y, in_pair, after)

    def experts_down(act, after=()):
        return down(pipe, act, [w_out, w_out_pair], out_y, out_pair, rests, after)

    far_own, far_sent = experts_down(experts_up(far, far_z))
    near_own, near_sent = experts_down(experts_up(near, near_z, [far_own]))
    far_sum, near_sent = total(far_own, across(far_sent, 4), [near_sent])
    backs = [
        groups_on(far_sum[(count - 1) * cap : count * cap], groups - count)
        for count in range(1, groups)
    ]
    near_sums = [near_own, across(near_sent, 4)]
    output = finish(hidden, gates, flat, near_sums, backs, groups, cap)
    return output.reshape(1, 1, tokens, width)


def solution(mesh):
    return jax.shard_map(
        body,
        mesh=mesh,
        in_specs=(
            P("expert", "pipe", None, None),
            P("expert", "pipe", None, None),
            P("expert", "pipe", None, None),
            P(),
            P(None, "expert"),
            P("expert", None),
            P("expert", "pipe", None),
            P("expert", "pipe", None),
            P("expert", "pipe", None),
        ),
        out_specs=P("expert", "pipe", None, None),
        check_vma=False,
    )
```

```python
import functools
import math

import jax
import jax.numpy as jnp
from jax import lax
from jax.experimental import pallas as pl
from jax.experimental.pallas import tpu as pltpu
from jax.sharding import PartitionSpec as P

HEADS = 16
HD = 128
WSPLIT = 8
EPS = 1e-06
FAR_WEIGHT = 3_000_000_000
FAR_STEPS = 4
CROSS_STEPS = 1
CROSS_WEIGHT = 3_000_000_000
BACK_WEIGHT = 10_000_000_000
VMEM_LIMIT = 32 * 1024 * 1024
PART_LIMIT = 60 * 1024 * 1024

VMEM = pl.BlockSpec(memory_space=pltpu.VMEM)
SMEM = pl.BlockSpec(memory_space=pltpu.SMEM)
ANY = pl.BlockSpec(memory_space=pl.ANY)


def struct(shape, dtype=jnp.bfloat16):
    return jax.ShapeDtypeStruct(shape, dtype)


def call(
    kernel, outs, in_specs, name, flops, moved, scratch=(), out_specs=None, aliases=None, limit=VMEM_LIMIT
):
    return pl.pallas_call(
        kernel,
        out_shape=outs,
        in_specs=in_specs,
        out_specs=out_specs or jax.tree.map(lambda _: VMEM, outs),
        scratch_shapes=list(scratch),
        input_output_aliases=aliases or {},
        compiler_params=pltpu.CompilerParams(vmem_limit_bytes=limit),
        cost_estimate=pl.CostEstimate(flops=flops, bytes_accessed=moved, transcendentals=0),
        name=name,
    )


def as_column(row):
    count = row.shape[1]
    down = lax.broadcasted_iota(jnp.int32, (count, count), 0)
    along = lax.broadcasted_iota(jnp.int32, (count, count), 1)
    return jnp.sum(jnp.where(down == along, row, jnp.zeros_like(row)), axis=1, keepdims=True)


def stage_kernel(groups, cap, *refs):
    group_ref, state_in, query_in, gain_in, expert_ref, slot_ref, gate_ref = refs[:7]
    state_out, query_out, gain_out, flat_row, flat_column, gate_column = refs[7:]
    state_out[...] = state_in[...]
    query_out[...] = query_in[...]
    gain_out[...] = gain_in[...]
    offset = expert_ref[...] - group_ref[0]
    offset = jnp.where(offset < 0, offset + groups, offset)
    slot = slot_ref[...]
    flat = jnp.where(slot >= 0, offset * cap + slot, -1)
    flat_row[...] = flat
    flat_column[...] = as_column(flat)
    gate_column[...] = as_column(gate_ref[...])


def stage(group, state, query, gain, expert_id, slot, gate, groups, cap):
    tokens, width = state.shape
    outs = [
        struct((tokens, width)),
        struct((tokens, width)),
        struct((1, width), jnp.float32),
        struct((1, tokens), jnp.int32),
        struct((tokens, 1), jnp.int32),
        struct((tokens, 1), jnp.float32),
    ]
    return call(
        functools.partial(stage_kernel, groups, cap),
        outs,
        [SMEM] + [VMEM] * 6,
        "stage",
        tokens * tokens,
        8 * tokens * width,
    )(group, state, query, gain, expert_id, slot, gate)


def gate_kernel(*refs):
    pass


def after_all(values, others, weight=1):
    return call(
        gate_kernel,
        [struct(value.shape) for value in values],
        [ANY] * (len(values) + len(others)),
        "hand_on",
        weight,
        1,
        out_specs=[ANY] * len(values),
        aliases={i: i for i in range(len(values))},
    )(*values, *others)


def attend_kernel(pieces, groups, cap, *refs):
    state_ref, query_ref, gain_ref, flat_ref = refs[:4]
    kv_refs = refs[4 : 4 + pieces]
    hidden_ref = refs[-1 - groups]
    packed_refs = refs[-groups:]
    tokens, width = state_ref.shape
    local = kv_refs[0].shape[0] // 2
    scale = 1.0 / math.sqrt(HD)
    squares = jnp.zeros((tokens, HD), jnp.float32)
    for head in range(HEADS):
        cols = slice(head * HD, (head + 1) * HD)
        keys = jnp.concatenate([r[:local, cols] for r in kv_refs], axis=0)
        values = jnp.concatenate([r[local:, cols] for r in kv_refs], axis=0)
        scores = (
            lax.dot_general(
                query_ref[:, cols],
                keys,
                (((1,), (1,)), ((), ())),
                preferred_element_type=jnp.float32,
            )
            * scale
        )
        raised = jnp.exp(scores - jnp.max(scores, axis=1, keepdims=True))
        total = jnp.sum(raised, axis=1, keepdims=True)
        mixed = jnp.dot(raised.astype(jnp.bfloat16), values, preferred_element_type=jnp.float32)
        hidden = state_ref[:, cols].astype(jnp.float32) + mixed / total
        hidden_ref[:, cols] = hidden
        squares = squares + hidden * hidden
    mean_square = jnp.sum(squares, axis=1, keepdims=True) * (1.0 / width)
    inverse = lax.rsqrt(mean_square + EPS)
    rows = lax.broadcasted_iota(jnp.int32, (groups * cap, tokens), 0)
    selector = (rows == flat_ref[...]).astype(jnp.float32).astype(jnp.bfloat16)
    step = 512
    for at in range(0, width, step):
        cols = slice(at, at + step)
        normed = (hidden_ref[:, cols] * inverse * gain_ref[:, cols]).astype(jnp.bfloat16)
        packed = jnp.dot(selector, normed, preferred_element_type=jnp.float32).astype(jnp.bfloat16)
        for group in range(groups):
            packed_refs[group][:, cols] = packed[group * cap : (group + 1) * cap]


def attend(state, query, gain, flat, kv_pieces, groups, cap, after):
    tokens, width = state.shape
    outs = [struct((tokens, width), jnp.float32)] + [struct((cap, width))] * groups
    pieces = len(kv_pieces)
    return call(
        functools.partial(attend_kernel, pieces, groups, cap),
        outs,
        [VMEM] * (4 + pieces) + [ANY] * len(after),
        "attend",
        4 * tokens * pieces * kv_pieces[0].shape[0] * width,
        12 * tokens * width,
    )(state, query, gain, flat, *kv_pieces, *after)


def place(pipes, shift, pipe, size):
    at = pipe - shift
    at = jnp.where(at < 0, at + pipes, at)
    return pl.multiple_of(at * size, size)


def part_kernel(pipes, pipe_ref, w_in, w_out, in_part, out_part, out_rest, sems):
    depth, size = in_part.shape[0], out_part.shape[0]
    pipe = pipe_ref[0]
    copies = [
        pltpu.make_async_copy(source, target, sems.at[i])
        for i, (source, target) in enumerate(
            (
                (w_in.at[pl.ds(pl.multiple_of(pipe * depth, depth), depth)], in_part),
                (w_out.at[pl.ds(pl.multiple_of(pipe * size, size), size)], out_part),
                (w_out.at[pipes * size :], out_rest),
            )
        )
    ]
    for copy in copies:
        copy.start()
    for copy in copies:
        copy.wait()


def parts(pipe, w_in, w_out, pipes):
    width, units = w_in.shape
    size = units // 2 // pipes // 16 * 16
    return call(
        functools.partial(part_kernel, pipes),
        [
            struct((width // pipes, units)),
            struct((size, width)),
            struct((units - pipes * size, width)),
        ],
        [SMEM, ANY, ANY],
        "weight_parts",
        1,
        4 * units * width,
        scratch=[pltpu.SemaphoreType.DMA((3,))],
        limit=PART_LIMIT,
    )(pipe, w_in, w_out)


def up_kernel(own_in, z_in, w_own, w_pair, out_ref):
    entries = jnp.concatenate([own_in[...], z_in[...]], axis=0)
    weights = jnp.concatenate([w_own[...], w_pair[...]], axis=1)
    raw = jnp.dot(entries, weights, preferred_element_type=jnp.float32)
    out_ref[...] = jnp.maximum(raw, 0.0).astype(jnp.bfloat16)


def up(own, z, w_in):
    rows, width = own.shape
    units = w_in[0].shape[1]
    return call(
        up_kernel,
        struct((2 * rows, 2 * units)),
        [VMEM] * 4,
        "expert_up",
        8 * rows * width * units,
        4 * units * width,
    )(own, z, *w_in)


def up_y_kernel(pipes, *refs):
    pipe = refs[0][0]
    own_in, z_in = refs[1:3]
    y_parts = refs[3 : 3 + pipes]
    pair_parts = refs[3 + pipes : 3 + 2 * pipes]
    out_ref, entries = refs[-2:]
    rows, width = own_in.shape
    entries[:rows] = own_in[...]
    entries[rows:] = z_in[...]
    depth = width // pipes
    raw = jnp.zeros(out_ref.shape, jnp.float32)
    for shift in range(pipes):
        part = entries[:, pl.ds(place(pipes, shift, pipe, depth), depth)]
        weights = jnp.concatenate([y_parts[shift][...], pair_parts[shift][...]], axis=1)
        raw = raw + jnp.dot(part, weights, preferred_element_type=jnp.float32)
    out_ref[...] = jnp.maximum(raw, 0.0).astype(jnp.bfloat16)


def up_y(pipe, own, z, y_parts, pair_parts, after=()):
    rows, width = own.shape
    units = y_parts[0].shape[1]
    pipes = len(y_parts)
    return call(
        functools.partial(up_y_kernel, pipes),
        struct((2 * rows, 2 * units)),
        [SMEM] + [VMEM] * (2 + 2 * pipes) + [ANY] * len(after),
        "expert_up_y",
        8 * rows * width * units,
        4 * units * width,
        scratch=[pltpu.VMEM((2 * rows, width), jnp.bfloat16)],
    )(pipe, own, z, *y_parts, *pair_parts, *after)


def down_kernel(pipes, *refs):
    pipe = refs[0][0]
    act_ref, act_y_ref, w_own, w_pair = refs[1:5]
    y_parts, refs = refs[5 : 5 + pipes], refs[5 + pipes :]
    pair_parts, refs = refs[:pipes], refs[pipes:]
    y_rest, pair_rest = refs[:2]
    own_ref, z_ref, held = refs[-3:]
    rows, width = own_ref.shape
    units = w_own.shape[0]
    size = y_parts[0].shape[0]
    for shift in range(pipes):
        at = place(pipes, shift, pipe, size)
        held[pl.ds(at, size)] = y_parts[shift][...]
        held[pl.ds(pl.multiple_of(units + at, size), size)] = pair_parts[shift][...]
    held[pipes * size : units] = y_rest[...]
    held[units + pipes * size :] = pair_rest[...]
    step = 512
    for at in range(0, width, step):
        cols = slice(at, at + step)
        weights = jnp.concatenate([w_own[:, cols], w_pair[:, cols]], axis=0)
        part = jnp.dot(act_ref[...], weights, preferred_element_type=jnp.float32)
        part = part + jnp.dot(act_y_ref[...], held[:, cols], preferred_element_type=jnp.float32)
        part = part.astype(jnp.bfloat16)
        own_ref[:, cols] = part[:rows]
        z_ref[:, cols] = part[rows:]


def down(pipe, acts, w_out, y_parts, pair_parts, rests):
    rows = acts[0].shape[0] // 2
    units, width = w_out[0].shape
    pipes = len(y_parts)
    return call(
        functools.partial(down_kernel, pipes),
        [struct((rows, width))] * 2,
        [SMEM] + [VMEM] * (6 + 2 * pipes),
        "expert_down",
        16 * rows * width * units,
        8 * units * width,
        scratch=[pltpu.VMEM((2 * units, width), jnp.bfloat16)],
    )(pipe, *acts, *w_out, *y_parts, *pair_parts, *rests)


def total_kernel(held, own_ref, z_ref, *refs):
    refs[held][...] = (own_ref[...].astype(jnp.float32) + z_ref[...].astype(jnp.float32)).astype(
        jnp.bfloat16
    )


def total(own, z, held):
    outs = [struct(own.shape)] + [struct(value.shape) for value in held]
    return call(
        functools.partial(total_kernel, len(held)),
        outs,
        [VMEM] * 2 + [ANY] * len(held),
        "far_total",
        own.size,
        6 * own.size,
        out_specs=[VMEM] + [ANY] * len(held),
        aliases={2 + i: 1 + i for i in range(len(held))},
    )(own, z, *held)


def finish_kernel(groups, cap, *refs):
    hidden_ref, gate_ref, flat_ref = refs[:3]
    own_ref, z_ref = refs[3:5]
    back_refs = refs[5:-1]
    out_ref = refs[-1]
    tokens, width = hidden_ref.shape
    slots = lax.broadcasted_iota(jnp.int32, (tokens, groups * cap), 1)
    picker = (slots == flat_ref[...]).astype(jnp.float32).astype(jnp.bfloat16)
    step = 512
    for at in range(0, width, step):
        cols = slice(at, at + step)
        near = (own_ref[:, cols].astype(jnp.float32) + z_ref[:, cols].astype(jnp.float32)).astype(
            jnp.bfloat16
        )
        found = jnp.concatenate([near] + [r[:, cols] for r in back_refs], axis=0)
        picked = jnp.dot(picker, found, preferred_element_type=jnp.float32)
        out_ref[:, cols] = (hidden_ref[:, cols] + gate_ref[...] * picked).astype(jnp.bfloat16)


def finish(hidden, gate, flat, sums, backs, groups, cap):
    tokens, width = hidden.shape
    operands = [hidden, gate, flat, *sums, *backs]
    return call(
        functools.partial(finish_kernel, groups, cap),
        struct((tokens, width)),
        [VMEM] * len(operands),
        "finish",
        4 * tokens * cap * groups * width,
        16 * tokens * width,
    )(*operands)


def body(state, query, enc_kv, gain, w_in, w_out, expert_id, slot, gate):
    tokens, width = state.shape[2:]
    devices = lax.axis_size("expert")
    pipes = lax.axis_size("pipe")
    groups = devices // WSPLIT
    cap = 3 * tokens // (2 * groups)

    def across(value, bit):
        return lax.ppermute(value, "expert", [(i, i ^ bit) for i in range(devices)])

    def groups_on(value, count):
        shift = count * WSPLIT
        return lax.ppermute(value, "expert", [(i, (i + shift) % devices) for i in range(devices)])

    kv = jnp.transpose(enc_kv[0], (1, 0, 2)).reshape(-1, width)
    kv_pieces = [kv]
    for shift in range(1, pipes):
        perm = [(i, (i + shift) % pipes) for i in range(pipes)]
        kv_pieces.append(lax.ppermute(kv, "pipe", perm))
    def along(value):
        perms = [[(i, (i + shift) % pipes) for i in range(pipes)] for shift in range(1, pipes)]
        return [value] + [lax.ppermute(value, "pipe", perm) for perm in perms]

    def paired(parts):
        return [across(value, 1) for value in parts]

    pipe = lax.axis_index("pipe").astype(jnp.int32)
    w_in_pair, w_out_pair = across(w_in, 1), across(w_out, 1)
    pipe = pipe.reshape(1)
    in_part, out_part, out_rest = parts(pipe, w_in, w_out, pipes)
    in_y = across(in_part, 2)

    group = (lax.axis_index("expert") // WSPLIT).astype(jnp.int32).reshape(1)
    staged = stage(
        group,
        state[0, 0],
        query[0, 0],
        gain.reshape(1, width),
        expert_id[0],
        slot[0],
        gate[0],
        groups,
        cap,
    )
    flat, gates = staged[4:]
    hidden, near, *packed = attend(
        *staged[:4], kv_pieces, groups, cap, after=[w_in_pair, w_out_pair]
    )
    far = [groups_on(block, count) for count, block in enumerate(packed, 1)]
    far = jnp.concatenate(far, axis=0) if len(far) > 1 else far[0]

    (in_y,) = after_all([in_y], [near])
    out_part, out_rest = after_all([out_part, out_rest], [in_y])
    out_y = across(out_part, 2)
    rest_y = across(out_rest, 2)
    in_y = after_all(along(in_y), [])
    in_pair = paired(in_y)
    (out_y,) = after_all([out_y], [in_y[-1]])
    out_y = after_all(along(out_y), [])
    out_pair = paired(out_y)
    rests = [rest_y, across(rest_y, 1)]

    near_z = across(near, 4)
    far = [far]
    for step in range(CROSS_STEPS):
        far = after_all(far, [] if step else [near_z], CROSS_WEIGHT)
    (far,) = far
    far_z = [across(far, 4)]
    for _ in range(FAR_STEPS):
        far_z = after_all(far_z, [], FAR_WEIGHT)
    (far_z,) = far_z

    def experts(own, z, after=()):
        acts = up(own, z, [w_in, w_in_pair]), up_y(pipe, own, z, in_y, in_pair, after)
        return down(pipe, acts, [w_out, w_out_pair], out_y, out_pair, rests)

    far_own, far_sent = experts(far, far_z)
    near_own, near_sent = experts(near, near_z, [far_own])
    far_sum, near_sent = total(far_own, across(far_sent, 4), [near_sent])
    backs = [
        groups_on(far_sum[(count - 1) * cap : count * cap], groups - count)
        for count in range(1, groups)
    ]
    backs = after_all(backs, [], BACK_WEIGHT)
    near_sums = [near_own, across(near_sent, 4)]
    output = finish(hidden, gates, flat, near_sums, backs, groups, cap)
    return output.reshape(1, 1, tokens, width)


def solution(mesh):
    return jax.shard_map(
        body,
        mesh=mesh,
        in_specs=(
            P("expert", "pipe", None, None),
            P("expert", "pipe", None, None),
            P("expert", "pipe", None, None),
            P(),
            P(None, "expert"),
            P("expert", None),
            P("expert", "pipe", None),
            P("expert", "pipe", None),
            P("expert", "pipe", None),
        ),
        out_specs=P("expert", "pipe", None, None),
        check_vma=False,
    )
```

```python
import functools
import math

import jax
import jax.numpy as jnp
from jax import lax
from jax.experimental import pallas as pl
from jax.experimental.pallas import tpu as pltpu
from jax.sharding import PartitionSpec as P

HEADS = 16
HD = 128
WSPLIT = 8
EPS = 1e-06
FAR_WEIGHT = 3_000_000_000
FAR_STEPS = 4
CROSS_STEPS = 1
CROSS_WEIGHT = 3_000_000_000
BACK_WEIGHT = 10_000_000_000
VMEM_LIMIT = 32 * 1024 * 1024
PART_LIMIT = 60 * 1024 * 1024

VMEM = pl.BlockSpec(memory_space=pltpu.VMEM)
SMEM = pl.BlockSpec(memory_space=pltpu.SMEM)
ANY = pl.BlockSpec(memory_space=pl.ANY)


def struct(shape, dtype=jnp.bfloat16):
    return jax.ShapeDtypeStruct(shape, dtype)


def call(
    kernel, outs, in_specs, name, flops, moved, scratch=(), out_specs=None, aliases=None, limit=VMEM_LIMIT
):
    return pl.pallas_call(
        kernel,
        out_shape=outs,
        in_specs=in_specs,
        out_specs=out_specs or jax.tree.map(lambda _: VMEM, outs),
        scratch_shapes=list(scratch),
        input_output_aliases=aliases or {},
        compiler_params=pltpu.CompilerParams(vmem_limit_bytes=limit),
        cost_estimate=pl.CostEstimate(flops=flops, bytes_accessed=moved, transcendentals=0),
        name=name,
    )


def as_column(row):
    count = row.shape[1]
    down = lax.broadcasted_iota(jnp.int32, (count, count), 0)
    along = lax.broadcasted_iota(jnp.int32, (count, count), 1)
    return jnp.sum(jnp.where(down == along, row, jnp.zeros_like(row)), axis=1, keepdims=True)


def stage_kernel(groups, cap, *refs):
    group_ref, state_in, query_in, gain_in, expert_ref, slot_ref, gate_ref = refs[:7]
    state_out, query_out, gain_out, flat_row, flat_column, gate_column = refs[7:]
    state_out[...] = state_in[...]
    query_out[...] = query_in[...]
    gain_out[...] = gain_in[...]
    offset = expert_ref[...] - group_ref[0]
    offset = jnp.where(offset < 0, offset + groups, offset)
    slot = slot_ref[...]
    flat = jnp.where(slot >= 0, offset * cap + slot, -1)
    flat_row[...] = flat
    flat_column[...] = as_column(flat)
    gate_column[...] = as_column(gate_ref[...])


def stage(group, state, query, gain, expert_id, slot, gate, groups, cap):
    tokens, width = state.shape
    outs = [
        struct((tokens, width)),
        struct((tokens, width)),
        struct((1, width), jnp.float32),
        struct((1, tokens), jnp.int32),
        struct((tokens, 1), jnp.int32),
        struct((tokens, 1), jnp.float32),
    ]
    return call(
        functools.partial(stage_kernel, groups, cap),
        outs,
        [SMEM] + [VMEM] * 6,
        "stage",
        tokens * tokens,
        8 * tokens * width,
    )(group, state, query, gain, expert_id, slot, gate)


def gate_kernel(*refs):
    pass


def after_all(values, others, weight=1):
    return call(
        gate_kernel,
        [struct(value.shape) for value in values],
        [ANY] * (len(values) + len(others)),
        "hand_on",
        weight,
        1,
        out_specs=[ANY] * len(values),
        aliases={i: i for i in range(len(values))},
    )(*values, *others)


def attend_kernel(pieces, groups, cap, *refs):
    state_ref, query_ref, gain_ref, flat_ref = refs[:4]
    kv_refs = refs[4 : 4 + pieces]
    hidden_ref = refs[-1 - groups]
    packed_refs = refs[-groups:]
    tokens, width = state_ref.shape
    local = kv_refs[0].shape[0] // 2
    scale = 1.0 / math.sqrt(HD)
    squares = jnp.zeros((tokens, HD), jnp.float32)
    for head in range(HEADS):
        cols = slice(head * HD, (head + 1) * HD)
        keys = jnp.concatenate([r[:local, cols] for r in kv_refs], axis=0)
        values = jnp.concatenate([r[local:, cols] for r in kv_refs], axis=0)
        scores = (
            lax.dot_general(
                query_ref[:, cols],
                keys,
                (((1,), (1,)), ((), ())),
                preferred_element_type=jnp.float32,
            )
            * scale
        )
        raised = jnp.exp(scores - jnp.max(scores, axis=1, keepdims=True))
        total = jnp.sum(raised, axis=1, keepdims=True)
        mixed = jnp.dot(raised.astype(jnp.bfloat16), values, preferred_element_type=jnp.float32)
        hidden = state_ref[:, cols].astype(jnp.float32) + mixed / total
        hidden_ref[:, cols] = hidden
        squares = squares + hidden * hidden
    mean_square = jnp.sum(squares, axis=1, keepdims=True) * (1.0 / width)
    inverse = lax.rsqrt(mean_square + EPS)
    rows = lax.broadcasted_iota(jnp.int32, (groups * cap, tokens), 0)
    selector = (rows == flat_ref[...]).astype(jnp.float32).astype(jnp.bfloat16)
    step = 512
    for at in range(0, width, step):
        cols = slice(at, at + step)
        normed = (hidden_ref[:, cols] * inverse * gain_ref[:, cols]).astype(jnp.bfloat16)
        packed = jnp.dot(selector, normed, preferred_element_type=jnp.float32).astype(jnp.bfloat16)
        for group in range(groups):
            packed_refs[group][:, cols] = packed[group * cap : (group + 1) * cap]


def attend(state, query, gain, flat, kv_pieces, groups, cap, after):
    tokens, width = state.shape
    outs = [struct((tokens, width), jnp.float32)] + [struct((cap, width))] * groups
    pieces = len(kv_pieces)
    return call(
        functools.partial(attend_kernel, pieces, groups, cap),
        outs,
        [VMEM] * (4 + pieces) + [ANY] * len(after),
        "attend",
        4 * tokens * pieces * kv_pieces[0].shape[0] * width,
        12 * tokens * width,
    )(state, query, gain, flat, *kv_pieces, *after)


def place(pipes, shift, pipe, size):
    at = pipe - shift
    at = jnp.where(at < 0, at + pipes, at)
    return pl.multiple_of(at * size, size)


def part_kernel(pipe_ref, whole, part, sem):
    size = part.shape[0]
    at = pl.multiple_of(pipe_ref[0] * size, size)
    copy = pltpu.make_async_copy(whole.at[pl.ds(at, size)], part, sem)
    copy.start()
    copy.wait()


def cut_part(pipe, whole, size):
    return call(
        part_kernel,
        struct((size, whole.shape[1])),
        [SMEM, ANY],
        "weight_part",
        1,
        4 * size * whole.shape[1],
        scratch=[pltpu.SemaphoreType.DMA],
        limit=PART_LIMIT,
    )(pipe, whole)


def hold_kernel(pipes, pipe_ref, w_in, w_out, in_held, out_held, out_part, out_rest, sems):
    size = out_part.shape[0]
    at = pl.multiple_of(pipe_ref[0] * size, size)
    copies = [
        pltpu.make_async_copy(source, target, sems.at[i])
        for i, (source, target) in enumerate(
            (
                (w_in, in_held),
                (w_out, out_held),
                (w_out.at[pl.ds(at, size)], out_part),
                (w_out.at[pipes * size :], out_rest),
            )
        )
    ]
    for copy in copies:
        copy.start()
    for copy in copies:
        copy.wait()


def hold(pipe, w_in, w_out, pipes):
    units, width = w_out.shape
    size = units // 2 // pipes // 16 * 16
    return call(
        functools.partial(hold_kernel, pipes),
        [
            struct(w_in.shape),
            struct(w_out.shape),
            struct((size, width)),
            struct((units - pipes * size, width)),
        ],
        [SMEM, ANY, ANY],
        "hold_weights",
        1,
        8 * units * width,
        scratch=[pltpu.SemaphoreType.DMA((4,))],
    )(pipe, w_in, w_out)


def up_kernel(own_in, z_in, w_own, w_pair, out_ref):
    entries = jnp.concatenate([own_in[...], z_in[...]], axis=0)
    weights = jnp.concatenate([w_own[...], w_pair[...]], axis=1)
    raw = jnp.dot(entries, weights, preferred_element_type=jnp.float32)
    out_ref[...] = jnp.maximum(raw, 0.0).astype(jnp.bfloat16)


def up(own, z, w_in):
    rows, width = own.shape
    units = w_in[0].shape[1]
    return call(
        up_kernel,
        struct((2 * rows, 2 * units)),
        [VMEM] * 4,
        "expert_up",
        8 * rows * width * units,
        4 * units * width,
    )(own, z, *w_in)


def up_y_kernel(pipes, *refs):
    pipe = refs[0][0]
    own_in, z_in = refs[1:3]
    y_parts = refs[3 : 3 + pipes]
    pair_parts = refs[3 + pipes : 3 + 2 * pipes]
    out_ref, entries = refs[-2:]
    rows, width = own_in.shape
    entries[:rows] = own_in[...]
    entries[rows:] = z_in[...]
    depth = width // pipes
    raw = jnp.zeros(out_ref.shape, jnp.float32)
    for shift in range(pipes):
        part = entries[:, pl.ds(place(pipes, shift, pipe, depth), depth)]
        weights = jnp.concatenate([y_parts[shift][...], pair_parts[shift][...]], axis=1)
        raw = raw + jnp.dot(part, weights, preferred_element_type=jnp.float32)
    out_ref[...] = jnp.maximum(raw, 0.0).astype(jnp.bfloat16)


def up_y(pipe, own, z, y_parts, pair_parts, after=()):
    rows, width = own.shape
    units = y_parts[0].shape[1]
    pipes = len(y_parts)
    return call(
        functools.partial(up_y_kernel, pipes),
        struct((2 * rows, 2 * units)),
        [SMEM] + [VMEM] * (2 + 2 * pipes) + [ANY] * len(after),
        "expert_up_y",
        8 * rows * width * units,
        4 * units * width,
        scratch=[pltpu.VMEM((2 * rows, width), jnp.bfloat16)],
    )(pipe, own, z, *y_parts, *pair_parts, *after)


def down_kernel(pipes, *refs):
    pipe = refs[0][0]
    act_ref, act_y_ref, w_own, w_pair = refs[1:5]
    y_parts, refs = refs[5 : 5 + pipes], refs[5 + pipes :]
    pair_parts, refs = refs[:pipes], refs[pipes:]
    y_rest, pair_rest = refs[:2]
    own_ref, z_ref, held = refs[-3:]
    rows, width = own_ref.shape
    units = w_own.shape[0]
    size = y_parts[0].shape[0]
    for shift in range(pipes):
        at = place(pipes, shift, pipe, size)
        held[pl.ds(at, size)] = y_parts[shift][...]
        held[pl.ds(pl.multiple_of(units + at, size), size)] = pair_parts[shift][...]
    held[pipes * size : units] = y_rest[...]
    held[units + pipes * size :] = pair_rest[...]
    activation = jnp.concatenate([act_ref[...], act_y_ref[...]], axis=1)
    step = 512
    for at in range(0, width, step):
        cols = slice(at, at + step)
        weights = jnp.concatenate([w_own[:, cols], w_pair[:, cols], held[:, cols]], axis=0)
        part = jnp.dot(activation, weights, preferred_element_type=jnp.float32)
        part = part.astype(jnp.bfloat16)
        own_ref[:, cols] = part[:rows]
        z_ref[:, cols] = part[rows:]


def down(pipe, acts, w_out, y_parts, pair_parts, rests):
    rows = acts[0].shape[0] // 2
    units, width = w_out[0].shape
    pipes = len(y_parts)
    return call(
        functools.partial(down_kernel, pipes),
        [struct((rows, width))] * 2,
        [SMEM] + [VMEM] * (6 + 2 * pipes),
        "expert_down",
        16 * rows * width * units,
        8 * units * width,
        scratch=[pltpu.VMEM((2 * units, width), jnp.bfloat16)],
    )(pipe, *acts, *w_out, *y_parts, *pair_parts, *rests)


def total_kernel(held, own_ref, z_ref, *refs):
    refs[held][...] = (own_ref[...].astype(jnp.float32) + z_ref[...].astype(jnp.float32)).astype(
        jnp.bfloat16
    )


def total(own, z, held):
    outs = [struct(own.shape)] + [struct(value.shape) for value in held]
    return call(
        functools.partial(total_kernel, len(held)),
        outs,
        [VMEM] * 2 + [ANY] * len(held),
        "far_total",
        own.size,
        6 * own.size,
        out_specs=[VMEM] + [ANY] * len(held),
        aliases={2 + i: 1 + i for i in range(len(held))},
    )(own, z, *held)


def finish_kernel(groups, cap, *refs):
    hidden_ref, gate_ref, flat_ref = refs[:3]
    own_ref, z_ref = refs[3:5]
    back_refs = refs[5:-1]
    out_ref = refs[-1]
    tokens, width = hidden_ref.shape
    slots = lax.broadcasted_iota(jnp.int32, (tokens, groups * cap), 1)
    picker = (slots == flat_ref[...]).astype(jnp.float32).astype(jnp.bfloat16)
    step = 512
    for at in range(0, width, step):
        cols = slice(at, at + step)
        near = (own_ref[:, cols].astype(jnp.float32) + z_ref[:, cols].astype(jnp.float32)).astype(
            jnp.bfloat16
        )
        found = jnp.concatenate([near] + [r[:, cols] for r in back_refs], axis=0)
        picked = jnp.dot(picker, found, preferred_element_type=jnp.float32)
        out_ref[:, cols] = (hidden_ref[:, cols] + gate_ref[...] * picked).astype(jnp.bfloat16)


def finish(hidden, gate, flat, sums, backs, groups, cap):
    tokens, width = hidden.shape
    operands = [hidden, gate, flat, *sums, *backs]
    return call(
        functools.partial(finish_kernel, groups, cap),
        struct((tokens, width)),
        [VMEM] * len(operands),
        "finish",
        4 * tokens * cap * groups * width,
        16 * tokens * width,
    )(*operands)


def body(state, query, enc_kv, gain, w_in, w_out, expert_id, slot, gate):
    tokens, width = state.shape[2:]
    devices = lax.axis_size("expert")
    pipes = lax.axis_size("pipe")
    groups = devices // WSPLIT
    cap = 3 * tokens // (2 * groups)

    def across(value, bit):
        return lax.ppermute(value, "expert", [(i, i ^ bit) for i in range(devices)])

    def groups_on(value, count):
        shift = count * WSPLIT
        return lax.ppermute(value, "expert", [(i, (i + shift) % devices) for i in range(devices)])

    kv = jnp.transpose(enc_kv[0], (1, 0, 2)).reshape(-1, width)
    kv_pieces = [kv]
    for shift in range(1, pipes):
        perm = [(i, (i + shift) % pipes) for i in range(pipes)]
        kv_pieces.append(lax.ppermute(kv, "pipe", perm))
    def along(value):
        perms = [[(i, (i + shift) % pipes) for i in range(pipes)] for shift in range(1, pipes)]
        return [value] + [lax.ppermute(value, "pipe", perm) for perm in perms]

    def paired(parts):
        return [across(value, 1) for value in parts]

    pipe = lax.axis_index("pipe").astype(jnp.int32)
    w_in_pair, w_out_pair = across(w_in, 1), across(w_out, 1)
    pipe = pipe.reshape(1)
    in_part = cut_part(pipe, w_in, width // pipes)
    w_in_held, w_out_held, out_part, out_rest = hold(pipe, w_in, w_out, pipes)
    in_y = across(in_part, 2)

    group = (lax.axis_index("expert") // WSPLIT).astype(jnp.int32).reshape(1)
    staged = stage(
        group,
        state[0, 0],
        query[0, 0],
        gain.reshape(1, width),
        expert_id[0],
        slot[0],
        gate[0],
        groups,
        cap,
    )
    flat, gates = staged[4:]
    hidden, near, *packed = attend(
        *staged[:4], kv_pieces, groups, cap, after=[w_in_pair, w_out_pair, w_out_held]
    )
    far = [groups_on(block, count) for count, block in enumerate(packed, 1)]
    far = jnp.concatenate(far, axis=0) if len(far) > 1 else far[0]

    (in_y,) = after_all([in_y], [near])
    out_part, out_rest = after_all([out_part, out_rest], [in_y])
    out_y = across(out_part, 2)
    rest_y = across(out_rest, 2)
    in_y = after_all(along(in_y), [])
    in_pair = paired(in_y)

    near_z = across(near, 4)
    far = [far]
    for step in range(CROSS_STEPS):
        far = after_all(far, [] if step else [near_z], CROSS_WEIGHT)
    (far,) = far
    far_z = [across(far, 4)]
    for _ in range(FAR_STEPS):
        far_z = after_all(far_z, [], FAR_WEIGHT)
    (far_z,) = far_z

    def experts_up(own, z, after=()):
        own_act = up(own, z, [w_in_held, w_in_pair])
        return own_act, up_y(pipe, own, z, in_y, in_pair, after)

    far_acts = experts_up(far, far_z)
    (out_y,) = after_all([out_y], [in_y[-1]])
    out_y = after_all(along(out_y), [*far_acts])
    out_pair = paired(out_y)
    rests = [rest_y, across(rest_y, 1)]

    def experts_down(acts):
        return down(pipe, acts, [w_out_held, w_out_pair], out_y, out_pair, rests)

    far_own, far_sent = experts_down(far_acts)
    near_own, near_sent = experts_down(experts_up(near, near_z, [far_own]))
    far_sum, near_sent = total(far_own, across(far_sent, 4), [near_sent])
    backs = [
        groups_on(far_sum[(count - 1) * cap : count * cap], groups - count)
        for count in range(1, groups)
    ]
    backs = after_all(backs, [], BACK_WEIGHT)
    near_sums = [near_own, across(near_sent, 4)]
    output = finish(hidden, gates, flat, near_sums, backs, groups, cap)
    return output.reshape(1, 1, tokens, width)


def solution(mesh):
    return jax.shard_map(
        body,
        mesh=mesh,
        in_specs=(
            P("expert", "pipe", None, None),
            P("expert", "pipe", None, None),
            P("expert", "pipe", None, None),
            P(),
            P(None, "expert"),
            P("expert", None),
            P("expert", "pipe", None),
            P("expert", "pipe", None),
            P("expert", "pipe", None),
        ),
        out_specs=P("expert", "pipe", None, None),
        check_vma=False,
    )
```

```python
import functools
import math

import jax
import jax.numpy as jnp
from jax import lax
from jax.experimental import pallas as pl
from jax.experimental.pallas import tpu as pltpu
from jax.sharding import PartitionSpec as P

HEADS = 16
HD = 128
WSPLIT = 8
EPS = 1e-06
FAR_WEIGHT = 3_000_000_000
FAR_STEPS = 4
CROSS_STEPS = 1
CROSS_WEIGHT = 3_000_000_000
BACK_WEIGHT = 10_000_000_000
VMEM_LIMIT = 32 * 1024 * 1024
PART_LIMIT = 60 * 1024 * 1024

VMEM = pl.BlockSpec(memory_space=pltpu.VMEM)
SMEM = pl.BlockSpec(memory_space=pltpu.SMEM)
ANY = pl.BlockSpec(memory_space=pl.ANY)


def struct(shape, dtype=jnp.bfloat16):
    return jax.ShapeDtypeStruct(shape, dtype)


def call(
    kernel, outs, in_specs, name, flops, moved, scratch=(), out_specs=None, aliases=None, limit=VMEM_LIMIT
):
    return pl.pallas_call(
        kernel,
        out_shape=outs,
        in_specs=in_specs,
        out_specs=out_specs or jax.tree.map(lambda _: VMEM, outs),
        scratch_shapes=list(scratch),
        input_output_aliases=aliases or {},
        compiler_params=pltpu.CompilerParams(vmem_limit_bytes=limit),
        cost_estimate=pl.CostEstimate(flops=flops, bytes_accessed=moved, transcendentals=0),
        name=name,
    )


def as_column(row):
    count = row.shape[1]
    down = lax.broadcasted_iota(jnp.int32, (count, count), 0)
    along = lax.broadcasted_iota(jnp.int32, (count, count), 1)
    return jnp.sum(jnp.where(down == along, row, jnp.zeros_like(row)), axis=1, keepdims=True)


def stage_kernel(groups, cap, *refs):
    group_ref, state_in, query_in, gain_in, expert_ref, slot_ref, gate_ref = refs[:7]
    state_out, query_out, gain_out, flat_row, flat_column, gate_column = refs[7:]
    state_out[...] = state_in[...]
    query_out[...] = query_in[...]
    gain_out[...] = gain_in[...]
    offset = expert_ref[...] - group_ref[0]
    offset = jnp.where(offset < 0, offset + groups, offset)
    slot = slot_ref[...]
    flat = jnp.where(slot >= 0, offset * cap + slot, -1)
    flat_row[...] = flat
    flat_column[...] = as_column(flat)
    gate_column[...] = as_column(gate_ref[...])


def stage(group, state, query, gain, expert_id, slot, gate, groups, cap):
    tokens, width = state.shape
    outs = [
        struct((tokens, width)),
        struct((tokens, width)),
        struct((1, width), jnp.float32),
        struct((1, tokens), jnp.int32),
        struct((tokens, 1), jnp.int32),
        struct((tokens, 1), jnp.float32),
    ]
    return call(
        functools.partial(stage_kernel, groups, cap),
        outs,
        [SMEM] + [VMEM] * 6,
        "stage",
        tokens * tokens,
        8 * tokens * width,
    )(group, state, query, gain, expert_id, slot, gate)


def gate_kernel(*refs):
    pass


def after_all(values, others, weight=1):
    return call(
        gate_kernel,
        [struct(value.shape) for value in values],
        [ANY] * (len(values) + len(others)),
        "hand_on",
        weight,
        1,
        out_specs=[ANY] * len(values),
        aliases={i: i for i in range(len(values))},
    )(*values, *others)


def attend_kernel(pieces, groups, cap, *refs):
    state_ref, query_ref, gain_ref, flat_ref = refs[:4]
    kv_refs = refs[4 : 4 + pieces]
    hidden_ref = refs[-1 - groups]
    packed_refs = refs[-groups:]
    tokens, width = state_ref.shape
    local = kv_refs[0].shape[0] // 2
    scale = 1.0 / math.sqrt(HD)
    def one_head(head, squares):
        cols = pl.ds(pl.multiple_of(head * HD, HD), HD)
        keys = jnp.concatenate([r[:local, cols] for r in kv_refs], axis=0)
        values = jnp.concatenate([r[local:, cols] for r in kv_refs], axis=0)
        scores = (
            lax.dot_general(
                query_ref[:, cols],
                keys,
                (((1,), (1,)), ((), ())),
                preferred_element_type=jnp.float32,
            )
            * scale
        )
        raised = jnp.exp(scores - jnp.max(scores, axis=1, keepdims=True))
        total = jnp.sum(raised, axis=1, keepdims=True)
        mixed = jnp.dot(raised.astype(jnp.bfloat16), values, preferred_element_type=jnp.float32)
        hidden = state_ref[:, cols].astype(jnp.float32) + mixed / total
        hidden_ref[:, cols] = hidden
        return squares + hidden * hidden

    squares = lax.fori_loop(
        0, HEADS, one_head, jnp.zeros((tokens, HD), jnp.float32), unroll=HEADS // 4
    )
    mean_square = jnp.sum(squares, axis=1, keepdims=True) * (1.0 / width)
    inverse = lax.rsqrt(mean_square + EPS)
    rows = lax.broadcasted_iota(jnp.int32, (groups * cap, tokens), 0)
    selector = (rows == flat_ref[...]).astype(jnp.float32).astype(jnp.bfloat16)
    step = 512
    for at in range(0, width, step):
        cols = slice(at, at + step)
        normed = (hidden_ref[:, cols] * inverse * gain_ref[:, cols]).astype(jnp.bfloat16)
        packed = jnp.dot(selector, normed, preferred_element_type=jnp.float32).astype(jnp.bfloat16)
        for group in range(groups):
            packed_refs[group][:, cols] = packed[group * cap : (group + 1) * cap]


def attend(state, query, gain, flat, kv_pieces, groups, cap, after):
    tokens, width = state.shape
    outs = [struct((tokens, width), jnp.float32)] + [struct((cap, width))] * groups
    pieces = len(kv_pieces)
    return call(
        functools.partial(attend_kernel, pieces, groups, cap),
        outs,
        [VMEM] * (4 + pieces) + [ANY] * len(after),
        "attend",
        4 * tokens * pieces * kv_pieces[0].shape[0] * width,
        12 * tokens * width,
    )(state, query, gain, flat, *kv_pieces, *after)


def place(pipes, shift, pipe, size):
    at = pipe - shift
    at = jnp.where(at < 0, at + pipes, at)
    return pl.multiple_of(at * size, size)


def part_kernel(pipe_ref, whole, part, sem):
    size = part.shape[0]
    at = pl.multiple_of(pipe_ref[0] * size, size)
    copy = pltpu.make_async_copy(whole.at[pl.ds(at, size)], part, sem)
    copy.start()
    copy.wait()


def cut_part(pipe, whole, size):
    return call(
        part_kernel,
        struct((size, whole.shape[1])),
        [SMEM, ANY],
        "weight_part",
        1,
        4 * size * whole.shape[1],
        scratch=[pltpu.SemaphoreType.DMA],
        out_specs=ANY,
        limit=PART_LIMIT,
    )(pipe, whole)


def hold_kernel(pipes, pipe_ref, w_in, w_out, *refs):
    in_held, out_held, out_part, out_rest, sems = refs[-5:]
    size = out_part.shape[0]
    at = pl.multiple_of(pipe_ref[0] * size, size)
    copies = [
        pltpu.make_async_copy(source, target, sems.at[i])
        for i, (source, target) in enumerate(
            (
                (w_in, in_held),
                (w_out, out_held),
                (w_out.at[pl.ds(at, size)], out_part),
                (w_out.at[pipes * size :], out_rest),
            )
        )
    ]
    for copy in copies:
        copy.start()
    for copy in copies:
        copy.wait()


def hold(pipe, w_in, w_out, pipes, after):
    units, width = w_out.shape
    size = units // 2 // pipes // 16 * 16
    return call(
        functools.partial(hold_kernel, pipes),
        [
            struct(w_in.shape),
            struct(w_out.shape),
            struct((size, width)),
            struct((units - pipes * size, width)),
        ],
        [SMEM, ANY, ANY] + [ANY] * len(after),
        "hold_weights",
        1,
        8 * units * width,
        scratch=[pltpu.SemaphoreType.DMA((4,))],
    )(pipe, w_in, w_out, *after)


def up_kernel(own_in, z_in, w_own, w_pair, out_ref):
    entries = jnp.concatenate([own_in[...], z_in[...]], axis=0)
    weights = jnp.concatenate([w_own[...], w_pair[...]], axis=1)
    raw = jnp.dot(entries, weights, preferred_element_type=jnp.float32)
    out_ref[...] = jnp.maximum(raw, 0.0).astype(jnp.bfloat16)


def up(own, z, w_in):
    rows, width = own.shape
    units = w_in[0].shape[1]
    return call(
        up_kernel,
        struct((2 * rows, 2 * units)),
        [VMEM] * 4,
        "expert_up",
        8 * rows * width * units,
        4 * units * width,
    )(own, z, *w_in)


def up_y_kernel(pipes, *refs):
    pipe = refs[0][0]
    own_in, z_in = refs[1:3]
    y_parts = refs[3 : 3 + pipes]
    pair_parts = refs[3 + pipes : 3 + 2 * pipes]
    out_ref, entries = refs[-2:]
    rows, width = own_in.shape
    entries[:rows] = own_in[...]
    entries[rows:] = z_in[...]
    depth = width // pipes
    raw = jnp.zeros(out_ref.shape, jnp.float32)
    for shift in range(pipes):
        part = entries[:, pl.ds(place(pipes, shift, pipe, depth), depth)]
        weights = jnp.concatenate([y_parts[shift][...], pair_parts[shift][...]], axis=1)
        raw = raw + jnp.dot(part, weights, preferred_element_type=jnp.float32)
    out_ref[...] = jnp.maximum(raw, 0.0).astype(jnp.bfloat16)


def up_y(pipe, own, z, y_parts, pair_parts, after=()):
    rows, width = own.shape
    units = y_parts[0].shape[1]
    pipes = len(y_parts)
    return call(
        functools.partial(up_y_kernel, pipes),
        struct((2 * rows, 2 * units)),
        [SMEM] + [VMEM] * (2 + 2 * pipes) + [ANY] * len(after),
        "expert_up_y",
        8 * rows * width * units,
        4 * units * width,
        scratch=[pltpu.VMEM((2 * rows, width), jnp.bfloat16)],
    )(pipe, own, z, *y_parts, *pair_parts, *after)


def down_kernel(pipes, *refs):
    pipe = refs[0][0]
    act_ref, act_y_ref, w_own, w_pair = refs[1:5]
    y_parts, refs = refs[5 : 5 + pipes], refs[5 + pipes :]
    pair_parts, refs = refs[:pipes], refs[pipes:]
    y_rest, pair_rest = refs[:2]
    own_ref, z_ref, held = refs[-3:]
    rows, width = own_ref.shape
    units = w_own.shape[0]
    size = y_parts[0].shape[0]
    for shift in range(pipes):
        at = place(pipes, shift, pipe, size)
        held[pl.ds(at, size)] = y_parts[shift][...]
        held[pl.ds(pl.multiple_of(units + at, size), size)] = pair_parts[shift][...]
    held[pipes * size : units] = y_rest[...]
    held[units + pipes * size :] = pair_rest[...]
    activation = jnp.concatenate([act_ref[...], act_y_ref[...]], axis=1)
    step = 512

    def block(i, carry):
        cols = pl.ds(pl.multiple_of(i * step, step), step)
        weights = jnp.concatenate([w_own[:, cols], w_pair[:, cols], held[:, cols]], axis=0)
        part = jnp.dot(activation, weights, preferred_element_type=jnp.float32)
        part = part.astype(jnp.bfloat16)
        own_ref[:, cols] = part[:rows]
        z_ref[:, cols] = part[rows:]
        return carry

    lax.fori_loop(0, width // step, block, 0)


def down(pipe, acts, w_out, y_parts, pair_parts, rests):
    rows = acts[0].shape[0] // 2
    units, width = w_out[0].shape
    pipes = len(y_parts)
    return call(
        functools.partial(down_kernel, pipes),
        [struct((rows, width))] * 2,
        [SMEM] + [VMEM] * (6 + 2 * pipes),
        "expert_down",
        16 * rows * width * units,
        8 * units * width,
        scratch=[pltpu.VMEM((2 * units, width), jnp.bfloat16)],
    )(pipe, *acts, *w_out, *y_parts, *pair_parts, *rests)


def total_kernel(held, own_ref, z_ref, *refs):
    refs[held][...] = (own_ref[...].astype(jnp.float32) + z_ref[...].astype(jnp.float32)).astype(
        jnp.bfloat16
    )


def total(own, z, held):
    outs = [struct(own.shape)] + [struct(value.shape) for value in held]
    return call(
        functools.partial(total_kernel, len(held)),
        outs,
        [VMEM] * 2 + [ANY] * len(held),
        "far_total",
        own.size,
        6 * own.size,
        out_specs=[VMEM] + [ANY] * len(held),
        aliases={2 + i: 1 + i for i in range(len(held))},
    )(own, z, *held)


def finish_kernel(groups, cap, *refs):
    hidden_ref, gate_ref, flat_ref = refs[:3]
    own_ref, z_ref = refs[3:5]
    back_refs = refs[5:-1]
    out_ref = refs[-1]
    tokens, width = hidden_ref.shape
    slots = lax.broadcasted_iota(jnp.int32, (tokens, groups * cap), 1)
    picker = (slots == flat_ref[...]).astype(jnp.float32).astype(jnp.bfloat16)
    step = 512
    for at in range(0, width, step):
        cols = slice(at, at + step)
        near = (own_ref[:, cols].astype(jnp.float32) + z_ref[:, cols].astype(jnp.float32)).astype(
            jnp.bfloat16
        )
        found = jnp.concatenate([near] + [r[:, cols] for r in back_refs], axis=0)
        picked = jnp.dot(picker, found, preferred_element_type=jnp.float32)
        out_ref[:, cols] = (hidden_ref[:, cols] + gate_ref[...] * picked).astype(jnp.bfloat16)


def finish(hidden, gate, flat, sums, backs, groups, cap):
    tokens, width = hidden.shape
    operands = [hidden, gate, flat, *sums, *backs]
    return call(
        functools.partial(finish_kernel, groups, cap),
        struct((tokens, width)),
        [VMEM] * len(operands),
        "finish",
        4 * tokens * cap * groups * width,
        16 * tokens * width,
    )(*operands)


def body(state, query, enc_kv, gain, w_in, w_out, expert_id, slot, gate):
    tokens, width = state.shape[2:]
    devices = lax.axis_size("expert")
    pipes = lax.axis_size("pipe")
    groups = devices // WSPLIT
    cap = 3 * tokens // (2 * groups)

    def across(value, bit):
        return lax.ppermute(value, "expert", [(i, i ^ bit) for i in range(devices)])

    def groups_on(value, count):
        shift = count * WSPLIT
        return lax.ppermute(value, "expert", [(i, (i + shift) % devices) for i in range(devices)])

    kv = jnp.transpose(enc_kv[0], (1, 0, 2)).reshape(-1, width)
    kv_pieces = [kv]
    for shift in range(1, pipes):
        perm = [(i, (i + shift) % pipes) for i in range(pipes)]
        kv_pieces.append(lax.ppermute(kv, "pipe", perm))
    def along(value):
        perms = [[(i, (i + shift) % pipes) for i in range(pipes)] for shift in range(1, pipes)]
        return [value] + [lax.ppermute(value, "pipe", perm) for perm in perms]

    def paired(parts):
        return [across(value, 1) for value in parts]

    pipe = lax.axis_index("pipe").astype(jnp.int32)
    w_in_pair, w_out_pair = across(w_in, 1), across(w_out, 1)
    pipe = pipe.reshape(1)
    in_part = cut_part(pipe, w_in, width // pipes)
    in_y = across(in_part, 2)

    group = (lax.axis_index("expert") // WSPLIT).astype(jnp.int32).reshape(1)
    staged = stage(
        group,
        state[0, 0],
        query[0, 0],
        gain.reshape(1, width),
        expert_id[0],
        slot[0],
        gate[0],
        groups,
        cap,
    )
    flat, gates = staged[4:]
    hidden, near, *packed = attend(
        *staged[:4], kv_pieces, groups, cap, after=[w_in_pair, w_out_pair]
    )
    far = [groups_on(block, count) for count, block in enumerate(packed, 1)]
    far = jnp.concatenate(far, axis=0) if len(far) > 1 else far[0]

    w_in_held, w_out_held, out_part, out_rest = hold(pipe, w_in, w_out, pipes, [near])
    (in_y,) = after_all([in_y], [out_part])
    out_part, out_rest = after_all([out_part, out_rest], [in_y])
    out_y = across(out_part, 2)
    rest_y = across(out_rest, 2)
    in_y = after_all(along(in_y), [])
    in_pair = paired(in_y)

    near_z = across(near, 4)
    far = [far]
    for step in range(CROSS_STEPS):
        far = after_all(far, [] if step else [near_z], CROSS_WEIGHT)
    (far,) = far
    far_z = [across(far, 4)]
    for _ in range(FAR_STEPS):
        far_z = after_all(far_z, [], FAR_WEIGHT)
    (far_z,) = far_z

    def experts_up(own, z, after=()):
        own_act = up(own, z, [w_in_held, w_in_pair])
        return own_act, up_y(pipe, own, z, in_y, in_pair, after)

    far_acts = experts_up(far, far_z)
    (out_y,) = after_all([out_y], [in_y[-1]])
    out_y = after_all(along(out_y), [*far_acts])
    out_pair = paired(out_y)
    rests = [rest_y, across(rest_y, 1)]

    def experts_down(acts):
        return down(pipe, acts, [w_out_held, w_out_pair], out_y, out_pair, rests)

    far_own, far_sent = experts_down(far_acts)
    near_own, near_sent = experts_down(experts_up(near, near_z, [far_own]))
    far_sum, near_sent = total(far_own, across(far_sent, 4), [near_sent])
    backs = [
        groups_on(far_sum[(count - 1) * cap : count * cap], groups - count)
        for count in range(1, groups)
    ]
    backs = after_all(backs, [], BACK_WEIGHT)
    near_sums = [near_own, across(near_sent, 4)]
    output = finish(hidden, gates, flat, near_sums, backs, groups, cap)
    return output.reshape(1, 1, tokens, width)


def solution(mesh):
    return jax.shard_map(
        body,
        mesh=mesh,
        in_specs=(
            P("expert", "pipe", None, None),
            P("expert", "pipe", None, None),
            P("expert", "pipe", None, None),
            P(),
            P(None, "expert"),
            P("expert", None),
            P("expert", "pipe", None),
            P("expert", "pipe", None),
            P("expert", "pipe", None),
        ),
        out_specs=P("expert", "pipe", None, None),
        check_vma=False,
    )
```

```python
import functools
import math

import jax
import jax.numpy as jnp
from jax import lax
from jax.experimental import pallas as pl
from jax.experimental.pallas import tpu as pltpu
from jax.sharding import PartitionSpec as P

HEADS = 16
HD = 128
WSPLIT = 8
EPS = 1e-06
FAR_WEIGHT = 3_000_000_000
FAR_STEPS = 4
CROSS_STEPS = 1
CROSS_WEIGHT = 3_000_000_000
BACK_WEIGHT = 10_000_000_000
VMEM_LIMIT = 32 * 1024 * 1024
PART_LIMIT = 60 * 1024 * 1024

VMEM = pl.BlockSpec(memory_space=pltpu.VMEM)
SMEM = pl.BlockSpec(memory_space=pltpu.SMEM)
ANY = pl.BlockSpec(memory_space=pl.ANY)


def struct(shape, dtype=jnp.bfloat16):
    return jax.ShapeDtypeStruct(shape, dtype)


def call(
    kernel, outs, in_specs, name, flops, moved, scratch=(), out_specs=None, aliases=None, limit=VMEM_LIMIT
):
    return pl.pallas_call(
        kernel,
        out_shape=outs,
        in_specs=in_specs,
        out_specs=out_specs or jax.tree.map(lambda _: VMEM, outs),
        scratch_shapes=list(scratch),
        input_output_aliases=aliases or {},
        compiler_params=pltpu.CompilerParams(vmem_limit_bytes=limit),
        cost_estimate=pl.CostEstimate(flops=flops, bytes_accessed=moved, transcendentals=0),
        name=name,
    )


def as_column(row):
    count = row.shape[1]
    down = lax.broadcasted_iota(jnp.int32, (count, count), 0)
    along = lax.broadcasted_iota(jnp.int32, (count, count), 1)
    return jnp.sum(jnp.where(down == along, row, jnp.zeros_like(row)), axis=1, keepdims=True)


def stage_kernel(groups, cap, *refs):
    group_ref, state_in, query_in, gain_in, expert_ref, slot_ref, gate_ref = refs[:7]
    state_out, query_out, gain_out, flat_row, flat_column, gate_column = refs[7:]
    state_out[...] = state_in[...]
    query_out[...] = query_in[...]
    gain_out[...] = gain_in[...]
    offset = expert_ref[...] - group_ref[0]
    offset = jnp.where(offset < 0, offset + groups, offset)
    slot = slot_ref[...]
    flat = jnp.where(slot >= 0, offset * cap + slot, -1)
    flat_row[...] = flat
    flat_column[...] = as_column(flat)
    gate_column[...] = as_column(gate_ref[...])


def stage(group, state, query, gain, expert_id, slot, gate, groups, cap):
    tokens, width = state.shape
    outs = [
        struct((tokens, width)),
        struct((tokens, width)),
        struct((1, width), jnp.float32),
        struct((1, tokens), jnp.int32),
        struct((tokens, 1), jnp.int32),
        struct((tokens, 1), jnp.float32),
    ]
    return call(
        functools.partial(stage_kernel, groups, cap),
        outs,
        [SMEM] + [VMEM] * 6,
        "stage",
        tokens * tokens,
        8 * tokens * width,
    )(group, state, query, gain, expert_id, slot, gate)


def gate_kernel(*refs):
    pass


def after_all(values, others, weight=1):
    return call(
        gate_kernel,
        [struct(value.shape) for value in values],
        [ANY] * (len(values) + len(others)),
        "hand_on",
        weight,
        1,
        out_specs=[ANY] * len(values),
        aliases={i: i for i in range(len(values))},
    )(*values, *others)


def attend_kernel(pieces, groups, cap, *refs):
    state_ref, query_ref, gain_ref, flat_ref = refs[:4]
    kv_refs = refs[4 : 4 + pieces]
    hidden_ref = refs[-1 - groups]
    packed_refs = refs[-groups:]
    tokens, width = state_ref.shape
    local = kv_refs[0].shape[0] // 2
    scale = 1.0 / math.sqrt(HD)
    squares = jnp.zeros((tokens, HD), jnp.float32)
    for head in range(HEADS):
        cols = slice(head * HD, (head + 1) * HD)
        keys = jnp.concatenate([r[:local, cols] for r in kv_refs], axis=0)
        values = jnp.concatenate([r[local:, cols] for r in kv_refs], axis=0)
        scores = (
            lax.dot_general(
                query_ref[:, cols],
                keys,
                (((1,), (1,)), ((), ())),
                preferred_element_type=jnp.float32,
            )
            * scale
        )
        raised = jnp.exp(scores - jnp.max(scores, axis=1, keepdims=True))
        total = jnp.sum(raised, axis=1, keepdims=True)
        mixed = jnp.dot(raised.astype(jnp.bfloat16), values, preferred_element_type=jnp.float32)
        hidden = state_ref[:, cols].astype(jnp.float32) + mixed / total
        hidden_ref[:, cols] = hidden
        squares = squares + hidden * hidden
    mean_square = jnp.sum(squares, axis=1, keepdims=True) * (1.0 / width)
    inverse = lax.rsqrt(mean_square + EPS)
    rows = lax.broadcasted_iota(jnp.int32, (groups * cap, tokens), 0)
    selector = (rows == flat_ref[...]).astype(jnp.float32).astype(jnp.bfloat16)
    step = 512
    for at in range(0, width, step):
        cols = slice(at, at + step)
        normed = (hidden_ref[:, cols] * inverse * gain_ref[:, cols]).astype(jnp.bfloat16)
        packed = jnp.dot(selector, normed, preferred_element_type=jnp.float32).astype(jnp.bfloat16)
        for group in range(groups):
            packed_refs[group][:, cols] = packed[group * cap : (group + 1) * cap]


def attend(state, query, gain, flat, kv_pieces, groups, cap, after):
    tokens, width = state.shape
    outs = [struct((tokens, width), jnp.float32)] + [struct((cap, width))] * groups
    pieces = len(kv_pieces)
    return call(
        functools.partial(attend_kernel, pieces, groups, cap),
        outs,
        [VMEM] * (4 + pieces) + [ANY] * len(after),
        "attend",
        4 * tokens * pieces * kv_pieces[0].shape[0] * width,
        12 * tokens * width,
    )(state, query, gain, flat, *kv_pieces, *after)


def place(pipes, shift, pipe, size):
    at = pipe - shift
    at = jnp.where(at < 0, at + pipes, at)
    return pl.multiple_of(at * size, size)


def part_kernel(stride, first, pipe_ref, whole, part, sem):
    size = part.shape[0]
    at = pl.multiple_of(pipe_ref[0] * stride + first, size)
    copy = pltpu.make_async_copy(whole.at[pl.ds(at, size)], part, sem)
    copy.start()
    copy.wait()


def cut_part(pipe, whole, stride, first, size):
    return call(
        functools.partial(part_kernel, stride, first),
        struct((size, whole.shape[1])),
        [SMEM, ANY],
        "weight_part",
        1,
        4 * size * whole.shape[1],
        scratch=[pltpu.SemaphoreType.DMA],
        limit=PART_LIMIT,
    )(pipe, whole)


def hold_kernel(pipes, pipe_ref, w_in, w_out, *refs):
    in_held, out_held, out_part, out_rest, sems = refs[-5:]
    size = out_part.shape[0]
    at = pl.multiple_of(pipe_ref[0] * size, size)
    copies = [
        pltpu.make_async_copy(source, target, sems.at[i])
        for i, (source, target) in enumerate(
            (
                (w_in, in_held),
                (w_out, out_held),
                (w_out.at[pl.ds(at, size)], out_part),
                (w_out.at[pipes * size :], out_rest),
            )
        )
    ]
    for copy in copies:
        copy.start()
    for copy in copies:
        copy.wait()


def hold(pipe, w_in, w_out, pipes, after):
    units, width = w_out.shape
    size = units * 7 // 12 // pipes // 16 * 16
    return call(
        functools.partial(hold_kernel, pipes),
        [
            struct(w_in.shape),
            struct(w_out.shape),
            struct((size, width)),
            struct((units - pipes * size, width)),
        ],
        [SMEM, ANY, ANY] + [ANY] * len(after),
        "hold_weights",
        1,
        8 * units * width,
        scratch=[pltpu.SemaphoreType.DMA((4,))],
    )(pipe, w_in, w_out, *after)


def up_kernel(own_in, z_in, w_own, w_pair, out_ref):
    entries = jnp.concatenate([own_in[...], z_in[...]], axis=0)
    weights = jnp.concatenate([w_own[...], w_pair[...]], axis=1)
    raw = jnp.dot(entries, weights, preferred_element_type=jnp.float32)
    out_ref[...] = jnp.maximum(raw, 0.0).astype(jnp.bfloat16)


def up(own, z, w_in):
    rows, width = own.shape
    units = w_in[0].shape[1]
    return call(
        up_kernel,
        struct((2 * rows, 2 * units)),
        [VMEM] * 4,
        "expert_up",
        8 * rows * width * units,
        4 * units * width,
    )(own, z, *w_in)


def up_y_kernel(pipes, halves, *refs):
    pipe = refs[0][0]
    act_ref, own_in, z_in = refs[1:4]
    count = pipes * halves
    y_parts = refs[4 : 4 + count]
    pair_parts = refs[4 + count : 4 + 2 * count]
    out_ref, entries = refs[-2:]
    rows, width = own_in.shape
    units = act_ref.shape[1]
    entries[:rows] = own_in[...]
    entries[rows:] = z_in[...]
    out_ref[:, :units] = act_ref[...]
    depth = width // count
    raw = jnp.zeros(act_ref.shape, jnp.float32)
    for i in range(count):
        half, shift = divmod(i, pipes)
        at = place(pipes, shift, pipe, halves * depth) + half * depth
        part = entries[:, pl.ds(pl.multiple_of(at, depth), depth)]
        weights = jnp.concatenate([y_parts[i][...], pair_parts[i][...]], axis=1)
        raw = raw + jnp.dot(part, weights, preferred_element_type=jnp.float32)
    out_ref[:, units:] = jnp.maximum(raw, 0.0).astype(jnp.bfloat16)


def up_y(pipe, act, own, z, y_parts, pair_parts, pipes, after=()):
    rows, width = own.shape
    units = y_parts[0].shape[1]
    count = len(y_parts)
    return call(
        functools.partial(up_y_kernel, pipes, count // pipes),
        struct((2 * rows, 4 * units)),
        [SMEM] + [VMEM] * (3 + 2 * count) + [ANY] * len(after),
        "expert_up_y",
        8 * rows * width * units,
        4 * units * width,
        scratch=[pltpu.VMEM((2 * rows, width), jnp.bfloat16)],
    )(pipe, act, own, z, *y_parts, *pair_parts, *after)


def down_kernel(pipes, *refs):
    pipe = refs[0][0]
    act_ref, w_own, w_pair = refs[1:4]
    y_parts, refs = refs[4 : 4 + pipes], refs[4 + pipes :]
    pair_parts, refs = refs[:pipes], refs[pipes:]
    y_rest, pair_rest = refs[:2]
    own_ref, z_ref, held = refs[-3:]
    rows, width = own_ref.shape
    units = w_own.shape[0]
    size = y_parts[0].shape[0]
    for shift in range(pipes):
        at = place(pipes, shift, pipe, size)
        held[pl.ds(at, size)] = y_parts[shift][...]
        held[pl.ds(pl.multiple_of(units + at, size), size)] = pair_parts[shift][...]
    held[pipes * size : units] = y_rest[...]
    held[units + pipes * size :] = pair_rest[...]
    step = 512
    for at in range(0, width, step):
        cols = slice(at, at + step)
        weights = jnp.concatenate([w_own[:, cols], w_pair[:, cols], held[:, cols]], axis=0)
        part = jnp.dot(act_ref[...], weights, preferred_element_type=jnp.float32)
        part = part.astype(jnp.bfloat16)
        own_ref[:, cols] = part[:rows]
        z_ref[:, cols] = part[rows:]


def down(pipe, act, w_out, y_parts, pair_parts, rests, after=()):
    rows = act.shape[0] // 2
    units, width = w_out[0].shape
    pipes = len(y_parts)
    return call(
        functools.partial(down_kernel, pipes),
        [struct((rows, width))] * 2,
        [SMEM] + [VMEM] * (5 + 2 * pipes) + [ANY] * len(after),
        "expert_down",
        16 * rows * width * units,
        8 * units * width,
        scratch=[pltpu.VMEM((2 * units, width), jnp.bfloat16)],
    )(pipe, act, *w_out, *y_parts, *pair_parts, *rests, *after)


def total_kernel(held, own_ref, z_ref, *refs):
    refs[held][...] = (own_ref[...].astype(jnp.float32) + z_ref[...].astype(jnp.float32)).astype(
        jnp.bfloat16
    )


def total(own, z, held):
    outs = [struct(own.shape)] + [struct(value.shape) for value in held]
    return call(
        functools.partial(total_kernel, len(held)),
        outs,
        [VMEM] * 2 + [ANY] * len(held),
        "far_total",
        own.size,
        6 * own.size,
        out_specs=[VMEM] + [ANY] * len(held),
        aliases={2 + i: 1 + i for i in range(len(held))},
    )(own, z, *held)


def finish_kernel(groups, cap, *refs):
    hidden_ref, gate_ref, flat_ref = refs[:3]
    own_ref, z_ref = refs[3:5]
    back_refs = refs[5:-1]
    out_ref = refs[-1]
    tokens, width = hidden_ref.shape
    slots = lax.broadcasted_iota(jnp.int32, (tokens, groups * cap), 1)
    picker = (slots == flat_ref[...]).astype(jnp.float32).astype(jnp.bfloat16)
    step = 512
    for at in range(0, width, step):
        cols = slice(at, at + step)
        near = (own_ref[:, cols].astype(jnp.float32) + z_ref[:, cols].astype(jnp.float32)).astype(
            jnp.bfloat16
        )
        found = jnp.concatenate([near] + [r[:, cols] for r in back_refs], axis=0)
        picked = jnp.dot(picker, found, preferred_element_type=jnp.float32)
        out_ref[:, cols] = (hidden_ref[:, cols] + gate_ref[...] * picked).astype(jnp.bfloat16)


def finish(hidden, gate, flat, sums, backs, groups, cap):
    tokens, width = hidden.shape
    operands = [hidden, gate, flat, *sums, *backs]
    return call(
        functools.partial(finish_kernel, groups, cap),
        struct((tokens, width)),
        [VMEM] * len(operands),
        "finish",
        4 * tokens * cap * groups * width,
        16 * tokens * width,
    )(*operands)


def body(state, query, enc_kv, gain, w_in, w_out, expert_id, slot, gate):
    tokens, width = state.shape[2:]
    devices = lax.axis_size("expert")
    pipes = lax.axis_size("pipe")
    groups = devices // WSPLIT
    cap = 3 * tokens // (2 * groups)

    def across(value, bit):
        return lax.ppermute(value, "expert", [(i, i ^ bit) for i in range(devices)])

    def groups_on(value, count):
        shift = count * WSPLIT
        return lax.ppermute(value, "expert", [(i, (i + shift) % devices) for i in range(devices)])

    kv = jnp.transpose(enc_kv[0], (1, 0, 2)).reshape(-1, width)
    kv_pieces = [kv]
    for shift in range(1, pipes):
        perm = [(i, (i + shift) % pipes) for i in range(pipes)]
        kv_pieces.append(lax.ppermute(kv, "pipe", perm))
    def along(value):
        perms = [[(i, (i + shift) % pipes) for i in range(pipes)] for shift in range(1, pipes)]
        return [value] + [lax.ppermute(value, "pipe", perm) for perm in perms]

    def paired(parts):
        return [across(value, 1) for value in parts]

    pipe = lax.axis_index("pipe").astype(jnp.int32)
    w_in_pair, w_out_pair = across(w_in, 1), across(w_out, 1)
    pipe = pipe.reshape(1)
    depth = width // pipes
    in_y, in_late = (cut_part(pipe, w_in, depth, at, depth // 2) for at in (0, depth // 2))
    in_y = across(in_y, 2)
    in_late = across(*after_all([in_late], kv_pieces[1:2]), 2)

    group = (lax.axis_index("expert") // WSPLIT).astype(jnp.int32).reshape(1)
    staged = stage(
        group,
        state[0, 0],
        query[0, 0],
        gain.reshape(1, width),
        expert_id[0],
        slot[0],
        gate[0],
        groups,
        cap,
    )
    flat, gates = staged[4:]
    hidden, near, *packed = attend(
        *staged[:4], kv_pieces, groups, cap, after=[w_in_pair, w_out_pair]
    )
    far = [groups_on(block, count) for count, block in enumerate(packed, 1)]
    far = jnp.concatenate(far, axis=0) if len(far) > 1 else far[0]

    w_in_held, w_out_held, out_part, out_rest = hold(pipe, w_in, w_out, pipes, [near])
    in_first = along(*after_all([in_y], [out_part]))
    in_last = after_all([in_late], [in_first[0]])
    out_part, out_rest = after_all([out_part, out_rest], in_last)
    in_last = along(*in_last)
    out_y, rest_y = across(out_part, 2), across(out_rest, 2)

    near_z = across(near, 4)
    far = [far]
    for step in range(CROSS_STEPS):
        far = after_all(far, [] if step else [near_z], CROSS_WEIGHT)
    (far,) = far
    far_z = [across(far, 4)]
    in_sent = in_last[-1]
    in_parts = after_all([*in_first, *in_last], far_z)
    for _ in range(FAR_STEPS):
        far_z = after_all(far_z, [], FAR_WEIGHT)
    (far_z,) = far_z

    in_pair = paired(in_parts)

    def experts_up(own, z, after=()):
        act = up(own, z, [w_in_held, w_in_pair])
        return up_y(pipe, act, own, z, in_parts, in_pair, pipes, after)

    far_act = experts_up(far, far_z)
    out_parts = along(*after_all([out_y], [in_sent]))
    *out_parts[1:], rest_y = after_all([*out_parts[1:], rest_y], [far_act])
    out_pair = paired(out_parts)
    rests = [rest_y, across(rest_y, 1)]

    def experts_down(act, after=()):
        return down(pipe, act, [w_out_held, w_out_pair], out_parts, out_pair, rests, after)

    far_own, far_sent = experts_down(far_act)
    near_own, near_sent = experts_down(experts_up(near, near_z, [far_own]))
    far_sum, near_sent = total(far_own, across(far_sent, 4), [near_sent])
    backs = [
        groups_on(far_sum[(count - 1) * cap : count * cap], groups - count)
        for count in range(1, groups)
    ]
    backs = after_all(backs, [], BACK_WEIGHT)
    near_sums = [near_own, across(near_sent, 4)]
    output = finish(hidden, gates, flat, near_sums, backs, groups, cap)
    return output.reshape(1, 1, tokens, width)


def solution(mesh):
    return jax.shard_map(
        body,
        mesh=mesh,
        in_specs=(
            P("expert", "pipe", None, None),
            P("expert", "pipe", None, None),
            P("expert", "pipe", None, None),
            P(),
            P(None, "expert"),
            P("expert", None),
            P("expert", "pipe", None),
            P("expert", "pipe", None),
            P("expert", "pipe", None),
        ),
        out_specs=P("expert", "pipe", None, None),
        check_vma=False,
    )
```

```python
import functools
import math

import jax
import jax.numpy as jnp
from jax import lax
from jax.experimental import pallas as pl
from jax.experimental.pallas import tpu as pltpu
from jax.sharding import PartitionSpec as P

HEADS = 16
HD = 128
WSPLIT = 8
EPS = 1e-06
FAR_WEIGHT = 3_000_000_000
FAR_STEPS = 4
CROSS_STEPS = 1
CROSS_WEIGHT = 3_000_000_000
BACK_WEIGHT = 10_000_000_000
VMEM_LIMIT = 32 * 1024 * 1024
PART_LIMIT = 60 * 1024 * 1024

VMEM = pl.BlockSpec(memory_space=pltpu.VMEM)
SMEM = pl.BlockSpec(memory_space=pltpu.SMEM)
ANY = pl.BlockSpec(memory_space=pl.ANY)


def struct(shape, dtype=jnp.bfloat16):
    return jax.ShapeDtypeStruct(shape, dtype)


def call(
    kernel, outs, in_specs, name, flops, moved, scratch=(), out_specs=None, aliases=None, limit=VMEM_LIMIT
):
    return pl.pallas_call(
        kernel,
        out_shape=outs,
        in_specs=in_specs,
        out_specs=out_specs or jax.tree.map(lambda _: VMEM, outs),
        scratch_shapes=list(scratch),
        input_output_aliases=aliases or {},
        compiler_params=pltpu.CompilerParams(vmem_limit_bytes=limit),
        cost_estimate=pl.CostEstimate(flops=flops, bytes_accessed=moved, transcendentals=0),
        name=name,
    )


def as_column(row):
    count = row.shape[1]
    down = lax.broadcasted_iota(jnp.int32, (count, count), 0)
    along = lax.broadcasted_iota(jnp.int32, (count, count), 1)
    return jnp.sum(jnp.where(down == along, row, jnp.zeros_like(row)), axis=1, keepdims=True)


def stage_kernel(groups, cap, *refs):
    group_ref, state_in, query_in, gain_in, expert_ref, slot_ref, gate_ref = refs[:7]
    state_out, query_out, gain_out, flat_row, flat_column, gate_column = refs[7:]
    state_out[...] = state_in[...]
    query_out[...] = query_in[...]
    gain_out[...] = gain_in[...]
    offset = expert_ref[...] - group_ref[0]
    offset = jnp.where(offset < 0, offset + groups, offset)
    slot = slot_ref[...]
    flat = jnp.where(slot >= 0, offset * cap + slot, -1)
    flat_row[...] = flat
    flat_column[...] = as_column(flat)
    gate_column[...] = as_column(gate_ref[...])


def stage(group, state, query, gain, expert_id, slot, gate, groups, cap):
    tokens, width = state.shape
    outs = [
        struct((tokens, width)),
        struct((tokens, width)),
        struct((1, width), jnp.float32),
        struct((1, tokens), jnp.int32),
        struct((tokens, 1), jnp.int32),
        struct((tokens, 1), jnp.float32),
    ]
    return call(
        functools.partial(stage_kernel, groups, cap),
        outs,
        [SMEM] + [VMEM] * 6,
        "stage",
        tokens * tokens,
        8 * tokens * width,
    )(group, state, query, gain, expert_id, slot, gate)


def gate_kernel(*refs):
    pass


def after_all(values, others, weight=1):
    return call(
        gate_kernel,
        [struct(value.shape) for value in values],
        [ANY] * (len(values) + len(others)),
        "hand_on",
        weight,
        1,
        out_specs=[ANY] * len(values),
        aliases={i: i for i in range(len(values))},
    )(*values, *others)


def attend_kernel(pieces, groups, cap, *refs):
    state_ref, query_ref, gain_ref, flat_ref = refs[:4]
    kv_refs = refs[4 : 4 + pieces]
    hidden_ref = refs[-1 - groups]
    packed_refs = refs[-groups:]
    tokens, width = state_ref.shape
    local = kv_refs[0].shape[0] // 2
    scale = 1.0 / math.sqrt(HD)
    squares = jnp.zeros((tokens, HD), jnp.float32)
    for head in range(HEADS):
        cols = slice(head * HD, (head + 1) * HD)
        keys = jnp.concatenate([r[:local, cols] for r in kv_refs], axis=0)
        values = jnp.concatenate([r[local:, cols] for r in kv_refs], axis=0)
        scores = (
            lax.dot_general(
                query_ref[:, cols],
                keys,
                (((1,), (1,)), ((), ())),
                preferred_element_type=jnp.float32,
            )
            * scale
        )
        raised = jnp.exp(scores - jnp.max(scores, axis=1, keepdims=True))
        total = jnp.sum(raised, axis=1, keepdims=True)
        mixed = jnp.dot(raised.astype(jnp.bfloat16), values, preferred_element_type=jnp.float32)
        hidden = state_ref[:, cols].astype(jnp.float32) + mixed / total
        hidden_ref[:, cols] = hidden
        squares = squares + hidden * hidden
    mean_square = jnp.sum(squares, axis=1, keepdims=True) * (1.0 / width)
    inverse = lax.rsqrt(mean_square + EPS)
    rows = lax.broadcasted_iota(jnp.int32, (groups * cap, tokens), 0)
    selector = (rows == flat_ref[...]).astype(jnp.float32).astype(jnp.bfloat16)
    step = 512
    for at in range(0, width, step):
        cols = slice(at, at + step)
        normed = (hidden_ref[:, cols] * inverse * gain_ref[:, cols]).astype(jnp.bfloat16)
        packed = jnp.dot(selector, normed, preferred_element_type=jnp.float32).astype(jnp.bfloat16)
        for group in range(groups):
            packed_refs[group][:, cols] = packed[group * cap : (group + 1) * cap]


def attend(state, query, gain, flat, kv_pieces, groups, cap, after):
    tokens, width = state.shape
    outs = [struct((tokens, width), jnp.float32)] + [struct((cap, width))] * groups
    pieces = len(kv_pieces)
    return call(
        functools.partial(attend_kernel, pieces, groups, cap),
        outs,
        [VMEM] * (4 + pieces) + [ANY] * len(after),
        "attend",
        4 * tokens * pieces * kv_pieces[0].shape[0] * width,
        12 * tokens * width,
    )(state, query, gain, flat, *kv_pieces, *after)


def place(pipes, shift, pipe, size):
    at = pipe - shift
    at = jnp.where(at < 0, at + pipes, at)
    return pl.multiple_of(at * size, size)


def part_kernel(stride, first, pipe_ref, whole, part, sem):
    size = part.shape[0]
    at = pl.multiple_of(pipe_ref[0] * stride + first, size)
    copy = pltpu.make_async_copy(whole.at[pl.ds(at, size)], part, sem)
    copy.start()
    copy.wait()


def cut_part(pipe, whole, stride, first, size):
    return call(
        functools.partial(part_kernel, stride, first),
        struct((size, whole.shape[1])),
        [SMEM, ANY],
        "weight_part",
        1,
        4 * size * whole.shape[1],
        scratch=[pltpu.SemaphoreType.DMA],
        limit=PART_LIMIT,
    )(pipe, whole)


def hold_kernel(pipes, pipe_ref, w_in, w_out, *refs):
    in_held, out_held, out_part, out_rest, sems = refs[-5:]
    size = out_part.shape[0]
    at = pl.multiple_of(pipe_ref[0] * size, size)
    copies = [
        pltpu.make_async_copy(source, target, sems.at[i])
        for i, (source, target) in enumerate(
            (
                (w_in, in_held),
                (w_out, out_held),
                (w_out.at[pl.ds(at, size)], out_part),
                (w_out.at[pipes * size :], out_rest),
            )
        )
    ]
    for copy in copies:
        copy.start()
    for copy in copies:
        copy.wait()


def hold(pipe, w_in, w_out, pipes, after):
    units, width = w_out.shape
    size = units * 7 // 12 // pipes // 16 * 16
    return call(
        functools.partial(hold_kernel, pipes),
        [
            struct(w_in.shape),
            struct(w_out.shape),
            struct((size, width)),
            struct((units - pipes * size, width)),
        ],
        [SMEM, ANY, ANY] + [ANY] * len(after),
        "hold_weights",
        1,
        8 * units * width,
        scratch=[pltpu.SemaphoreType.DMA((4,))],
    )(pipe, w_in, w_out, *after)


def up_kernel(own_in, z_in, w_own, w_pair, out_ref):
    entries = jnp.concatenate([own_in[...], z_in[...]], axis=0)
    weights = jnp.concatenate([w_own[...], w_pair[...]], axis=1)
    raw = jnp.dot(entries, weights, preferred_element_type=jnp.float32)
    out_ref[...] = jnp.maximum(raw, 0.0).astype(jnp.bfloat16)


def up(own, z, w_in):
    rows, width = own.shape
    units = w_in[0].shape[1]
    return call(
        up_kernel,
        struct((2 * rows, 2 * units)),
        [VMEM] * 4,
        "expert_up",
        8 * rows * width * units,
        4 * units * width,
    )(own, z, *w_in)


def up_y_kernel(pipes, halves, *refs):
    pipe = refs[0][0]
    act_ref, own_in, z_in = refs[1:4]
    count = pipes * halves
    y_parts = refs[4 : 4 + count]
    pair_parts = refs[4 + count : 4 + 2 * count]
    out_ref, entries = refs[-2:]
    rows, width = own_in.shape
    units = act_ref.shape[1]
    entries[:rows] = own_in[...]
    entries[rows:] = z_in[...]
    out_ref[:, :units] = act_ref[...]
    depth = width // count
    raw = jnp.zeros(act_ref.shape, jnp.float32)
    for i in range(count):
        half, shift = divmod(i, pipes)
        at = place(pipes, shift, pipe, halves * depth) + half * depth
        part = entries[:, pl.ds(pl.multiple_of(at, depth), depth)]
        weights = jnp.concatenate([y_parts[i][...], pair_parts[i][...]], axis=1)
        raw = raw + jnp.dot(part, weights, preferred_element_type=jnp.float32)
    out_ref[:, units:] = jnp.maximum(raw, 0.0).astype(jnp.bfloat16)


def up_y(pipe, act, own, z, y_parts, pair_parts, pipes, after=()):
    rows, width = own.shape
    units = y_parts[0].shape[1]
    count = len(y_parts)
    return call(
        functools.partial(up_y_kernel, pipes, count // pipes),
        struct((2 * rows, 4 * units)),
        [SMEM] + [VMEM] * (3 + 2 * count) + [ANY] * len(after),
        "expert_up_y",
        8 * rows * width * units,
        4 * units * width,
        scratch=[pltpu.VMEM((2 * rows, width), jnp.bfloat16)],
    )(pipe, act, own, z, *y_parts, *pair_parts, *after)


def down_kernel(pipes, first, *refs):
    pipe = refs[0][0]
    act_ref, w_own, w_pair = refs[1:4]
    y_parts, refs = refs[4 : 4 + pipes], refs[4 + pipes :]
    pair_parts, refs = refs[:pipes], refs[pipes:]
    y_rest, pair_rest = refs[:2]
    own_ref, z_ref, held = refs[-3:]
    rows, width = own_ref.shape
    whole = slice(first, first + width)
    units = w_own.shape[0]
    size = y_parts[0].shape[0]
    for shift in range(pipes):
        at = place(pipes, shift, pipe, size)
        held[pl.ds(at, size)] = y_parts[shift][:, whole]
        held[pl.ds(pl.multiple_of(units + at, size), size)] = pair_parts[shift][:, whole]
    held[pipes * size : units] = y_rest[:, whole]
    held[units + pipes * size :] = pair_rest[:, whole]
    step = 512
    for at in range(0, width, step):
        cols = slice(at, at + step)
        there = slice(first + at, first + at + step)
        weights = jnp.concatenate([w_own[:, there], w_pair[:, there], held[:, cols]], axis=0)
        part = jnp.dot(act_ref[...], weights, preferred_element_type=jnp.float32)
        part = part.astype(jnp.bfloat16)
        own_ref[:, cols] = part[:rows]
        z_ref[:, cols] = part[rows:]


def down(pipe, act, w_out, y_parts, pair_parts, rests, first, width, after=()):
    rows = act.shape[0] // 2
    units = w_out[0].shape[0]
    pipes = len(y_parts)
    return call(
        functools.partial(down_kernel, pipes, first),
        [struct((rows, width))] * 2,
        [SMEM] + [VMEM] * (5 + 2 * pipes) + [ANY] * len(after),
        "expert_down",
        16 * rows * width * units,
        8 * units * width,
        scratch=[pltpu.VMEM((2 * units, width), jnp.bfloat16)],
    )(pipe, act, *w_out, *y_parts, *pair_parts, *rests, *after)


def total_kernel(held, own_ref, z_ref, *refs):
    refs[held][...] = (own_ref[...].astype(jnp.float32) + z_ref[...].astype(jnp.float32)).astype(
        jnp.bfloat16
    )


def total(own, z, held):
    outs = [struct(own.shape)] + [struct(value.shape) for value in held]
    return call(
        functools.partial(total_kernel, len(held)),
        outs,
        [VMEM] * 2 + [ANY] * len(held),
        "far_total",
        own.size,
        6 * own.size,
        out_specs=[VMEM] + [ANY] * len(held),
        aliases={2 + i: 1 + i for i in range(len(held))},
    )(own, z, *held)


def finish_kernel(groups, cap, *refs):
    hidden_ref, gate_ref, flat_ref = refs[:3]
    own_ref, z_ref = refs[3:5]
    back_refs = refs[5:-1]
    out_ref = refs[-1]
    tokens, width = hidden_ref.shape
    slots = lax.broadcasted_iota(jnp.int32, (tokens, groups * cap), 1)
    picker = (slots == flat_ref[...]).astype(jnp.float32).astype(jnp.bfloat16)
    step = 512
    for at in range(0, width, step):
        cols = slice(at, at + step)
        near = (own_ref[:, cols].astype(jnp.float32) + z_ref[:, cols].astype(jnp.float32)).astype(
            jnp.bfloat16
        )
        side, inner = divmod(at, width // 2)
        backs = [r[:, inner : inner + step] for r in back_refs[side::2]]
        found = jnp.concatenate([near, *backs], axis=0)
        picked = jnp.dot(picker, found, preferred_element_type=jnp.float32)
        out_ref[:, cols] = (hidden_ref[:, cols] + gate_ref[...] * picked).astype(jnp.bfloat16)


def finish(hidden, gate, flat, sums, backs, groups, cap):
    tokens, width = hidden.shape
    operands = [hidden, gate, flat, *sums, *backs]
    return call(
        functools.partial(finish_kernel, groups, cap),
        struct((tokens, width)),
        [VMEM] * len(operands),
        "finish",
        4 * tokens * cap * groups * width,
        16 * tokens * width,
    )(*operands)


def body(state, query, enc_kv, gain, w_in, w_out, expert_id, slot, gate):
    tokens, width = state.shape[2:]
    devices = lax.axis_size("expert")
    pipes = lax.axis_size("pipe")
    groups = devices // WSPLIT
    cap = 3 * tokens // (2 * groups)

    def across(value, bit):
        return lax.ppermute(value, "expert", [(i, i ^ bit) for i in range(devices)])

    def groups_on(value, count):
        shift = count * WSPLIT
        return lax.ppermute(value, "expert", [(i, (i + shift) % devices) for i in range(devices)])

    def along(value):
        perms = [[(i, (i + shift) % pipes) for i in range(pipes)] for shift in range(1, pipes)]
        return [value] + [lax.ppermute(value, "pipe", perm) for perm in perms]

    def paired(parts):
        return [across(value, 1) for value in parts]

    pipe = lax.axis_index("pipe").astype(jnp.int32)
    w_in_pair, w_out_pair = across(w_in, 1), across(w_out, 1)
    pipe = pipe.reshape(1)
    depth = width // pipes
    in_y, in_late = (cut_part(pipe, w_in, depth, at, depth // 2) for at in (0, depth // 2))
    kv = jnp.transpose(enc_kv[0], (1, 0, 2)).reshape(-1, width)
    (kv,) = after_all([kv], [in_y])
    kv_pieces = [kv]
    for shift in range(1, pipes):
        perm = [(i, (i + shift) % pipes) for i in range(pipes)]
        kv_pieces.append(lax.ppermute(kv, "pipe", perm))
    in_y = across(in_y, 2)
    in_late = across(*after_all([in_late], kv_pieces[1:2]), 2)

    group = (lax.axis_index("expert") // WSPLIT).astype(jnp.int32).reshape(1)
    staged = stage(
        group,
        state[0, 0],
        query[0, 0],
        gain.reshape(1, width),
        expert_id[0],
        slot[0],
        gate[0],
        groups,
        cap,
    )
    flat, gates = staged[4:]
    hidden, near, *packed = attend(
        *staged[:4], kv_pieces, groups, cap, after=[w_in_pair, w_out_pair]
    )
    far = [groups_on(block, count) for count, block in enumerate(packed, 1)]
    far = jnp.concatenate(far, axis=0) if len(far) > 1 else far[0]

    w_in_held, w_out_held, out_part, out_rest = hold(pipe, w_in, w_out, pipes, [near])
    in_first = along(*after_all([in_y], [out_part]))
    in_last = after_all([in_late], [in_first[0]])
    out_part, out_rest = after_all([out_part, out_rest], in_last)
    in_last = along(*in_last)
    out_y, rest_y = across(out_part, 2), across(out_rest, 2)

    near_z = across(near, 4)
    far = [far]
    for step in range(CROSS_STEPS):
        far = after_all(far, [] if step else [near_z], CROSS_WEIGHT)
    (far,) = far
    far_z = [across(far, 4)]
    in_sent = in_last[-1]
    in_parts = after_all([*in_first, *in_last], far_z)
    for _ in range(FAR_STEPS):
        far_z = after_all(far_z, [], FAR_WEIGHT)
    (far_z,) = far_z

    in_pair = paired(in_parts)

    def experts_up(own, z, after=()):
        act = up(own, z, [w_in_held, w_in_pair])
        return up_y(pipe, act, own, z, in_parts, in_pair, pipes, after)

    far_act = experts_up(far, far_z)
    out_parts = along(*after_all([out_y], [in_sent]))
    out_pair = paired(out_parts[:1])
    *out_parts[1:], rest_y = after_all([*out_parts[1:], rest_y], [far_act, *out_pair])
    out_pair += paired(out_parts[1:])
    rests = [rest_y, across(rest_y, 1)]

    def experts_down(act, first, size, after=()):
        return down(
            pipe, act, [w_out_held, w_out_pair], out_parts, out_pair, rests, first, size, after
        )

    half = width // 2
    far_a, sent_a = experts_down(far_act, 0, half)
    far_b, sent_b = experts_down(far_act, half, half, [far_a])
    near_act = experts_up(near, near_z, [far_b])
    (sent_b,) = after_all([sent_b], [near_act])
    near_own, near_sent = experts_down(near_act, 0, width)
    (sum_a,) = total(far_a, across(sent_a, 4), [])
    sum_b, near_sent = total(far_b, across(sent_b, 4), [near_sent])
    backs = [
        groups_on(side[(count - 1) * cap : count * cap], groups - count)
        for count in range(1, groups)
        for side in (sum_a, sum_b)
    ]
    backs = after_all(backs, [], BACK_WEIGHT)
    near_sums = [near_own, across(near_sent, 4)]
    output = finish(hidden, gates, flat, near_sums, backs, groups, cap)
    return output.reshape(1, 1, tokens, width)


def solution(mesh):
    return jax.shard_map(
        body,
        mesh=mesh,
        in_specs=(
            P("expert", "pipe", None, None),
            P("expert", "pipe", None, None),
            P("expert", "pipe", None, None),
            P(),
            P(None, "expert"),
            P("expert", None),
            P("expert", "pipe", None),
            P("expert", "pipe", None),
            P("expert", "pipe", None),
        ),
        out_specs=P("expert", "pipe", None, None),
        check_vma=False,
    )
```

```python
import functools
import math

import jax
import jax.numpy as jnp
from jax import lax
from jax.experimental import pallas as pl
from jax.experimental.pallas import tpu as pltpu
from jax.sharding import PartitionSpec as P

HEADS = 16
HD = 128
WSPLIT = 8
EPS = 1e-06
FAR_WEIGHT = 3_000_000_000
FAR_STEPS = 4
CROSS_STEPS = 1
CROSS_WEIGHT = 3_000_000_000
SUM_WEIGHT = 1_000_000_000
BACK_WEIGHT = 3_000_000_000
VMEM_LIMIT = 32 * 1024 * 1024
PART_LIMIT = 60 * 1024 * 1024

VMEM = pl.BlockSpec(memory_space=pltpu.VMEM)
SMEM = pl.BlockSpec(memory_space=pltpu.SMEM)
ANY = pl.BlockSpec(memory_space=pl.ANY)


def struct(shape, dtype=jnp.bfloat16):
    return jax.ShapeDtypeStruct(shape, dtype)


def call(
    kernel, outs, in_specs, name, flops, moved, scratch=(), out_specs=None, aliases=None, limit=VMEM_LIMIT
):
    return pl.pallas_call(
        kernel,
        out_shape=outs,
        in_specs=in_specs,
        out_specs=out_specs or jax.tree.map(lambda _: VMEM, outs),
        scratch_shapes=list(scratch),
        input_output_aliases=aliases or {},
        compiler_params=pltpu.CompilerParams(vmem_limit_bytes=limit),
        cost_estimate=pl.CostEstimate(flops=flops, bytes_accessed=moved, transcendentals=0),
        name=name,
    )


def as_column(row):
    count = row.shape[1]
    down = lax.broadcasted_iota(jnp.int32, (count, count), 0)
    along = lax.broadcasted_iota(jnp.int32, (count, count), 1)
    return jnp.sum(jnp.where(down == along, row, jnp.zeros_like(row)), axis=1, keepdims=True)


def stage_kernel(groups, cap, *refs):
    group_ref, state_in, query_in, gain_in, expert_ref, slot_ref, gate_ref = refs[:7]
    state_out, query_out, gain_out, flat_row, flat_column, gate_column = refs[7:]
    state_out[...] = state_in[...]
    query_out[...] = query_in[...]
    gain_out[...] = gain_in[...]
    offset = expert_ref[...] - group_ref[0]
    offset = jnp.where(offset < 0, offset + groups, offset)
    slot = slot_ref[...]
    flat = jnp.where(slot >= 0, offset * cap + slot, -1)
    flat_row[...] = flat
    flat_column[...] = as_column(flat)
    gate_column[...] = as_column(gate_ref[...])


def stage(group, state, query, gain, expert_id, slot, gate, groups, cap):
    tokens, width = state.shape
    outs = [
        struct((tokens, width)),
        struct((tokens, width)),
        struct((1, width), jnp.float32),
        struct((1, tokens), jnp.int32),
        struct((tokens, 1), jnp.int32),
        struct((tokens, 1), jnp.float32),
    ]
    return call(
        functools.partial(stage_kernel, groups, cap),
        outs,
        [SMEM] + [VMEM] * 6,
        "stage",
        tokens * tokens,
        8 * tokens * width,
    )(group, state, query, gain, expert_id, slot, gate)


def gate_kernel(*refs):
    pass


def after_all(values, others, weight=1):
    return call(
        gate_kernel,
        [struct(value.shape) for value in values],
        [ANY] * (len(values) + len(others)),
        "hand_on",
        weight,
        1,
        out_specs=[ANY] * len(values),
        aliases={i: i for i in range(len(values))},
    )(*values, *others)


def attend_kernel(pieces, groups, cap, *refs):
    state_ref, query_ref, gain_ref, flat_ref = refs[:4]
    kv_refs = refs[4 : 4 + pieces]
    hidden_ref = refs[-1 - groups]
    packed_refs = refs[-groups:]
    tokens, width = state_ref.shape
    local = kv_refs[0].shape[0] // 2
    scale = 1.0 / math.sqrt(HD)
    squares = jnp.zeros((tokens, HD), jnp.float32)
    for head in range(HEADS):
        cols = slice(head * HD, (head + 1) * HD)
        keys = jnp.concatenate([r[:local, cols] for r in kv_refs], axis=0)
        values = jnp.concatenate([r[local:, cols] for r in kv_refs], axis=0)
        scores = (
            lax.dot_general(
                query_ref[:, cols],
                keys,
                (((1,), (1,)), ((), ())),
                preferred_element_type=jnp.float32,
            )
            * scale
        )
        raised = jnp.exp(scores - jnp.max(scores, axis=1, keepdims=True))
        total = jnp.sum(raised, axis=1, keepdims=True)
        mixed = jnp.dot(raised.astype(jnp.bfloat16), values, preferred_element_type=jnp.float32)
        hidden = state_ref[:, cols].astype(jnp.float32) + mixed / total
        hidden_ref[:, cols] = hidden
        squares = squares + hidden * hidden
    mean_square = jnp.sum(squares, axis=1, keepdims=True) * (1.0 / width)
    inverse = lax.rsqrt(mean_square + EPS)
    rows = lax.broadcasted_iota(jnp.int32, (groups * cap, tokens), 0)
    selector = (rows == flat_ref[...]).astype(jnp.float32).astype(jnp.bfloat16)
    step = 512
    for at in range(0, width, step):
        cols = slice(at, at + step)
        normed = (hidden_ref[:, cols] * inverse * gain_ref[:, cols]).astype(jnp.bfloat16)
        packed = jnp.dot(selector, normed, preferred_element_type=jnp.float32).astype(jnp.bfloat16)
        for group in range(groups):
            packed_refs[group][:, cols] = packed[group * cap : (group + 1) * cap]


def attend(state, query, gain, flat, kv_pieces, groups, cap, after):
    tokens, width = state.shape
    outs = [struct((tokens, width), jnp.float32)] + [struct((cap, width))] * groups
    pieces = len(kv_pieces)
    return call(
        functools.partial(attend_kernel, pieces, groups, cap),
        outs,
        [VMEM] * (4 + pieces) + [ANY] * len(after),
        "attend",
        4 * tokens * pieces * kv_pieces[0].shape[0] * width,
        12 * tokens * width,
    )(state, query, gain, flat, *kv_pieces, *after)


def place(pipes, shift, pipe, size):
    at = pipe - shift
    at = jnp.where(at < 0, at + pipes, at)
    return pl.multiple_of(at * size, size)


def part_kernel(stride, first, pipe_ref, whole, part, sem):
    size = part.shape[0]
    at = pl.multiple_of(pipe_ref[0] * stride + first, size)
    copy = pltpu.make_async_copy(whole.at[pl.ds(at, size)], part, sem)
    copy.start()
    copy.wait()


def cut_part(pipe, whole, stride, first, size):
    return call(
        functools.partial(part_kernel, stride, first),
        struct((size, whole.shape[1])),
        [SMEM, ANY],
        "weight_part",
        1,
        4 * size * whole.shape[1],
        scratch=[pltpu.SemaphoreType.DMA],
        limit=PART_LIMIT,
    )(pipe, whole)


def hold_kernel(pipes, pipe_ref, w_in, w_out, *refs):
    in_held, out_held, out_part, out_rest, sems = refs[-5:]
    size = out_part.shape[0]
    at = pl.multiple_of(pipe_ref[0] * size, size)
    copies = [
        pltpu.make_async_copy(source, target, sems.at[i])
        for i, (source, target) in enumerate(
            (
                (w_in, in_held),
                (w_out, out_held),
                (w_out.at[pl.ds(at, size)], out_part),
                (w_out.at[pipes * size :], out_rest),
            )
        )
    ]
    for copy in copies:
        copy.start()
    for copy in copies:
        copy.wait()


def hold(pipe, w_in, w_out, pipes, after):
    units, width = w_out.shape
    size = units * 7 // 12 // pipes // 16 * 16
    return call(
        functools.partial(hold_kernel, pipes),
        [
            struct(w_in.shape),
            struct(w_out.shape),
            struct((size, width)),
            struct((units - pipes * size, width)),
        ],
        [SMEM, ANY, ANY] + [ANY] * len(after),
        "hold_weights",
        1,
        8 * units * width,
        scratch=[pltpu.SemaphoreType.DMA((4,))],
    )(pipe, w_in, w_out, *after)


def up_kernel(own_in, z_in, w_own, w_pair, out_ref):
    entries = jnp.concatenate([own_in[...], z_in[...]], axis=0)
    weights = jnp.concatenate([w_own[...], w_pair[...]], axis=1)
    raw = jnp.dot(entries, weights, preferred_element_type=jnp.float32)
    out_ref[...] = jnp.maximum(raw, 0.0).astype(jnp.bfloat16)


def up(own, z, w_in):
    rows, width = own.shape
    units = w_in[0].shape[1]
    return call(
        up_kernel,
        struct((2 * rows, 2 * units)),
        [VMEM] * 4,
        "expert_up",
        8 * rows * width * units,
        4 * units * width,
    )(own, z, *w_in)


def up_y_kernel(pipes, halves, *refs):
    pipe = refs[0][0]
    act_ref, own_in, z_in = refs[1:4]
    count = pipes * halves
    y_parts = refs[4 : 4 + count]
    pair_parts = refs[4 + count : 4 + 2 * count]
    out_ref, entries = refs[-2:]
    rows, width = own_in.shape
    units = act_ref.shape[1]
    entries[:rows] = own_in[...]
    entries[rows:] = z_in[...]
    out_ref[:, :units] = act_ref[...]
    depth = width // count
    raw = jnp.zeros(act_ref.shape, jnp.float32)
    for i in range(count):
        half, shift = divmod(i, pipes)
        at = place(pipes, shift, pipe, halves * depth) + half * depth
        part = entries[:, pl.ds(pl.multiple_of(at, depth), depth)]
        weights = jnp.concatenate([y_parts[i][...], pair_parts[i][...]], axis=1)
        raw = raw + jnp.dot(part, weights, preferred_element_type=jnp.float32)
    out_ref[:, units:] = jnp.maximum(raw, 0.0).astype(jnp.bfloat16)


def up_y(pipe, act, own, z, y_parts, pair_parts, pipes, after=()):
    rows, width = own.shape
    units = y_parts[0].shape[1]
    count = len(y_parts)
    return call(
        functools.partial(up_y_kernel, pipes, count // pipes),
        struct((2 * rows, 4 * units)),
        [SMEM] + [VMEM] * (3 + 2 * count) + [ANY] * len(after),
        "expert_up_y",
        8 * rows * width * units,
        4 * units * width,
        scratch=[pltpu.VMEM((2 * rows, width), jnp.bfloat16)],
    )(pipe, act, own, z, *y_parts, *pair_parts, *after)


def down_kernel(pipes, first, *refs):
    pipe = refs[0][0]
    act_ref, w_own, w_pair = refs[1:4]
    y_parts, refs = refs[4 : 4 + pipes], refs[4 + pipes :]
    pair_parts, refs = refs[:pipes], refs[pipes:]
    y_rest, pair_rest = refs[:2]
    own_ref, z_ref, held = refs[-3:]
    rows, width = own_ref.shape
    whole = slice(first, first + width)
    units = w_own.shape[0]
    size = y_parts[0].shape[0]
    for shift in range(pipes):
        at = place(pipes, shift, pipe, size)
        held[pl.ds(at, size)] = y_parts[shift][:, whole]
        held[pl.ds(pl.multiple_of(units + at, size), size)] = pair_parts[shift][:, whole]
    held[pipes * size : units] = y_rest[:, whole]
    held[units + pipes * size :] = pair_rest[:, whole]
    step = 512
    for at in range(0, width, step):
        cols = slice(at, at + step)
        there = slice(first + at, first + at + step)
        weights = jnp.concatenate([w_own[:, there], w_pair[:, there], held[:, cols]], axis=0)
        part = jnp.dot(act_ref[...], weights, preferred_element_type=jnp.float32)
        part = part.astype(jnp.bfloat16)
        own_ref[:, cols] = part[:rows]
        z_ref[:, cols] = part[rows:]


def down(pipe, act, w_out, y_parts, pair_parts, rests, first, width, after=()):
    rows = act.shape[0] // 2
    units = w_out[0].shape[0]
    pipes = len(y_parts)
    return call(
        functools.partial(down_kernel, pipes, first),
        [struct((rows, width))] * 2,
        [SMEM] + [VMEM] * (5 + 2 * pipes) + [ANY] * len(after),
        "expert_down",
        16 * rows * width * units,
        8 * units * width,
        scratch=[pltpu.VMEM((2 * units, width), jnp.bfloat16)],
    )(pipe, act, *w_out, *y_parts, *pair_parts, *rests, *after)


def total_kernel(held, own_ref, z_ref, *refs):
    refs[held][...] = (own_ref[...].astype(jnp.float32) + z_ref[...].astype(jnp.float32)).astype(
        jnp.bfloat16
    )


def total(own, z, held):
    outs = [struct(own.shape)] + [struct(value.shape) for value in held]
    return call(
        functools.partial(total_kernel, len(held)),
        outs,
        [VMEM] * 2 + [ANY] * len(held),
        "far_total",
        own.size,
        6 * own.size,
        out_specs=[VMEM] + [ANY] * len(held),
        aliases={2 + i: 1 + i for i in range(len(held))},
    )(own, z, *held)


def finish_kernel(groups, cap, *refs):
    hidden_ref, gate_ref, flat_ref = refs[:3]
    own_ref, z_ref = refs[3:5]
    back_refs = refs[5:-1]
    out_ref = refs[-1]
    tokens, width = hidden_ref.shape
    slots = lax.broadcasted_iota(jnp.int32, (tokens, groups * cap), 1)
    picker = (slots == flat_ref[...]).astype(jnp.float32).astype(jnp.bfloat16)
    step = 512
    for at in range(0, width, step):
        cols = slice(at, at + step)
        near = (own_ref[:, cols].astype(jnp.float32) + z_ref[:, cols].astype(jnp.float32)).astype(
            jnp.bfloat16
        )
        side, inner = divmod(at, width // 2)
        backs = [r[:, inner : inner + step] for r in back_refs[side::2]]
        found = jnp.concatenate([near, *backs], axis=0)
        picked = jnp.dot(picker, found, preferred_element_type=jnp.float32)
        out_ref[:, cols] = (hidden_ref[:, cols] + gate_ref[...] * picked).astype(jnp.bfloat16)


def finish(hidden, gate, flat, sums, backs, groups, cap):
    tokens, width = hidden.shape
    operands = [hidden, gate, flat, *sums, *backs]
    return call(
        functools.partial(finish_kernel, groups, cap),
        struct((tokens, width)),
        [VMEM] * len(operands),
        "finish",
        4 * tokens * cap * groups * width,
        16 * tokens * width,
    )(*operands)


def body(state, query, enc_kv, gain, w_in, w_out, expert_id, slot, gate):
    tokens, width = state.shape[2:]
    devices = lax.axis_size("expert")
    pipes = lax.axis_size("pipe")
    groups = devices // WSPLIT
    cap = 3 * tokens // (2 * groups)

    def across(value, bit):
        return lax.ppermute(value, "expert", [(i, i ^ bit) for i in range(devices)])

    def groups_on(value, count):
        shift = count * WSPLIT
        return lax.ppermute(value, "expert", [(i, (i + shift) % devices) for i in range(devices)])

    def along(value):
        perms = [[(i, (i + shift) % pipes) for i in range(pipes)] for shift in range(1, pipes)]
        return [value] + [lax.ppermute(value, "pipe", perm) for perm in perms]

    def paired(parts):
        return [across(value, 1) for value in parts]

    pipe = lax.axis_index("pipe").astype(jnp.int32)
    w_in_pair, w_out_pair = across(w_in, 1), across(w_out, 1)
    pipe = pipe.reshape(1)
    depth = width // pipes
    in_y, in_late = (cut_part(pipe, w_in, depth, at, depth // 2) for at in (0, depth // 2))
    kv = jnp.transpose(enc_kv[0], (1, 0, 2)).reshape(-1, width)
    (kv,) = after_all([kv], [in_y])
    kv_pieces = [kv]
    for shift in range(1, pipes):
        perm = [(i, (i + shift) % pipes) for i in range(pipes)]
        kv_pieces.append(lax.ppermute(kv, "pipe", perm))
    in_y = across(in_y, 2)
    in_late = across(*after_all([in_late], kv_pieces[1:2]), 2)

    group = (lax.axis_index("expert") // WSPLIT).astype(jnp.int32).reshape(1)
    staged = stage(
        group,
        state[0, 0],
        query[0, 0],
        gain.reshape(1, width),
        expert_id[0],
        slot[0],
        gate[0],
        groups,
        cap,
    )
    flat, gates = staged[4:]
    hidden, near, *packed = attend(
        *staged[:4], kv_pieces, groups, cap, after=[w_in_pair, w_out_pair]
    )
    far = [groups_on(block, count) for count, block in enumerate(packed, 1)]
    far = jnp.concatenate(far, axis=0) if len(far) > 1 else far[0]

    w_in_held, w_out_held, out_part, out_rest = hold(pipe, w_in, w_out, pipes, [near])
    in_first = along(*after_all([in_y], [out_part]))
    in_last = after_all([in_late], [in_first[0]])
    out_part, out_rest = after_all([out_part, out_rest], in_last)
    in_last = along(*in_last)
    out_y, rest_y = across(out_part, 2), across(out_rest, 2)

    near_z = across(near, 4)
    far = [far]
    for step in range(CROSS_STEPS):
        far = after_all(far, [] if step else [near_z], CROSS_WEIGHT)
    (far,) = far
    far_z = [across(far, 4)]
    in_sent = in_last[-1]
    in_parts = after_all([*in_first, *in_last], far_z)
    for _ in range(FAR_STEPS):
        far_z = after_all(far_z, [], FAR_WEIGHT)
    (far_z,) = far_z

    in_pair = paired(in_parts)

    def experts_up(own, z, after=()):
        act = up(own, z, [w_in_held, w_in_pair])
        return up_y(pipe, act, own, z, in_parts, in_pair, pipes, after)

    far_act = experts_up(far, far_z)
    out_parts = along(*after_all([out_y], [in_sent]))
    out_pair = paired(out_parts[:1])
    *out_parts[1:], rest_y = after_all([*out_parts[1:], rest_y], [far_act, *out_pair])
    out_pair += paired(out_parts[1:])
    rests = [rest_y, across(rest_y, 1)]

    def experts_down(act, first, size, after=()):
        return down(
            pipe, act, [w_out_held, w_out_pair], out_parts, out_pair, rests, first, size, after
        )

    half = width // 2
    far_a, sent_a = experts_down(far_act, 0, half)
    far_b, sent_b = experts_down(far_act, half, half, [far_a])
    near_act = experts_up(near, near_z, [far_b])
    (sent_b,) = after_all([sent_b], [near_act])
    near_own, near_sent = experts_down(near_act, 0, width)
    (sum_a,) = total(far_a, across(sent_a, 4), [])
    sum_b, near_sent = total(far_b, across(sent_b, 4), [near_sent])
    backs = [
        groups_on(side[(count - 1) * cap : count * cap], groups - count)
        for count in range(1, groups)
        for side in (sum_a, sum_b)
    ]
    backs[::2] = after_all(backs[::2], [], SUM_WEIGHT)
    backs[::2] = after_all(backs[::2], [], BACK_WEIGHT)
    near_sums = [near_own, across(near_sent, 4)]
    output = finish(hidden, gates, flat, near_sums, backs, groups, cap)
    return output.reshape(1, 1, tokens, width)


def solution(mesh):
    return jax.shard_map(
        body,
        mesh=mesh,
        in_specs=(
            P("expert", "pipe", None, None),
            P("expert", "pipe", None, None),
            P("expert", "pipe", None, None),
            P(),
            P(None, "expert"),
            P("expert", None),
            P("expert", "pipe", None),
            P("expert", "pipe", None),
            P("expert", "pipe", None),
        ),
        out_specs=P("expert", "pipe", None, None),
        check_vma=False,
    )
```

```python
import functools
import math

import jax
import jax.numpy as jnp
from jax import lax
from jax.experimental import pallas as pl
from jax.experimental.pallas import tpu as pltpu
from jax.sharding import PartitionSpec as P

HEADS = 16
HD = 128
WSPLIT = 8
EPS = 1e-06
FAR_WEIGHT = 3_000_000_000
FAR_STEPS = 4
CROSS_STEPS = 1
CROSS_WEIGHT = 3_000_000_000
FIRST_WEIGHT = 8_000_000_000
SUM_WEIGHT = 1_000_000_000
BACK_WEIGHT = 3_000_000_000
VMEM_LIMIT = 32 * 1024 * 1024
PART_LIMIT = 60 * 1024 * 1024

VMEM = pl.BlockSpec(memory_space=pltpu.VMEM)
SMEM = pl.BlockSpec(memory_space=pltpu.SMEM)
ANY = pl.BlockSpec(memory_space=pl.ANY)


def struct(shape, dtype=jnp.bfloat16):
    return jax.ShapeDtypeStruct(shape, dtype)


def call(
    kernel, outs, in_specs, name, flops, moved, scratch=(), out_specs=None, aliases=None, limit=VMEM_LIMIT
):
    return pl.pallas_call(
        kernel,
        out_shape=outs,
        in_specs=in_specs,
        out_specs=out_specs or jax.tree.map(lambda _: VMEM, outs),
        scratch_shapes=list(scratch),
        input_output_aliases=aliases or {},
        compiler_params=pltpu.CompilerParams(vmem_limit_bytes=limit),
        cost_estimate=pl.CostEstimate(flops=flops, bytes_accessed=moved, transcendentals=0),
        name=name,
    )


def as_column(row):
    count = row.shape[1]
    down = lax.broadcasted_iota(jnp.int32, (count, count), 0)
    along = lax.broadcasted_iota(jnp.int32, (count, count), 1)
    return jnp.sum(jnp.where(down == along, row, jnp.zeros_like(row)), axis=1, keepdims=True)


def stage_kernel(groups, cap, *refs):
    group_ref, state_in, query_in, gain_in, expert_ref, slot_ref, gate_ref = refs[:7]
    state_out, query_out, gain_out, flat_row, flat_column, gate_column = refs[7:]
    state_out[...] = state_in[...]
    query_out[...] = query_in[...]
    gain_out[...] = gain_in[...]
    offset = expert_ref[...] - group_ref[0]
    offset = jnp.where(offset < 0, offset + groups, offset)
    slot = slot_ref[...]
    flat = jnp.where(slot >= 0, offset * cap + slot, -1)
    flat_row[...] = flat
    flat_column[...] = as_column(flat)
    gate_column[...] = as_column(gate_ref[...])


def stage(group, state, query, gain, expert_id, slot, gate, groups, cap):
    tokens, width = state.shape
    outs = [
        struct((tokens, width)),
        struct((tokens, width)),
        struct((1, width), jnp.float32),
        struct((1, tokens), jnp.int32),
        struct((tokens, 1), jnp.int32),
        struct((tokens, 1), jnp.float32),
    ]
    return call(
        functools.partial(stage_kernel, groups, cap),
        outs,
        [SMEM] + [VMEM] * 6,
        "stage",
        tokens * tokens,
        8 * tokens * width,
    )(group, state, query, gain, expert_id, slot, gate)


def gate_kernel(*refs):
    pass


def after_all(values, others, weight=1):
    return call(
        gate_kernel,
        [struct(value.shape) for value in values],
        [ANY] * (len(values) + len(others)),
        "hand_on",
        weight,
        1,
        out_specs=[ANY] * len(values),
        aliases={i: i for i in range(len(values))},
    )(*values, *others)


def attend_kernel(pieces, groups, cap, *refs):
    state_ref, query_ref, gain_ref, flat_ref = refs[:4]
    kv_refs = refs[4 : 4 + pieces]
    hidden_ref = refs[-1 - groups]
    packed_refs = refs[-groups:]
    tokens, width = state_ref.shape
    local = kv_refs[0].shape[0] // 2
    scale = 1.0 / math.sqrt(HD)
    squares = jnp.zeros((tokens, HD), jnp.float32)
    for head in range(HEADS):
        cols = slice(head * HD, (head + 1) * HD)
        keys = jnp.concatenate([r[:local, cols] for r in kv_refs], axis=0)
        values = jnp.concatenate([r[local:, cols] for r in kv_refs], axis=0)
        scores = (
            lax.dot_general(
                query_ref[:, cols],
                keys,
                (((1,), (1,)), ((), ())),
                preferred_element_type=jnp.float32,
            )
            * scale
        )
        raised = jnp.exp(scores - jnp.max(scores, axis=1, keepdims=True))
        total = jnp.sum(raised, axis=1, keepdims=True)
        mixed = jnp.dot(raised.astype(jnp.bfloat16), values, preferred_element_type=jnp.float32)
        hidden = state_ref[:, cols].astype(jnp.float32) + mixed / total
        hidden_ref[:, cols] = hidden
        squares = squares + hidden * hidden
    mean_square = jnp.sum(squares, axis=1, keepdims=True) * (1.0 / width)
    inverse = lax.rsqrt(mean_square + EPS)
    rows = lax.broadcasted_iota(jnp.int32, (groups * cap, tokens), 0)
    selector = (rows == flat_ref[...]).astype(jnp.float32).astype(jnp.bfloat16)
    step = 512
    for at in range(0, width, step):
        cols = slice(at, at + step)
        normed = (hidden_ref[:, cols] * inverse * gain_ref[:, cols]).astype(jnp.bfloat16)
        packed = jnp.dot(selector, normed, preferred_element_type=jnp.float32).astype(jnp.bfloat16)
        for group in range(groups):
            packed_refs[group][:, cols] = packed[group * cap : (group + 1) * cap]


def attend(state, query, gain, flat, kv_pieces, groups, cap, after):
    tokens, width = state.shape
    outs = [struct((tokens, width), jnp.float32)] + [struct((cap, width))] * groups
    pieces = len(kv_pieces)
    return call(
        functools.partial(attend_kernel, pieces, groups, cap),
        outs,
        [VMEM] * (4 + pieces) + [ANY] * len(after),
        "attend",
        4 * tokens * pieces * kv_pieces[0].shape[0] * width,
        12 * tokens * width,
    )(state, query, gain, flat, *kv_pieces, *after)


def place(pipes, shift, pipe, size):
    at = pipe - shift
    at = jnp.where(at < 0, at + pipes, at)
    return pl.multiple_of(at * size, size)


def part_kernel(stride, first, pipe_ref, whole, part, sem):
    size = part.shape[0]
    at = pl.multiple_of(pipe_ref[0] * stride + first, size)
    copy = pltpu.make_async_copy(whole.at[pl.ds(at, size)], part, sem)
    copy.start()
    copy.wait()


def cut_part(pipe, whole, stride, first, size):
    return call(
        functools.partial(part_kernel, stride, first),
        struct((size, whole.shape[1])),
        [SMEM, ANY],
        "weight_part",
        1,
        4 * size * whole.shape[1],
        scratch=[pltpu.SemaphoreType.DMA],
        limit=PART_LIMIT,
    )(pipe, whole)


def hold_kernel(pipes, pipe_ref, w_in, w_out, *refs):
    in_held, out_held, out_part, out_rest, sems = refs[-5:]
    size = out_part.shape[0]
    at = pl.multiple_of(pipe_ref[0] * size, size)
    copies = [
        pltpu.make_async_copy(source, target, sems.at[i])
        for i, (source, target) in enumerate(
            (
                (w_in, in_held),
                (w_out, out_held),
                (w_out.at[pl.ds(at, size)], out_part),
                (w_out.at[pipes * size :], out_rest),
            )
        )
    ]
    for copy in copies:
        copy.start()
    for copy in copies:
        copy.wait()


def hold(pipe, w_in, w_out, pipes, after):
    units, width = w_out.shape
    size = units * 7 // 12 // pipes // 16 * 16
    return call(
        functools.partial(hold_kernel, pipes),
        [
            struct(w_in.shape),
            struct(w_out.shape),
            struct((size, width)),
            struct((units - pipes * size, width)),
        ],
        [SMEM, ANY, ANY] + [ANY] * len(after),
        "hold_weights",
        1,
        8 * units * width,
        scratch=[pltpu.SemaphoreType.DMA((4,))],
    )(pipe, w_in, w_out, *after)


def up_kernel(own_in, z_in, w_own, w_pair, out_ref):
    entries = jnp.concatenate([own_in[...], z_in[...]], axis=0)
    weights = jnp.concatenate([w_own[...], w_pair[...]], axis=1)
    raw = jnp.dot(entries, weights, preferred_element_type=jnp.float32)
    out_ref[...] = jnp.maximum(raw, 0.0).astype(jnp.bfloat16)


def up(own, z, w_in):
    rows, width = own.shape
    units = w_in[0].shape[1]
    return call(
        up_kernel,
        struct((2 * rows, 2 * units)),
        [VMEM] * 4,
        "expert_up",
        8 * rows * width * units,
        4 * units * width,
    )(own, z, *w_in)


def up_y_kernel(pipes, halves, *refs):
    pipe = refs[0][0]
    act_ref, own_in, z_in = refs[1:4]
    count = pipes * halves
    y_parts = refs[4 : 4 + count]
    pair_parts = refs[4 + count : 4 + 2 * count]
    out_ref, entries = refs[-2:]
    rows, width = own_in.shape
    units = act_ref.shape[1]
    entries[:rows] = own_in[...]
    entries[rows:] = z_in[...]
    out_ref[:, :units] = act_ref[...]
    depth = width // count
    raw = jnp.zeros(act_ref.shape, jnp.float32)
    for i in range(count):
        half, shift = divmod(i, pipes)
        at = place(pipes, shift, pipe, halves * depth) + half * depth
        part = entries[:, pl.ds(pl.multiple_of(at, depth), depth)]
        weights = jnp.concatenate([y_parts[i][...], pair_parts[i][...]], axis=1)
        raw = raw + jnp.dot(part, weights, preferred_element_type=jnp.float32)
    out_ref[:, units:] = jnp.maximum(raw, 0.0).astype(jnp.bfloat16)


def up_y(pipe, act, own, z, y_parts, pair_parts, pipes, after=()):
    rows, width = own.shape
    units = y_parts[0].shape[1]
    count = len(y_parts)
    return call(
        functools.partial(up_y_kernel, pipes, count // pipes),
        struct((2 * rows, 4 * units)),
        [SMEM] + [VMEM] * (3 + 2 * count) + [ANY] * len(after),
        "expert_up_y",
        8 * rows * width * units,
        4 * units * width,
        scratch=[pltpu.VMEM((2 * rows, width), jnp.bfloat16)],
    )(pipe, act, own, z, *y_parts, *pair_parts, *after)


def down_kernel(pipes, first, *refs):
    pipe = refs[0][0]
    act_ref, w_own, w_pair = refs[1:4]
    y_parts, refs = refs[4 : 4 + pipes], refs[4 + pipes :]
    pair_parts, refs = refs[:pipes], refs[pipes:]
    y_rest, pair_rest = refs[:2]
    own_ref, z_ref, held = refs[-3:]
    rows, width = own_ref.shape
    whole = slice(first, first + width)
    units = w_own.shape[0]
    size = y_parts[0].shape[0]
    for shift in range(pipes):
        at = place(pipes, shift, pipe, size)
        held[pl.ds(at, size)] = y_parts[shift][:, whole]
        held[pl.ds(pl.multiple_of(units + at, size), size)] = pair_parts[shift][:, whole]
    held[pipes * size : units] = y_rest[:, whole]
    held[units + pipes * size :] = pair_rest[:, whole]
    step = 512
    for at in range(0, width, step):
        cols = slice(at, at + step)
        there = slice(first + at, first + at + step)
        weights = jnp.concatenate([w_own[:, there], w_pair[:, there], held[:, cols]], axis=0)
        part = jnp.dot(act_ref[...], weights, preferred_element_type=jnp.float32)
        part = part.astype(jnp.bfloat16)
        own_ref[:, cols] = part[:rows]
        z_ref[:, cols] = part[rows:]


def down(pipe, act, w_out, y_parts, pair_parts, rests, first, width, after=()):
    rows = act.shape[0] // 2
    units = w_out[0].shape[0]
    pipes = len(y_parts)
    return call(
        functools.partial(down_kernel, pipes, first),
        [struct((rows, width))] * 2,
        [SMEM] + [VMEM] * (5 + 2 * pipes) + [ANY] * len(after),
        "expert_down",
        16 * rows * width * units,
        8 * units * width,
        scratch=[pltpu.VMEM((2 * units, width), jnp.bfloat16)],
    )(pipe, act, *w_out, *y_parts, *pair_parts, *rests, *after)


def total_kernel(held, own_ref, z_ref, *refs):
    refs[held][...] = (own_ref[...].astype(jnp.float32) + z_ref[...].astype(jnp.float32)).astype(
        jnp.bfloat16
    )


def total(own, z, held):
    outs = [struct(own.shape)] + [struct(value.shape) for value in held]
    return call(
        functools.partial(total_kernel, len(held)),
        outs,
        [VMEM] * 2 + [ANY] * len(held),
        "far_total",
        own.size,
        6 * own.size,
        out_specs=[VMEM] + [ANY] * len(held),
        aliases={2 + i: 1 + i for i in range(len(held))},
    )(own, z, *held)


def finish_kernel(groups, cap, *refs):
    hidden_ref, gate_ref, flat_ref = refs[:3]
    own_ref, z_ref = refs[3:5]
    back_refs = refs[5:-1]
    out_ref = refs[-1]
    tokens, width = hidden_ref.shape
    slots = lax.broadcasted_iota(jnp.int32, (tokens, groups * cap), 1)
    picker = (slots == flat_ref[...]).astype(jnp.float32).astype(jnp.bfloat16)
    step = 512
    for at in range(0, width, step):
        cols = slice(at, at + step)
        near = (own_ref[:, cols].astype(jnp.float32) + z_ref[:, cols].astype(jnp.float32)).astype(
            jnp.bfloat16
        )
        side, inner = divmod(at, width // 2)
        backs = [r[:, inner : inner + step] for r in back_refs[side::2]]
        found = jnp.concatenate([near, *backs], axis=0)
        picked = jnp.dot(picker, found, preferred_element_type=jnp.float32)
        out_ref[:, cols] = (hidden_ref[:, cols] + gate_ref[...] * picked).astype(jnp.bfloat16)


def finish(hidden, gate, flat, sums, backs, groups, cap):
    tokens, width = hidden.shape
    operands = [hidden, gate, flat, *sums, *backs]
    return call(
        functools.partial(finish_kernel, groups, cap),
        struct((tokens, width)),
        [VMEM] * len(operands),
        "finish",
        4 * tokens * cap * groups * width,
        16 * tokens * width,
    )(*operands)


def body(state, query, enc_kv, gain, w_in, w_out, expert_id, slot, gate):
    tokens, width = state.shape[2:]
    devices = lax.axis_size("expert")
    pipes = lax.axis_size("pipe")
    groups = devices // WSPLIT
    cap = 3 * tokens // (2 * groups)

    def across(value, bit):
        return lax.ppermute(value, "expert", [(i, i ^ bit) for i in range(devices)])

    def groups_on(value, count):
        shift = count * WSPLIT
        return lax.ppermute(value, "expert", [(i, (i + shift) % devices) for i in range(devices)])

    def along(value):
        perms = [[(i, (i + shift) % pipes) for i in range(pipes)] for shift in range(1, pipes)]
        return [value] + [lax.ppermute(value, "pipe", perm) for perm in perms]

    def paired(parts):
        return [across(value, 1) for value in parts]

    pipe = lax.axis_index("pipe").astype(jnp.int32)
    w_in_pair, w_out_pair = across(w_in, 1), across(w_out, 1)
    pipe = pipe.reshape(1)
    depth = width // pipes
    in_y = lax.dynamic_slice_in_dim(w_in, pipe[0] * depth, depth // 2, 0)
    in_late = cut_part(pipe, w_in, depth, depth // 2, depth // 2)
    kv = jnp.transpose(enc_kv[0], (1, 0, 2)).reshape(-1, width)
    (kv,) = after_all([kv], [in_y])
    kv_pieces = [kv]
    for shift in range(1, pipes):
        perm = [(i, (i + shift) % pipes) for i in range(pipes)]
        kv_pieces.append(lax.ppermute(kv, "pipe", perm))
    in_y = across(in_y, 2)
    in_late = across(*after_all([in_late], kv_pieces[1:2]), 2)

    group = (lax.axis_index("expert") // WSPLIT).astype(jnp.int32).reshape(1)
    staged = stage(
        group,
        state[0, 0],
        query[0, 0],
        gain.reshape(1, width),
        expert_id[0],
        slot[0],
        gate[0],
        groups,
        cap,
    )
    flat, gates = staged[4:]
    hidden, near, *packed = attend(
        *staged[:4], kv_pieces, groups, cap, after=[w_in_pair, w_out_pair]
    )
    far = [groups_on(block, count) for count, block in enumerate(packed, 1)]
    far = jnp.concatenate(far, axis=0) if len(far) > 1 else far[0]

    w_in_held, w_out_held, out_part, out_rest = hold(pipe, w_in, w_out, pipes, [near])
    in_first = along(*after_all([in_y], [out_part], FIRST_WEIGHT))
    in_last = after_all([in_late], [in_first[0]])
    out_part, out_rest = after_all([out_part, out_rest], in_last)
    in_last = along(*in_last)
    out_y, rest_y = across(out_part, 2), across(out_rest, 2)

    near_z = across(near, 4)
    far = [far]
    for step in range(CROSS_STEPS):
        far = after_all(far, [] if step else [near_z], CROSS_WEIGHT)
    (far,) = far
    far_z = [across(far, 4)]
    in_sent = in_last[-1]
    in_parts = after_all([*in_first, *in_last], far_z)
    for _ in range(FAR_STEPS):
        far_z = after_all(far_z, [], FAR_WEIGHT)
    (far_z,) = far_z

    in_pair = paired(in_parts)

    def experts_up(own, z, after=()):
        act = up(own, z, [w_in_held, w_in_pair])
        return up_y(pipe, act, own, z, in_parts, in_pair, pipes, after)

    far_act = experts_up(far, far_z)
    out_parts = along(*after_all([out_y], [in_sent]))
    out_pair = paired(out_parts[:1])
    *out_parts[1:], rest_y = after_all([*out_parts[1:], rest_y], [far_act, *out_pair])
    out_pair += paired(out_parts[1:])
    rests = [rest_y, across(rest_y, 1)]

    def experts_down(act, first, size, after=()):
        return down(
            pipe, act, [w_out_held, w_out_pair], out_parts, out_pair, rests, first, size, after
        )

    half = width // 2
    far_a, sent_a = experts_down(far_act, 0, half)
    far_b, sent_b = experts_down(far_act, half, half, [far_a])
    near_act = experts_up(near, near_z, [far_b])
    (sent_b,) = after_all([sent_b], [near_act])
    near_own, near_sent = experts_down(near_act, 0, width)
    (sum_a,) = total(far_a, across(sent_a, 4), [])
    sum_b, near_sent = total(far_b, across(sent_b, 4), [near_sent])
    backs = [
        groups_on(side[(count - 1) * cap : count * cap], groups - count)
        for count in range(1, groups)
        for side in (sum_a, sum_b)
    ]
    backs[::2] = after_all(backs[::2], [], SUM_WEIGHT)
    backs[::2] = after_all(backs[::2], [], BACK_WEIGHT)
    near_sums = [near_own, across(near_sent, 4)]
    output = finish(hidden, gates, flat, near_sums, backs, groups, cap)
    return output.reshape(1, 1, tokens, width)


def solution(mesh):
    return jax.shard_map(
        body,
        mesh=mesh,
        in_specs=(
            P("expert", "pipe", None, None),
            P("expert", "pipe", None, None),
            P("expert", "pipe", None, None),
            P(),
            P(None, "expert"),
            P("expert", None),
            P("expert", "pipe", None),
            P("expert", "pipe", None),
            P("expert", "pipe", None),
        ),
        out_specs=P("expert", "pipe", None, None),
        check_vma=False,
    )
```

```python
import functools
import math

import jax
import jax.numpy as jnp
from jax import lax
from jax.experimental import pallas as pl
from jax.experimental.pallas import tpu as pltpu
from jax.sharding import PartitionSpec as P

HEADS = 16
HD = 128
WSPLIT = 8
EPS = 1e-06
FAR_WEIGHT = 3_000_000_000
FAR_STEPS = 4
CROSS_STEPS = 1
CROSS_WEIGHT = 3_000_000_000
FIRST_WEIGHT = 2_000_000_000
SUM_WEIGHT = 1_000_000_000
BACK_WEIGHT = 3_000_000_000
VMEM_LIMIT = 32 * 1024 * 1024
PART_LIMIT = 60 * 1024 * 1024

VMEM = pl.BlockSpec(memory_space=pltpu.VMEM)
SMEM = pl.BlockSpec(memory_space=pltpu.SMEM)
ANY = pl.BlockSpec(memory_space=pl.ANY)


def struct(shape, dtype=jnp.bfloat16):
    return jax.ShapeDtypeStruct(shape, dtype)


def call(
    kernel, outs, in_specs, name, flops, moved, scratch=(), out_specs=None, aliases=None, limit=VMEM_LIMIT
):
    return pl.pallas_call(
        kernel,
        out_shape=outs,
        in_specs=in_specs,
        out_specs=out_specs or jax.tree.map(lambda _: VMEM, outs),
        scratch_shapes=list(scratch),
        input_output_aliases=aliases or {},
        compiler_params=pltpu.CompilerParams(vmem_limit_bytes=limit),
        cost_estimate=pl.CostEstimate(flops=flops, bytes_accessed=moved, transcendentals=0),
        name=name,
    )


def as_column(row):
    count = row.shape[1]
    down = lax.broadcasted_iota(jnp.int32, (count, count), 0)
    along = lax.broadcasted_iota(jnp.int32, (count, count), 1)
    return jnp.sum(jnp.where(down == along, row, jnp.zeros_like(row)), axis=1, keepdims=True)


def stage_kernel(groups, cap, *refs):
    group_ref, state_in, query_in, gain_in, expert_ref, slot_ref, gate_ref = refs[:7]
    state_out, query_out, gain_out, flat_row, flat_column, gate_column = refs[7:]
    state_out[...] = state_in[...]
    query_out[...] = query_in[...]
    gain_out[...] = gain_in[...]
    offset = expert_ref[...] - group_ref[0]
    offset = jnp.where(offset < 0, offset + groups, offset)
    slot = slot_ref[...]
    flat = jnp.where(slot >= 0, offset * cap + slot, -1)
    flat_row[...] = flat
    flat_column[...] = as_column(flat)
    gate_column[...] = as_column(gate_ref[...])


def stage(group, state, query, gain, expert_id, slot, gate, groups, cap):
    tokens, width = state.shape
    outs = [
        struct((tokens, width)),
        struct((tokens, width)),
        struct((1, width), jnp.float32),
        struct((1, tokens), jnp.int32),
        struct((tokens, 1), jnp.int32),
        struct((tokens, 1), jnp.float32),
    ]
    return call(
        functools.partial(stage_kernel, groups, cap),
        outs,
        [SMEM] + [VMEM] * 6,
        "stage",
        tokens * tokens,
        8 * tokens * width,
    )(group, state, query, gain, expert_id, slot, gate)


def gate_kernel(*refs):
    pass


def after_all(values, others, weight=1):
    return call(
        gate_kernel,
        [struct(value.shape) for value in values],
        [ANY] * (len(values) + len(others)),
        "hand_on",
        weight,
        1,
        out_specs=[ANY] * len(values),
        aliases={i: i for i in range(len(values))},
    )(*values, *others)


def attend_kernel(pieces, groups, cap, *refs):
    state_ref, query_ref, gain_ref, flat_ref = refs[:4]
    kv_refs = refs[4 : 4 + pieces]
    hidden_ref = refs[-1 - groups]
    packed_refs = refs[-groups:]
    tokens, width = state_ref.shape
    local = kv_refs[0].shape[0] // 2
    scale = 1.0 / math.sqrt(HD)
    squares = jnp.zeros((tokens, HD), jnp.float32)
    for head in range(HEADS):
        cols = slice(head * HD, (head + 1) * HD)
        keys = jnp.concatenate([r[:local, cols] for r in kv_refs], axis=0)
        values = jnp.concatenate([r[local:, cols] for r in kv_refs], axis=0)
        scores = (
            lax.dot_general(
                query_ref[:, cols],
                keys,
                (((1,), (1,)), ((), ())),
                preferred_element_type=jnp.float32,
            )
            * scale
        )
        raised = jnp.exp(scores - jnp.max(scores, axis=1, keepdims=True))
        total = jnp.sum(raised, axis=1, keepdims=True)
        mixed = jnp.dot(raised.astype(jnp.bfloat16), values, preferred_element_type=jnp.float32)
        hidden = state_ref[:, cols].astype(jnp.float32) + mixed / total
        hidden_ref[:, cols] = hidden
        squares = squares + hidden * hidden
    mean_square = jnp.sum(squares, axis=1, keepdims=True) * (1.0 / width)
    inverse = lax.rsqrt(mean_square + EPS)
    rows = lax.broadcasted_iota(jnp.int32, (groups * cap, tokens), 0)
    selector = (rows == flat_ref[...]).astype(jnp.float32).astype(jnp.bfloat16)
    step = 512
    for at in range(0, width, step):
        cols = slice(at, at + step)
        normed = (hidden_ref[:, cols] * inverse * gain_ref[:, cols]).astype(jnp.bfloat16)
        packed = jnp.dot(selector, normed, preferred_element_type=jnp.float32).astype(jnp.bfloat16)
        for group in range(groups):
            packed_refs[group][:, cols] = packed[group * cap : (group + 1) * cap]


def attend(state, query, gain, flat, kv_pieces, groups, cap, after):
    tokens, width = state.shape
    outs = [struct((tokens, width), jnp.float32)] + [struct((cap, width))] * groups
    pieces = len(kv_pieces)
    return call(
        functools.partial(attend_kernel, pieces, groups, cap),
        outs,
        [VMEM] * (4 + pieces) + [ANY] * len(after),
        "attend",
        4 * tokens * pieces * kv_pieces[0].shape[0] * width,
        12 * tokens * width,
    )(state, query, gain, flat, *kv_pieces, *after)


def place(pipes, shift, pipe, size):
    at = pipe - shift
    at = jnp.where(at < 0, at + pipes, at)
    return pl.multiple_of(at * size, size)


def part_kernel(stride, first, pipe_ref, whole, part, sem):
    size = part.shape[0]
    at = pl.multiple_of(pipe_ref[0] * stride + first, size)
    copy = pltpu.make_async_copy(whole.at[pl.ds(at, size)], part, sem)
    copy.start()
    copy.wait()


def cut_part(pipe, whole, stride, first, size):
    return call(
        functools.partial(part_kernel, stride, first),
        struct((size, whole.shape[1])),
        [SMEM, ANY],
        "weight_part",
        1,
        4 * size * whole.shape[1],
        scratch=[pltpu.SemaphoreType.DMA],
        limit=PART_LIMIT,
    )(pipe, whole)


def hold_kernel(pipes, pipe_ref, w_in, w_out, *refs):
    in_held, out_held, out_part, out_rest, sems = refs[-5:]
    size = out_part.shape[0]
    at = pl.multiple_of(pipe_ref[0] * size, size)
    copies = [
        pltpu.make_async_copy(source, target, sems.at[i])
        for i, (source, target) in enumerate(
            (
                (w_in, in_held),
                (w_out, out_held),
                (w_out.at[pl.ds(at, size)], out_part),
                (w_out.at[pipes * size :], out_rest),
            )
        )
    ]
    for copy in copies:
        copy.start()
    for copy in copies:
        copy.wait()


def hold(pipe, w_in, w_out, pipes, after):
    units, width = w_out.shape
    size = units * 7 // 12 // pipes // 16 * 16
    return call(
        functools.partial(hold_kernel, pipes),
        [
            struct(w_in.shape),
            struct(w_out.shape),
            struct((size, width)),
            struct((units - pipes * size, width)),
        ],
        [SMEM, ANY, ANY] + [ANY] * len(after),
        "hold_weights",
        1,
        8 * units * width,
        scratch=[pltpu.SemaphoreType.DMA((4,))],
    )(pipe, w_in, w_out, *after)


def up_kernel(own_in, z_in, w_own, w_pair, out_ref):
    entries = jnp.concatenate([own_in[...], z_in[...]], axis=0)
    weights = jnp.concatenate([w_own[...], w_pair[...]], axis=1)
    raw = jnp.dot(entries, weights, preferred_element_type=jnp.float32)
    out_ref[...] = jnp.maximum(raw, 0.0).astype(jnp.bfloat16)


def up(own, z, w_in):
    rows, width = own.shape
    units = w_in[0].shape[1]
    return call(
        up_kernel,
        struct((2 * rows, 2 * units)),
        [VMEM] * 4,
        "expert_up",
        8 * rows * width * units,
        4 * units * width,
    )(own, z, *w_in)


def up_y_kernel(pipes, halves, *refs):
    pipe = refs[0][0]
    act_ref, own_in, z_in = refs[1:4]
    count = pipes * halves
    y_parts = refs[4 : 4 + count]
    pair_parts = refs[4 + count : 4 + 2 * count]
    out_ref, entries = refs[-2:]
    rows, width = own_in.shape
    units = act_ref.shape[1]
    entries[:rows] = own_in[...]
    entries[rows:] = z_in[...]
    out_ref[:, :units] = act_ref[...]
    depth = width // count
    raw = jnp.zeros(act_ref.shape, jnp.float32)
    for i in range(count):
        half, shift = divmod(i, pipes)
        at = place(pipes, shift, pipe, halves * depth) + half * depth
        part = entries[:, pl.ds(pl.multiple_of(at, depth), depth)]
        weights = jnp.concatenate([y_parts[i][...], pair_parts[i][...]], axis=1)
        raw = raw + jnp.dot(part, weights, preferred_element_type=jnp.float32)
    out_ref[:, units:] = jnp.maximum(raw, 0.0).astype(jnp.bfloat16)


def up_y(pipe, act, own, z, y_parts, pair_parts, pipes, after=()):
    rows, width = own.shape
    units = y_parts[0].shape[1]
    count = len(y_parts)
    return call(
        functools.partial(up_y_kernel, pipes, count // pipes),
        struct((2 * rows, 4 * units)),
        [SMEM] + [VMEM] * (3 + 2 * count) + [ANY] * len(after),
        "expert_up_y",
        8 * rows * width * units,
        4 * units * width,
        scratch=[pltpu.VMEM((2 * rows, width), jnp.bfloat16)],
    )(pipe, act, own, z, *y_parts, *pair_parts, *after)


def down_kernel(pipes, first, *refs):
    pipe = refs[0][0]
    act_ref, w_own, w_pair = refs[1:4]
    y_parts, refs = refs[4 : 4 + pipes], refs[4 + pipes :]
    pair_parts, refs = refs[:pipes], refs[pipes:]
    y_rest, pair_rest = refs[:2]
    own_ref, z_ref, held = refs[-3:]
    rows, width = own_ref.shape
    whole = slice(first, first + width)
    units = w_own.shape[0]
    size = y_parts[0].shape[0]
    for shift in range(pipes):
        at = place(pipes, shift, pipe, size)
        held[pl.ds(at, size)] = y_parts[shift][:, whole]
        held[pl.ds(pl.multiple_of(units + at, size), size)] = pair_parts[shift][:, whole]
    held[pipes * size : units] = y_rest[:, whole]
    held[units + pipes * size :] = pair_rest[:, whole]
    step = 512
    for at in range(0, width, step):
        cols = slice(at, at + step)
        there = slice(first + at, first + at + step)
        weights = jnp.concatenate([w_own[:, there], w_pair[:, there], held[:, cols]], axis=0)
        part = jnp.dot(act_ref[...], weights, preferred_element_type=jnp.float32)
        part = part.astype(jnp.bfloat16)
        own_ref[:, cols] = part[:rows]
        z_ref[:, cols] = part[rows:]


def down(pipe, act, w_out, y_parts, pair_parts, rests, first, width, after=()):
    rows = act.shape[0] // 2
    units = w_out[0].shape[0]
    pipes = len(y_parts)
    return call(
        functools.partial(down_kernel, pipes, first),
        [struct((rows, width))] * 2,
        [SMEM] + [VMEM] * (5 + 2 * pipes) + [ANY] * len(after),
        "expert_down",
        16 * rows * width * units,
        8 * units * width,
        scratch=[pltpu.VMEM((2 * units, width), jnp.bfloat16)],
    )(pipe, act, *w_out, *y_parts, *pair_parts, *rests, *after)


def total_kernel(held, own_ref, z_ref, *refs):
    refs[held][...] = (own_ref[...].astype(jnp.float32) + z_ref[...].astype(jnp.float32)).astype(
        jnp.bfloat16
    )


def total(own, z, held):
    outs = [struct(own.shape)] + [struct(value.shape) for value in held]
    return call(
        functools.partial(total_kernel, len(held)),
        outs,
        [VMEM] * 2 + [ANY] * len(held),
        "far_total",
        own.size,
        6 * own.size,
        out_specs=[VMEM] + [ANY] * len(held),
        aliases={2 + i: 1 + i for i in range(len(held))},
    )(own, z, *held)


def finish_kernel(groups, cap, *refs):
    hidden_ref, gate_ref, flat_ref = refs[:3]
    own_ref, z_ref = refs[3:5]
    back_refs = refs[5:-1]
    out_ref = refs[-1]
    tokens, width = hidden_ref.shape
    slots = lax.broadcasted_iota(jnp.int32, (tokens, groups * cap), 1)
    picker = (slots == flat_ref[...]).astype(jnp.float32).astype(jnp.bfloat16)
    step = 512
    for at in range(0, width, step):
        cols = slice(at, at + step)
        near = (own_ref[:, cols].astype(jnp.float32) + z_ref[:, cols].astype(jnp.float32)).astype(
            jnp.bfloat16
        )
        cut = back_refs[0].shape[1]
        side, inner = (0, at) if at < cut else (1, at - cut)
        backs = [r[:, inner : inner + step] for r in back_refs[side::2]]
        found = jnp.concatenate([near, *backs], axis=0)
        picked = jnp.dot(picker, found, preferred_element_type=jnp.float32)
        out_ref[:, cols] = (hidden_ref[:, cols] + gate_ref[...] * picked).astype(jnp.bfloat16)


def finish(hidden, gate, flat, sums, backs, groups, cap):
    tokens, width = hidden.shape
    operands = [hidden, gate, flat, *sums, *backs]
    return call(
        functools.partial(finish_kernel, groups, cap),
        struct((tokens, width)),
        [VMEM] * len(operands),
        "finish",
        4 * tokens * cap * groups * width,
        16 * tokens * width,
    )(*operands)


def body(state, query, enc_kv, gain, w_in, w_out, expert_id, slot, gate):
    tokens, width = state.shape[2:]
    devices = lax.axis_size("expert")
    pipes = lax.axis_size("pipe")
    groups = devices // WSPLIT
    cap = 3 * tokens // (2 * groups)

    def across(value, bit):
        return lax.ppermute(value, "expert", [(i, i ^ bit) for i in range(devices)])

    def groups_on(value, count):
        shift = count * WSPLIT
        return lax.ppermute(value, "expert", [(i, (i + shift) % devices) for i in range(devices)])

    def along(value):
        perms = [[(i, (i + shift) % pipes) for i in range(pipes)] for shift in range(1, pipes)]
        return [value] + [lax.ppermute(value, "pipe", perm) for perm in perms]

    def paired(parts):
        return [across(value, 1) for value in parts]

    pipe = lax.axis_index("pipe").astype(jnp.int32)
    w_in_pair, w_out_pair = across(w_in, 1), across(w_out, 1)
    pipe = pipe.reshape(1)
    depth = width // pipes
    in_y, in_late = (cut_part(pipe, w_in, depth, at, depth // 2) for at in (0, depth // 2))
    kv = jnp.transpose(enc_kv[0], (1, 0, 2)).reshape(-1, width)
    (kv,) = after_all([kv], [in_y])
    kv_pieces = [kv]
    for shift in range(1, pipes):
        perm = [(i, (i + shift) % pipes) for i in range(pipes)]
        kv_pieces.append(lax.ppermute(kv, "pipe", perm))
    in_y = across(in_y, 2)
    in_late = across(*after_all([in_late], kv_pieces[1:2]), 2)

    group = (lax.axis_index("expert") // WSPLIT).astype(jnp.int32).reshape(1)
    staged = stage(
        group,
        state[0, 0],
        query[0, 0],
        gain.reshape(1, width),
        expert_id[0],
        slot[0],
        gate[0],
        groups,
        cap,
    )
    flat, gates = staged[4:]
    hidden, near, *packed = attend(
        *staged[:4], kv_pieces, groups, cap, after=[w_in_pair, w_out_pair]
    )
    far = [groups_on(block, count) for count, block in enumerate(packed, 1)]
    far = jnp.concatenate(far, axis=0) if len(far) > 1 else far[0]

    w_in_held, w_out_held, out_part, out_rest = hold(pipe, w_in, w_out, pipes, [near])
    in_first = along(*after_all([in_y], [out_part]))
    in_last = after_all([in_late], [in_first[0]])
    out_part, out_rest = after_all([out_part, out_rest], in_last)
    in_last = along(*in_last)
    out_y, rest_y = across(out_part, 2), across(out_rest, 2)

    near_z = across(near, 4)
    far = [far]
    for step in range(CROSS_STEPS):
        far = after_all(far, [] if step else [near_z], CROSS_WEIGHT)
    (far,) = far
    far_z = [across(far, 4)]
    in_sent = in_last[-1]
    in_parts = after_all([*in_first, *in_last], far_z)
    for _ in range(FAR_STEPS):
        far_z = after_all(far_z, [], FAR_WEIGHT)
    (far_z,) = far_z

    in_pair = paired(in_parts)

    def experts_up(own, z, after=()):
        act = up(own, z, [w_in_held, w_in_pair])
        return up_y(pipe, act, own, z, in_parts, in_pair, pipes, after)

    far_act = experts_up(far, far_z)
    out_parts = along(*after_all([out_y], [in_sent]))
    out_pair = paired(out_parts[:1])
    *out_parts[1:], rest_y = after_all([*out_parts[1:], rest_y], [far_act, *out_pair])
    out_pair += paired(out_parts[1:])
    rests = [rest_y, across(rest_y, 1)]

    def experts_down(act, first, size, after=()):
        return down(
            pipe, act, [w_out_held, w_out_pair], out_parts, out_pair, rests, first, size, after
        )

    cut = width // 4
    far_a, sent_a = experts_down(far_act, 0, cut)
    far_b, sent_b = experts_down(far_act, cut, width - cut, [far_a])
    near_act = experts_up(near, near_z, [far_b])
    (sent_b,) = after_all([sent_b], [near_act])
    near_own, near_sent = experts_down(near_act, 0, width)
    (sum_a,) = total(far_a, *after_all([across(sent_a, 4)], [], FIRST_WEIGHT), [])
    sum_b, near_sent = total(far_b, across(sent_b, 4), [near_sent])
    backs = [
        groups_on(side[(count - 1) * cap : count * cap], groups - count)
        for count in range(1, groups)
        for side in (sum_a, sum_b)
    ]
    backs[::2] = after_all(backs[::2], [sum_b], SUM_WEIGHT)
    backs[::2] = after_all(backs[::2], [], BACK_WEIGHT)
    near_sums = [near_own, across(near_sent, 4)]
    output = finish(hidden, gates, flat, near_sums, backs, groups, cap)
    return output.reshape(1, 1, tokens, width)


def solution(mesh):
    return jax.shard_map(
        body,
        mesh=mesh,
        in_specs=(
            P("expert", "pipe", None, None),
            P("expert", "pipe", None, None),
            P("expert", "pipe", None, None),
            P(),
            P(None, "expert"),
            P("expert", None),
            P("expert", "pipe", None),
            P("expert", "pipe", None),
            P("expert", "pipe", None),
        ),
        out_specs=P("expert", "pipe", None, None),
        check_vma=False,
    )
```

```python
import functools
import math

import jax
import jax.numpy as jnp
from jax import lax
from jax.experimental import pallas as pl
from jax.experimental.pallas import tpu as pltpu
from jax.sharding import PartitionSpec as P

HEADS = 16
HD = 128
WSPLIT = 8
EPS = 1e-06
FAR_WEIGHT = 3_000_000_000
FAR_STEPS = 4
CROSS_STEPS = 1
CROSS_WEIGHT = 3_000_000_000
SUM_WEIGHT = 1_000_000_000
BACK_WEIGHT = 3_000_000_000
VMEM_LIMIT = 32 * 1024 * 1024
PART_LIMIT = 60 * 1024 * 1024

VMEM = pl.BlockSpec(memory_space=pltpu.VMEM)
SMEM = pl.BlockSpec(memory_space=pltpu.SMEM)
ANY = pl.BlockSpec(memory_space=pl.ANY)


def struct(shape, dtype=jnp.bfloat16):
    return jax.ShapeDtypeStruct(shape, dtype)


def call(
    kernel, outs, in_specs, name, flops, moved, scratch=(), out_specs=None, aliases=None, limit=VMEM_LIMIT
):
    return pl.pallas_call(
        kernel,
        out_shape=outs,
        in_specs=in_specs,
        out_specs=out_specs or jax.tree.map(lambda _: VMEM, outs),
        scratch_shapes=list(scratch),
        input_output_aliases=aliases or {},
        compiler_params=pltpu.CompilerParams(vmem_limit_bytes=limit),
        cost_estimate=pl.CostEstimate(flops=flops, bytes_accessed=moved, transcendentals=0),
        name=name,
    )


def as_column(row):
    count = row.shape[1]
    down = lax.broadcasted_iota(jnp.int32, (count, count), 0)
    along = lax.broadcasted_iota(jnp.int32, (count, count), 1)
    return jnp.sum(jnp.where(down == along, row, jnp.zeros_like(row)), axis=1, keepdims=True)


def stage_kernel(groups, cap, *refs):
    group_ref, state_in, query_in, gain_in, expert_ref, slot_ref, gate_ref = refs[:7]
    state_out, query_out, gain_out, flat_row, flat_column, gate_column = refs[7:]
    state_out[...] = state_in[...]
    query_out[...] = query_in[...]
    gain_out[...] = gain_in[...]
    offset = expert_ref[...] - group_ref[0]
    offset = jnp.where(offset < 0, offset + groups, offset)
    slot = slot_ref[...]
    flat = jnp.where(slot >= 0, offset * cap + slot, -1)
    flat_row[...] = flat
    flat_column[...] = as_column(flat)
    gate_column[...] = as_column(gate_ref[...])


def stage(group, state, query, gain, expert_id, slot, gate, groups, cap):
    tokens, width = state.shape
    outs = [
        struct((tokens, width)),
        struct((tokens, width)),
        struct((1, width), jnp.float32),
        struct((1, tokens), jnp.int32),
        struct((tokens, 1), jnp.int32),
        struct((tokens, 1), jnp.float32),
    ]
    return call(
        functools.partial(stage_kernel, groups, cap),
        outs,
        [SMEM] + [VMEM] * 6,
        "stage",
        tokens * tokens,
        8 * tokens * width,
    )(group, state, query, gain, expert_id, slot, gate)


def gate_kernel(*refs):
    pass


def after_all(values, others, weight=1):
    return call(
        gate_kernel,
        [struct(value.shape) for value in values],
        [ANY] * (len(values) + len(others)),
        "hand_on",
        weight,
        1,
        out_specs=[ANY] * len(values),
        aliases={i: i for i in range(len(values))},
    )(*values, *others)


def attend_kernel(pieces, groups, cap, *refs):
    state_ref, query_ref, gain_ref, flat_ref = refs[:4]
    kv_refs = refs[4 : 4 + pieces]
    hidden_ref = refs[-1 - groups]
    packed_refs = refs[-groups:]
    tokens, width = state_ref.shape
    local = kv_refs[0].shape[0] // 2
    scale = 1.0 / math.sqrt(HD)
    squares = jnp.zeros((tokens, HD), jnp.float32)
    for head in range(HEADS):
        cols = slice(head * HD, (head + 1) * HD)
        keys = jnp.concatenate([r[:local, cols] for r in kv_refs], axis=0)
        values = jnp.concatenate([r[local:, cols] for r in kv_refs], axis=0)
        scores = (
            lax.dot_general(
                query_ref[:, cols],
                keys,
                (((1,), (1,)), ((), ())),
                preferred_element_type=jnp.float32,
            )
            * scale
        )
        raised = jnp.exp(scores - jnp.max(scores, axis=1, keepdims=True))
        total = jnp.sum(raised, axis=1, keepdims=True)
        mixed = jnp.dot(raised.astype(jnp.bfloat16), values, preferred_element_type=jnp.float32)
        hidden = state_ref[:, cols].astype(jnp.float32) + mixed / total
        hidden_ref[:, cols] = hidden
        squares = squares + hidden * hidden
    mean_square = jnp.sum(squares, axis=1, keepdims=True) * (1.0 / width)
    inverse = lax.rsqrt(mean_square + EPS)
    rows = lax.broadcasted_iota(jnp.int32, (groups * cap, tokens), 0)
    selector = (rows == flat_ref[...]).astype(jnp.float32).astype(jnp.bfloat16)
    step = 512
    for at in range(0, width, step):
        cols = slice(at, at + step)
        normed = (hidden_ref[:, cols] * inverse * gain_ref[:, cols]).astype(jnp.bfloat16)
        packed = jnp.dot(selector, normed, preferred_element_type=jnp.float32).astype(jnp.bfloat16)
        for group in range(groups):
            packed_refs[group][:, cols] = packed[group * cap : (group + 1) * cap]


def attend(state, query, gain, flat, kv_pieces, groups, cap, after):
    tokens, width = state.shape
    outs = [struct((tokens, width), jnp.float32)] + [struct((cap, width))] * groups
    pieces = len(kv_pieces)
    return call(
        functools.partial(attend_kernel, pieces, groups, cap),
        outs,
        [VMEM] * (4 + pieces) + [ANY] * len(after),
        "attend",
        4 * tokens * pieces * kv_pieces[0].shape[0] * width,
        12 * tokens * width,
    )(state, query, gain, flat, *kv_pieces, *after)


def place(pipes, shift, pipe, size):
    at = pipe - shift
    at = jnp.where(at < 0, at + pipes, at)
    return pl.multiple_of(at * size, size)


def part_kernel(stride, first, pipe_ref, whole, part, sem):
    size = part.shape[0]
    at = pl.multiple_of(pipe_ref[0] * stride + first, size)
    copy = pltpu.make_async_copy(whole.at[pl.ds(at, size)], part, sem)
    copy.start()
    copy.wait()


def cut_part(pipe, whole, stride, first, size):
    return call(
        functools.partial(part_kernel, stride, first),
        struct((size, whole.shape[1])),
        [SMEM, ANY],
        "weight_part",
        1,
        4 * size * whole.shape[1],
        scratch=[pltpu.SemaphoreType.DMA],
        limit=PART_LIMIT,
    )(pipe, whole)


def hold_kernel(pipes, pipe_ref, w_in, w_out, *refs):
    in_held, out_held, out_part, out_rest, sems = refs[-5:]
    size = out_part.shape[0]
    at = pl.multiple_of(pipe_ref[0] * size, size)
    copies = [
        pltpu.make_async_copy(source, target, sems.at[i])
        for i, (source, target) in enumerate(
            (
                (w_in, in_held),
                (w_out, out_held),
                (w_out.at[pl.ds(at, size)], out_part),
                (w_out.at[pipes * size :], out_rest),
            )
        )
    ]
    for copy in copies:
        copy.start()
    for copy in copies:
        copy.wait()


def hold(pipe, w_in, w_out, pipes, after):
    units, width = w_out.shape
    size = units * 2 // 3 // pipes // 16 * 16
    return call(
        functools.partial(hold_kernel, pipes),
        [
            struct(w_in.shape),
            struct(w_out.shape),
            struct((size, width)),
            struct((units - pipes * size, width)),
        ],
        [SMEM, ANY, ANY] + [ANY] * len(after),
        "hold_weights",
        1,
        8 * units * width,
        scratch=[pltpu.SemaphoreType.DMA((4,))],
    )(pipe, w_in, w_out, *after)


def up_kernel(own_in, z_in, w_own, w_pair, out_ref):
    entries = jnp.concatenate([own_in[...], z_in[...]], axis=0)
    weights = jnp.concatenate([w_own[...], w_pair[...]], axis=1)
    raw = jnp.dot(entries, weights, preferred_element_type=jnp.float32)
    out_ref[...] = jnp.maximum(raw, 0.0).astype(jnp.bfloat16)


def up(own, z, w_in):
    rows, width = own.shape
    units = w_in[0].shape[1]
    return call(
        up_kernel,
        struct((2 * rows, 2 * units)),
        [VMEM] * 4,
        "expert_up",
        8 * rows * width * units,
        4 * units * width,
    )(own, z, *w_in)


def up_y_kernel(pipes, halves, *refs):
    pipe = refs[0][0]
    act_ref, own_in, z_in = refs[1:4]
    count = pipes * halves
    y_parts = refs[4 : 4 + count]
    pair_parts = refs[4 + count : 4 + 2 * count]
    out_ref, entries = refs[-2:]
    rows, width = own_in.shape
    units = act_ref.shape[1]
    entries[:rows] = own_in[...]
    entries[rows:] = z_in[...]
    out_ref[:, :units] = act_ref[...]
    depth = width // count
    raw = jnp.zeros(act_ref.shape, jnp.float32)
    for i in range(count):
        half, shift = divmod(i, pipes)
        at = place(pipes, shift, pipe, halves * depth) + half * depth
        part = entries[:, pl.ds(pl.multiple_of(at, depth), depth)]
        weights = jnp.concatenate([y_parts[i][...], pair_parts[i][...]], axis=1)
        raw = raw + jnp.dot(part, weights, preferred_element_type=jnp.float32)
    out_ref[:, units:] = jnp.maximum(raw, 0.0).astype(jnp.bfloat16)


def up_y(pipe, act, own, z, y_parts, pair_parts, pipes, after=()):
    rows, width = own.shape
    units = y_parts[0].shape[1]
    count = len(y_parts)
    return call(
        functools.partial(up_y_kernel, pipes, count // pipes),
        struct((2 * rows, 4 * units)),
        [SMEM] + [VMEM] * (3 + 2 * count) + [ANY] * len(after),
        "expert_up_y",
        8 * rows * width * units,
        4 * units * width,
        scratch=[pltpu.VMEM((2 * rows, width), jnp.bfloat16)],
    )(pipe, act, own, z, *y_parts, *pair_parts, *after)


def down_kernel(pipes, first, *refs):
    pipe = refs[0][0]
    act_ref, w_own, w_pair = refs[1:4]
    y_parts, refs = refs[4 : 4 + pipes], refs[4 + pipes :]
    pair_parts, refs = refs[:pipes], refs[pipes:]
    y_rest, pair_rest = refs[:2]
    own_ref, z_ref, held = refs[-3:]
    rows, width = own_ref.shape
    whole = slice(first, first + width)
    units = w_own.shape[0]
    size = y_parts[0].shape[0]
    for shift in range(pipes):
        at = place(pipes, shift, pipe, size)
        held[pl.ds(at, size)] = y_parts[shift][:, whole]
        held[pl.ds(pl.multiple_of(units + at, size), size)] = pair_parts[shift][:, whole]
    held[pipes * size : units] = y_rest[:, whole]
    held[units + pipes * size :] = pair_rest[:, whole]
    step = 512
    for at in range(0, width, step):
        cols = slice(at, at + step)
        there = slice(first + at, first + at + step)
        weights = jnp.concatenate([w_own[:, there], w_pair[:, there], held[:, cols]], axis=0)
        part = jnp.dot(act_ref[...], weights, preferred_element_type=jnp.float32)
        part = part.astype(jnp.bfloat16)
        own_ref[:, cols] = part[:rows]
        z_ref[:, cols] = part[rows:]


def down(pipe, act, w_out, y_parts, pair_parts, rests, first, width, after=()):
    rows = act.shape[0] // 2
    units = w_out[0].shape[0]
    pipes = len(y_parts)
    return call(
        functools.partial(down_kernel, pipes, first),
        [struct((rows, width))] * 2,
        [SMEM] + [VMEM] * (5 + 2 * pipes) + [ANY] * len(after),
        "expert_down",
        16 * rows * width * units,
        8 * units * width,
        scratch=[pltpu.VMEM((2 * units, width), jnp.bfloat16)],
    )(pipe, act, *w_out, *y_parts, *pair_parts, *rests, *after)


def total_kernel(held, own_ref, z_ref, *refs):
    refs[held][...] = (own_ref[...].astype(jnp.float32) + z_ref[...].astype(jnp.float32)).astype(
        jnp.bfloat16
    )


def total(own, z, held):
    outs = [struct(own.shape)] + [struct(value.shape) for value in held]
    return call(
        functools.partial(total_kernel, len(held)),
        outs,
        [VMEM] * 2 + [ANY] * len(held),
        "far_total",
        own.size,
        6 * own.size,
        out_specs=[VMEM] + [ANY] * len(held),
        aliases={2 + i: 1 + i for i in range(len(held))},
    )(own, z, *held)


def finish_kernel(groups, cap, *refs):
    hidden_ref, gate_ref, flat_ref = refs[:3]
    own_ref, z_ref = refs[3:5]
    back_refs = refs[5:-1]
    out_ref = refs[-1]
    tokens, width = hidden_ref.shape
    slots = lax.broadcasted_iota(jnp.int32, (tokens, groups * cap), 1)
    picker = (slots == flat_ref[...]).astype(jnp.float32).astype(jnp.bfloat16)
    step = 512
    for at in range(0, width, step):
        cols = slice(at, at + step)
        near = (own_ref[:, cols].astype(jnp.float32) + z_ref[:, cols].astype(jnp.float32)).astype(
            jnp.bfloat16
        )
        side, inner = divmod(at, width // 2)
        backs = [r[:, inner : inner + step] for r in back_refs[side::2]]
        found = jnp.concatenate([near, *backs], axis=0)
        picked = jnp.dot(picker, found, preferred_element_type=jnp.float32)
        out_ref[:, cols] = (hidden_ref[:, cols] + gate_ref[...] * picked).astype(jnp.bfloat16)


def finish(hidden, gate, flat, sums, backs, groups, cap):
    tokens, width = hidden.shape
    operands = [hidden, gate, flat, *sums, *backs]
    return call(
        functools.partial(finish_kernel, groups, cap),
        struct((tokens, width)),
        [VMEM] * len(operands),
        "finish",
        4 * tokens * cap * groups * width,
        16 * tokens * width,
    )(*operands)


def body(state, query, enc_kv, gain, w_in, w_out, expert_id, slot, gate):
    tokens, width = state.shape[2:]
    devices = lax.axis_size("expert")
    pipes = lax.axis_size("pipe")
    groups = devices // WSPLIT
    cap = 3 * tokens // (2 * groups)

    def across(value, bit):
        return lax.ppermute(value, "expert", [(i, i ^ bit) for i in range(devices)])

    def groups_on(value, count):
        shift = count * WSPLIT
        return lax.ppermute(value, "expert", [(i, (i + shift) % devices) for i in range(devices)])

    def along(value):
        perms = [[(i, (i + shift) % pipes) for i in range(pipes)] for shift in range(1, pipes)]
        return [value] + [lax.ppermute(value, "pipe", perm) for perm in perms]

    def paired(parts):
        return [across(value, 1) for value in parts]

    pipe = lax.axis_index("pipe").astype(jnp.int32)
    w_in_pair, w_out_pair = across(w_in, 1), across(w_out, 1)
    pipe = pipe.reshape(1)
    depth = width // pipes
    in_y, in_late = (cut_part(pipe, w_in, depth, at, depth // 2) for at in (0, depth // 2))
    kv = jnp.transpose(enc_kv[0], (1, 0, 2)).reshape(-1, width)
    (kv,) = after_all([kv], [in_y])
    kv_pieces = [kv]
    for shift in range(1, pipes):
        perm = [(i, (i + shift) % pipes) for i in range(pipes)]
        kv_pieces.append(lax.ppermute(kv, "pipe", perm))
    in_y = across(in_y, 2)
    in_late = across(*after_all([in_late], kv_pieces[1:2]), 2)

    group = (lax.axis_index("expert") // WSPLIT).astype(jnp.int32).reshape(1)
    staged = stage(
        group,
        state[0, 0],
        query[0, 0],
        gain.reshape(1, width),
        expert_id[0],
        slot[0],
        gate[0],
        groups,
        cap,
    )
    flat, gates = staged[4:]
    hidden, near, *packed = attend(
        *staged[:4], kv_pieces, groups, cap, after=[w_in_pair, w_out_pair]
    )
    far = [groups_on(block, count) for count, block in enumerate(packed, 1)]
    far = jnp.concatenate(far, axis=0) if len(far) > 1 else far[0]

    in_first = along(*after_all([in_y], [near]))
    w_in_held, w_out_held, out_part, out_rest = hold(pipe, w_in, w_out, pipes, in_first[:1])
    in_last = after_all([in_late], [in_first[0], out_part])
    out_part, out_rest = after_all([out_part, out_rest], in_last)
    in_last = along(*in_last)
    out_y, rest_y = across(out_part, 2), across(out_rest, 2)

    near_z = across(near, 4)
    far = [far]
    for step in range(CROSS_STEPS):
        far = after_all(far, [] if step else [near_z], CROSS_WEIGHT)
    (far,) = far
    far_z = [across(far, 4)]
    in_sent = in_last[-1]
    in_parts = after_all([*in_first, *in_last], far_z)
    for _ in range(FAR_STEPS):
        far_z = after_all(far_z, [], FAR_WEIGHT)
    (far_z,) = far_z

    in_pair = paired(in_parts)

    def experts_up(own, z, after=()):
        act = up(own, z, [w_in_held, w_in_pair])
        return up_y(pipe, act, own, z, in_parts, in_pair, pipes, after)

    far_act = experts_up(far, far_z)
    out_parts = along(*after_all([out_y], [in_sent]))
    out_pair = paired(out_parts[:1])
    *out_parts[1:], rest_y = after_all([*out_parts[1:], rest_y], [far_act, *out_pair])
    out_pair += paired(out_parts[1:])
    rests = [rest_y, across(rest_y, 1)]

    def experts_down(act, first, size, after=()):
        return down(
            pipe, act, [w_out_held, w_out_pair], out_parts, out_pair, rests, first, size, after
        )

    half = width // 2
    far_a, sent_a = experts_down(far_act, 0, half)
    far_b, sent_b = experts_down(far_act, half, half, [far_a])
    near_act = experts_up(near, near_z, [far_b])
    (sent_b,) = after_all([sent_b], [near_act])
    near_own, near_sent = experts_down(near_act, 0, width)
    (sum_a,) = total(far_a, across(sent_a, 4), [])
    sum_b, near_sent = total(far_b, across(sent_b, 4), [near_sent])
    backs = [
        groups_on(side[(count - 1) * cap : count * cap], groups - count)
        for count in range(1, groups)
        for side in (sum_a, sum_b)
    ]
    backs[::2] = after_all(backs[::2], [], SUM_WEIGHT)
    backs[::2] = after_all(backs[::2], [], BACK_WEIGHT)
    near_sums = [near_own, across(near_sent, 4)]
    output = finish(hidden, gates, flat, near_sums, backs, groups, cap)
    return output.reshape(1, 1, tokens, width)


def solution(mesh):
    return jax.shard_map(
        body,
        mesh=mesh,
        in_specs=(
            P("expert", "pipe", None, None),
            P("expert", "pipe", None, None),
            P("expert", "pipe", None, None),
            P(),
            P(None, "expert"),
            P("expert", None),
            P("expert", "pipe", None),
            P("expert", "pipe", None),
            P("expert", "pipe", None),
        ),
        out_specs=P("expert", "pipe", None, None),
        check_vma=False,
    )
```

```python
import functools
import math

import jax
import jax.numpy as jnp
from jax import lax
from jax.experimental import pallas as pl
from jax.experimental.pallas import tpu as pltpu
from jax.sharding import PartitionSpec as P

HEADS = 16
HD = 128
WSPLIT = 8
EPS = 1e-06
FAR_WEIGHT = 3_000_000_000
FAR_STEPS = 4
CROSS_STEPS = 1
CROSS_WEIGHT = 3_000_000_000
NEAR_WEIGHT = 1_000_000_000
SUM_WEIGHT = 1_000_000_000
BACK_WEIGHT = 3_000_000_000
VMEM_LIMIT = 32 * 1024 * 1024
PART_LIMIT = 60 * 1024 * 1024

VMEM = pl.BlockSpec(memory_space=pltpu.VMEM)
SMEM = pl.BlockSpec(memory_space=pltpu.SMEM)
ANY = pl.BlockSpec(memory_space=pl.ANY)


def struct(shape, dtype=jnp.bfloat16):
    return jax.ShapeDtypeStruct(shape, dtype)


def call(
    kernel, outs, in_specs, name, flops, moved, scratch=(), out_specs=None, aliases=None, limit=VMEM_LIMIT
):
    return pl.pallas_call(
        kernel,
        out_shape=outs,
        in_specs=in_specs,
        out_specs=out_specs or jax.tree.map(lambda _: VMEM, outs),
        scratch_shapes=list(scratch),
        input_output_aliases=aliases or {},
        compiler_params=pltpu.CompilerParams(vmem_limit_bytes=limit),
        cost_estimate=pl.CostEstimate(flops=flops, bytes_accessed=moved, transcendentals=0),
        name=name,
    )


def as_column(row):
    count = row.shape[1]
    down = lax.broadcasted_iota(jnp.int32, (count, count), 0)
    along = lax.broadcasted_iota(jnp.int32, (count, count), 1)
    return jnp.sum(jnp.where(down == along, row, jnp.zeros_like(row)), axis=1, keepdims=True)


def stage_kernel(groups, cap, *refs):
    group_ref, state_in, query_in, gain_in, expert_ref, slot_ref, gate_ref = refs[:7]
    state_out, query_out, gain_out, flat_row, flat_column, gate_column = refs[7:]
    state_out[...] = state_in[...]
    query_out[...] = query_in[...]
    gain_out[...] = gain_in[...]
    offset = expert_ref[...] - group_ref[0]
    offset = jnp.where(offset < 0, offset + groups, offset)
    slot = slot_ref[...]
    flat = jnp.where(slot >= 0, offset * cap + slot, -1)
    flat_row[...] = flat
    flat_column[...] = as_column(flat)
    gate_column[...] = as_column(gate_ref[...])


def stage(group, state, query, gain, expert_id, slot, gate, groups, cap):
    tokens, width = state.shape
    outs = [
        struct((tokens, width)),
        struct((tokens, width)),
        struct((1, width), jnp.float32),
        struct((1, tokens), jnp.int32),
        struct((tokens, 1), jnp.int32),
        struct((tokens, 1), jnp.float32),
    ]
    return call(
        functools.partial(stage_kernel, groups, cap),
        outs,
        [SMEM] + [VMEM] * 6,
        "stage",
        tokens * tokens,
        8 * tokens * width,
    )(group, state, query, gain, expert_id, slot, gate)


def gate_kernel(*refs):
    pass


def after_all(values, others, weight=1):
    return call(
        gate_kernel,
        [struct(value.shape) for value in values],
        [ANY] * (len(values) + len(others)),
        "hand_on",
        weight,
        1,
        out_specs=[ANY] * len(values),
        aliases={i: i for i in range(len(values))},
    )(*values, *others)


def attend_kernel(pieces, groups, cap, *refs):
    state_ref, query_ref, gain_ref, flat_ref = refs[:4]
    kv_refs = refs[4 : 4 + pieces]
    hidden_ref = refs[-1 - groups]
    packed_refs = refs[-groups:]
    tokens, width = state_ref.shape
    local = kv_refs[0].shape[0] // 2
    scale = 1.0 / math.sqrt(HD)
    squares = jnp.zeros((tokens, HD), jnp.float32)
    for head in range(HEADS):
        cols = slice(head * HD, (head + 1) * HD)
        keys = jnp.concatenate([r[:local, cols] for r in kv_refs], axis=0)
        values = jnp.concatenate([r[local:, cols] for r in kv_refs], axis=0)
        scores = (
            lax.dot_general(
                query_ref[:, cols],
                keys,
                (((1,), (1,)), ((), ())),
                preferred_element_type=jnp.float32,
            )
            * scale
        )
        raised = jnp.exp(scores - jnp.max(scores, axis=1, keepdims=True))
        total = jnp.sum(raised, axis=1, keepdims=True)
        mixed = jnp.dot(raised.astype(jnp.bfloat16), values, preferred_element_type=jnp.float32)
        hidden = state_ref[:, cols].astype(jnp.float32) + mixed / total
        hidden_ref[:, cols] = hidden
        squares = squares + hidden * hidden
    mean_square = jnp.sum(squares, axis=1, keepdims=True) * (1.0 / width)
    inverse = lax.rsqrt(mean_square + EPS)
    rows = lax.broadcasted_iota(jnp.int32, (groups * cap, tokens), 0)
    selector = (rows == flat_ref[...]).astype(jnp.float32).astype(jnp.bfloat16)
    step = 512
    for at in range(0, width, step):
        cols = slice(at, at + step)
        normed = (hidden_ref[:, cols] * inverse * gain_ref[:, cols]).astype(jnp.bfloat16)
        packed = jnp.dot(selector, normed, preferred_element_type=jnp.float32).astype(jnp.bfloat16)
        for group in range(groups):
            packed_refs[group][:, cols] = packed[group * cap : (group + 1) * cap]


def attend(state, query, gain, flat, kv_pieces, groups, cap, after):
    tokens, width = state.shape
    outs = [struct((tokens, width), jnp.float32)] + [struct((cap, width))] * groups
    pieces = len(kv_pieces)
    return call(
        functools.partial(attend_kernel, pieces, groups, cap),
        outs,
        [VMEM] * (4 + pieces) + [ANY] * len(after),
        "attend",
        4 * tokens * pieces * kv_pieces[0].shape[0] * width,
        12 * tokens * width,
    )(state, query, gain, flat, *kv_pieces, *after)


def place(pipes, shift, pipe, size):
    at = pipe - shift
    at = jnp.where(at < 0, at + pipes, at)
    return pl.multiple_of(at * size, size)


def part_kernel(stride, first, pipe_ref, whole, part, sem):
    size = part.shape[0]
    at = pl.multiple_of(pipe_ref[0] * stride + first, size)
    copy = pltpu.make_async_copy(whole.at[pl.ds(at, size)], part, sem)
    copy.start()
    copy.wait()


def cut_part(pipe, whole, stride, first, size):
    return call(
        functools.partial(part_kernel, stride, first),
        struct((size, whole.shape[1])),
        [SMEM, ANY],
        "weight_part",
        1,
        4 * size * whole.shape[1],
        scratch=[pltpu.SemaphoreType.DMA],
        limit=PART_LIMIT,
    )(pipe, whole)


def hold_kernel(pipes, pipe_ref, w_in, w_out, *refs):
    in_held, out_held, out_part, out_rest, sems = refs[-5:]
    size = out_part.shape[0]
    at = pl.multiple_of(pipe_ref[0] * size, size)
    copies = [
        pltpu.make_async_copy(source, target, sems.at[i])
        for i, (source, target) in enumerate(
            (
                (w_in, in_held),
                (w_out, out_held),
                (w_out.at[pl.ds(at, size)], out_part),
                (w_out.at[pipes * size :], out_rest),
            )
        )
    ]
    for copy in copies:
        copy.start()
    for copy in copies:
        copy.wait()


def hold(pipe, w_in, w_out, pipes, after):
    units, width = w_out.shape
    size = units * 7 // 12 // pipes // 16 * 16
    return call(
        functools.partial(hold_kernel, pipes),
        [
            struct(w_in.shape),
            struct(w_out.shape),
            struct((size, width)),
            struct((units - pipes * size, width)),
        ],
        [SMEM, ANY, ANY] + [ANY] * len(after),
        "hold_weights",
        1,
        8 * units * width,
        scratch=[pltpu.SemaphoreType.DMA((4,))],
    )(pipe, w_in, w_out, *after)


def up_kernel(own_in, z_in, w_own, w_pair, out_ref):
    entries = jnp.concatenate([own_in[...], z_in[...]], axis=0)
    weights = jnp.concatenate([w_own[...], w_pair[...]], axis=1)
    raw = jnp.dot(entries, weights, preferred_element_type=jnp.float32)
    out_ref[...] = jnp.maximum(raw, 0.0).astype(jnp.bfloat16)


def up(own, z, w_in):
    rows, width = own.shape
    units = w_in[0].shape[1]
    return call(
        up_kernel,
        struct((2 * rows, 2 * units)),
        [VMEM] * 4,
        "expert_up",
        8 * rows * width * units,
        4 * units * width,
    )(own, z, *w_in)


def up_y_kernel(pipes, halves, *refs):
    pipe = refs[0][0]
    act_ref, own_in, z_in = refs[1:4]
    count = pipes * halves
    y_parts = refs[4 : 4 + count]
    pair_parts = refs[4 + count : 4 + 2 * count]
    out_ref, entries = refs[-2:]
    rows, width = own_in.shape
    units = act_ref.shape[1]
    entries[:rows] = own_in[...]
    entries[rows:] = z_in[...]
    out_ref[:, :units] = act_ref[...]
    depth = width // count
    raw = jnp.zeros(act_ref.shape, jnp.float32)
    for i in range(count):
        half, shift = divmod(i, pipes)
        at = place(pipes, shift, pipe, halves * depth) + half * depth
        part = entries[:, pl.ds(pl.multiple_of(at, depth), depth)]
        weights = jnp.concatenate([y_parts[i][...], pair_parts[i][...]], axis=1)
        raw = raw + jnp.dot(part, weights, preferred_element_type=jnp.float32)
    out_ref[:, units:] = jnp.maximum(raw, 0.0).astype(jnp.bfloat16)


def up_y(pipe, act, own, z, y_parts, pair_parts, pipes, after=()):
    rows, width = own.shape
    units = y_parts[0].shape[1]
    count = len(y_parts)
    return call(
        functools.partial(up_y_kernel, pipes, count // pipes),
        struct((2 * rows, 4 * units)),
        [SMEM] + [VMEM] * (3 + 2 * count) + [ANY] * len(after),
        "expert_up_y",
        8 * rows * width * units,
        4 * units * width,
        scratch=[pltpu.VMEM((2 * rows, width), jnp.bfloat16)],
    )(pipe, act, own, z, *y_parts, *pair_parts, *after)


def down_kernel(pipes, first, *refs):
    pipe = refs[0][0]
    act_ref, w_own, w_pair = refs[1:4]
    y_parts, refs = refs[4 : 4 + pipes], refs[4 + pipes :]
    pair_parts, refs = refs[:pipes], refs[pipes:]
    y_rest, pair_rest = refs[:2]
    own_ref, z_ref, held = refs[-3:]
    rows, width = own_ref.shape
    whole = slice(first, first + width)
    units = w_own.shape[0]
    size = y_parts[0].shape[0]
    for shift in range(pipes):
        at = place(pipes, shift, pipe, size)
        held[pl.ds(at, size)] = y_parts[shift][:, whole]
        held[pl.ds(pl.multiple_of(units + at, size), size)] = pair_parts[shift][:, whole]
    held[pipes * size : units] = y_rest[:, whole]
    held[units + pipes * size :] = pair_rest[:, whole]
    step = 512
    for at in range(0, width, step):
        cols = slice(at, at + step)
        there = slice(first + at, first + at + step)
        weights = jnp.concatenate([w_own[:, there], w_pair[:, there], held[:, cols]], axis=0)
        part = jnp.dot(act_ref[...], weights, preferred_element_type=jnp.float32)
        part = part.astype(jnp.bfloat16)
        own_ref[:, cols] = part[:rows]
        z_ref[:, cols] = part[rows:]


def down(pipe, act, w_out, y_parts, pair_parts, rests, first, width, after=()):
    rows = act.shape[0] // 2
    units = w_out[0].shape[0]
    pipes = len(y_parts)
    return call(
        functools.partial(down_kernel, pipes, first),
        [struct((rows, width))] * 2,
        [SMEM] + [VMEM] * (5 + 2 * pipes) + [ANY] * len(after),
        "expert_down",
        16 * rows * width * units,
        8 * units * width,
        scratch=[pltpu.VMEM((2 * units, width), jnp.bfloat16)],
    )(pipe, act, *w_out, *y_parts, *pair_parts, *rests, *after)


def total_kernel(held, own_ref, z_ref, *refs):
    refs[held][...] = (own_ref[...].astype(jnp.float32) + z_ref[...].astype(jnp.float32)).astype(
        jnp.bfloat16
    )


def total(own, z, held):
    outs = [struct(own.shape)] + [struct(value.shape) for value in held]
    return call(
        functools.partial(total_kernel, len(held)),
        outs,
        [VMEM] * 2 + [ANY] * len(held),
        "far_total",
        own.size,
        6 * own.size,
        out_specs=[VMEM] + [ANY] * len(held),
        aliases={2 + i: 1 + i for i in range(len(held))},
    )(own, z, *held)


def finish_kernel(groups, cap, *refs):
    hidden_ref, gate_ref, flat_ref = refs[:3]
    own_ref, z_ref = refs[3:5]
    back_refs = refs[5:-1]
    out_ref = refs[-1]
    tokens, width = hidden_ref.shape
    slots = lax.broadcasted_iota(jnp.int32, (tokens, groups * cap), 1)
    picker = (slots == flat_ref[...]).astype(jnp.float32).astype(jnp.bfloat16)
    step = 512
    for at in range(0, width, step):
        cols = slice(at, at + step)
        near = (own_ref[:, cols].astype(jnp.float32) + z_ref[:, cols].astype(jnp.float32)).astype(
            jnp.bfloat16
        )
        side, inner = divmod(at, width // 2)
        backs = [r[:, inner : inner + step] for r in back_refs[side::2]]
        found = jnp.concatenate([near, *backs], axis=0)
        picked = jnp.dot(picker, found, preferred_element_type=jnp.float32)
        out_ref[:, cols] = (hidden_ref[:, cols] + gate_ref[...] * picked).astype(jnp.bfloat16)


def finish(hidden, gate, flat, sums, backs, groups, cap):
    tokens, width = hidden.shape
    operands = [hidden, gate, flat, *sums, *backs]
    return call(
        functools.partial(finish_kernel, groups, cap),
        struct((tokens, width)),
        [VMEM] * len(operands),
        "finish",
        4 * tokens * cap * groups * width,
        16 * tokens * width,
    )(*operands)


def body(state, query, enc_kv, gain, w_in, w_out, expert_id, slot, gate):
    tokens, width = state.shape[2:]
    devices = lax.axis_size("expert")
    pipes = lax.axis_size("pipe")
    groups = devices // WSPLIT
    cap = 3 * tokens // (2 * groups)

    def across(value, bit):
        return lax.ppermute(value, "expert", [(i, i ^ bit) for i in range(devices)])

    def groups_on(value, count):
        shift = count * WSPLIT
        return lax.ppermute(value, "expert", [(i, (i + shift) % devices) for i in range(devices)])

    def along(value):
        perms = [[(i, (i + shift) % pipes) for i in range(pipes)] for shift in range(1, pipes)]
        return [value] + [lax.ppermute(value, "pipe", perm) for perm in perms]

    def paired(parts):
        return [across(value, 1) for value in parts]

    pipe = lax.axis_index("pipe").astype(jnp.int32)
    w_in_pair, w_out_pair = across(w_in, 1), across(w_out, 1)
    pipe = pipe.reshape(1)
    depth = width // pipes
    in_y, in_late = (cut_part(pipe, w_in, depth, at, depth // 2) for at in (0, depth // 2))
    kv = jnp.transpose(enc_kv[0], (1, 0, 2)).reshape(-1, width)
    (kv,) = after_all([kv], [in_y])
    kv_pieces = [kv]
    for shift in range(1, pipes):
        perm = [(i, (i + shift) % pipes) for i in range(pipes)]
        kv_pieces.append(lax.ppermute(kv, "pipe", perm))
    in_y = across(in_y, 2)
    in_late = across(*after_all([in_late], kv_pieces[1:2]), 2)

    group = (lax.axis_index("expert") // WSPLIT).astype(jnp.int32).reshape(1)
    staged = stage(
        group,
        state[0, 0],
        query[0, 0],
        gain.reshape(1, width),
        expert_id[0],
        slot[0],
        gate[0],
        groups,
        cap,
    )
    flat, gates = staged[4:]
    hidden, near, *packed = attend(
        *staged[:4], kv_pieces, groups, cap, after=[w_in_pair, w_out_pair]
    )
    far = [groups_on(block, count) for count, block in enumerate(packed, 1)]
    far = jnp.concatenate(far, axis=0) if len(far) > 1 else far[0]

    w_in_held, w_out_held, out_part, out_rest = hold(pipe, w_in, w_out, pipes, [near])
    in_first = along(*after_all([in_y], [out_part]))
    in_last = after_all([in_late], [in_first[0]])
    out_part, out_rest = after_all([out_part, out_rest], in_last)
    in_last = along(*in_last)
    out_y, rest_y = across(out_part, 2), across(out_rest, 2)

    near_z = across(near, 4)
    far = [far]
    for step in range(CROSS_STEPS):
        far = after_all(far, [] if step else [near_z], CROSS_WEIGHT)
    (far,) = far
    far_z = [across(far, 4)]
    in_sent = in_last[-1]
    in_parts = after_all([*in_first, *in_last], far_z)
    for _ in range(FAR_STEPS):
        far_z = after_all(far_z, [], FAR_WEIGHT)
    (far_z,) = far_z

    in_pair = paired(in_parts)

    def experts_up(own, z, after=()):
        act = up(own, z, [w_in_held, w_in_pair])
        return up_y(pipe, act, own, z, in_parts, in_pair, pipes, after)

    far_act = experts_up(far, far_z)
    out_parts = along(*after_all([out_y], [in_sent]))
    out_pair = paired(out_parts[:1])
    *out_parts[1:], rest_y = after_all([*out_parts[1:], rest_y], [far_act, *out_pair])
    out_pair += paired(out_parts[1:])
    rests = [rest_y, across(rest_y, 1)]

    def experts_down(act, first, size, after=()):
        return down(
            pipe, act, [w_out_held, w_out_pair], out_parts, out_pair, rests, first, size, after
        )

    half = width // 2
    far_a, sent_a = experts_down(far_act, 0, half)
    far_b, sent_b = experts_down(far_act, half, half, [far_a])
    near_act = experts_up(near, near_z, [far_b])
    (sent_b,) = after_all([sent_b], [near_act])
    near_own, near_sent = experts_down(near_act, 0, width)
    sum_a, near_sent = total(far_a, across(sent_a, 4), [near_sent])
    (sum_b,) = total(far_b, across(sent_b, 4), [])
    backs = [
        groups_on(side[(count - 1) * cap : count * cap], groups - count)
        for count in range(1, groups)
        for side in (sum_a, sum_b)
    ]
    backs[::2] = after_all(backs[::2], [sum_b], SUM_WEIGHT)
    backs[::2] = after_all(backs[::2], [], BACK_WEIGHT)
    near_sums = [near_own, *after_all([across(near_sent, 4)], [], NEAR_WEIGHT)]
    output = finish(hidden, gates, flat, near_sums, backs, groups, cap)
    return output.reshape(1, 1, tokens, width)


def solution(mesh):
    return jax.shard_map(
        body,
        mesh=mesh,
        in_specs=(
            P("expert", "pipe", None, None),
            P("expert", "pipe", None, None),
            P("expert", "pipe", None, None),
            P(),
            P(None, "expert"),
            P("expert", None),
            P("expert", "pipe", None),
            P("expert", "pipe", None),
            P("expert", "pipe", None),
        ),
        out_specs=P("expert", "pipe", None, None),
        check_vma=False,
    )
```

```python
import functools
import math

import jax
import jax.numpy as jnp
from jax import lax
from jax.experimental import pallas as pl
from jax.experimental.pallas import tpu as pltpu
from jax.sharding import PartitionSpec as P

HEADS = 16
HD = 128
WSPLIT = 8
EPS = 1e-06
FAR_WEIGHT = 3_000_000_000
FAR_STEPS = 4
CROSS_STEPS = 1
CROSS_WEIGHT = 3_000_000_000
PART_WEIGHT = 1
FIRST_WEIGHT = 1
REST_STEPS = 1
REST_WEIGHT = 1
SUM_WEIGHT = 1_000_000_000
BACK_WEIGHT = 3_000_000_000
BACK_STEPS = 1
VMEM_LIMIT = 32 * 1024 * 1024
PART_LIMIT = 60 * 1024 * 1024

VMEM = pl.BlockSpec(memory_space=pltpu.VMEM)
SMEM = pl.BlockSpec(memory_space=pltpu.SMEM)
ANY = pl.BlockSpec(memory_space=pl.ANY)


def struct(shape, dtype=jnp.bfloat16):
    return jax.ShapeDtypeStruct(shape, dtype)


def call(
    kernel, outs, in_specs, name, flops, moved, scratch=(), out_specs=None, aliases=None, limit=VMEM_LIMIT
):
    return pl.pallas_call(
        kernel,
        out_shape=outs,
        in_specs=in_specs,
        out_specs=out_specs or jax.tree.map(lambda _: VMEM, outs),
        scratch_shapes=list(scratch),
        input_output_aliases=aliases or {},
        compiler_params=pltpu.CompilerParams(vmem_limit_bytes=limit),
        cost_estimate=pl.CostEstimate(flops=flops, bytes_accessed=moved, transcendentals=0),
        name=name,
    )


def as_column(row):
    count = row.shape[1]
    down = lax.broadcasted_iota(jnp.int32, (count, count), 0)
    along = lax.broadcasted_iota(jnp.int32, (count, count), 1)
    return jnp.sum(jnp.where(down == along, row, jnp.zeros_like(row)), axis=1, keepdims=True)


def stage_kernel(groups, cap, *refs):
    group_ref, state_in, query_in, gain_in, expert_ref, slot_ref, gate_ref = refs[:7]
    state_out, query_out, gain_out, flat_row, flat_column, gate_column = refs[7:]
    state_out[...] = state_in[...]
    query_out[...] = query_in[...]
    gain_out[...] = gain_in[...]
    offset = expert_ref[...] - group_ref[0]
    offset = jnp.where(offset < 0, offset + groups, offset)
    slot = slot_ref[...]
    flat = jnp.where(slot >= 0, offset * cap + slot, -1)
    flat_row[...] = flat
    flat_column[...] = as_column(flat)
    gate_column[...] = as_column(gate_ref[...])


def stage(group, state, query, gain, expert_id, slot, gate, groups, cap):
    tokens, width = state.shape
    outs = [
        struct((tokens, width)),
        struct((tokens, width)),
        struct((1, width), jnp.float32),
        struct((1, tokens), jnp.int32),
        struct((tokens, 1), jnp.int32),
        struct((tokens, 1), jnp.float32),
    ]
    return call(
        functools.partial(stage_kernel, groups, cap),
        outs,
        [SMEM] + [VMEM] * 6,
        "stage",
        tokens * tokens,
        8 * tokens * width,
    )(group, state, query, gain, expert_id, slot, gate)


def gate_kernel(*refs):
    pass


def after_all(values, others, weight=1):
    return call(
        gate_kernel,
        [struct(value.shape) for value in values],
        [ANY] * (len(values) + len(others)),
        "hand_on",
        weight,
        1,
        out_specs=[ANY] * len(values),
        aliases={i: i for i in range(len(values))},
    )(*values, *others)


def attend_kernel(pieces, groups, cap, *refs):
    state_ref, query_ref, gain_ref, flat_ref = refs[:4]
    kv_refs = refs[4 : 4 + pieces]
    hidden_ref = refs[-1 - groups]
    packed_refs = refs[-groups:]
    tokens, width = state_ref.shape
    local = kv_refs[0].shape[0] // 2
    scale = 1.0 / math.sqrt(HD)
    squares = jnp.zeros((tokens, HD), jnp.float32)
    for head in range(HEADS):
        cols = slice(head * HD, (head + 1) * HD)
        keys = jnp.concatenate([r[:local, cols] for r in kv_refs], axis=0)
        values = jnp.concatenate([r[local:, cols] for r in kv_refs], axis=0)
        scores = (
            lax.dot_general(
                query_ref[:, cols],
                keys,
                (((1,), (1,)), ((), ())),
                preferred_element_type=jnp.float32,
            )
            * scale
        )
        raised = jnp.exp(scores - jnp.max(scores, axis=1, keepdims=True))
        total = jnp.sum(raised, axis=1, keepdims=True)
        mixed = jnp.dot(raised.astype(jnp.bfloat16), values, preferred_element_type=jnp.float32)
        hidden = state_ref[:, cols].astype(jnp.float32) + mixed / total
        hidden_ref[:, cols] = hidden
        squares = squares + hidden * hidden
    mean_square = jnp.sum(squares, axis=1, keepdims=True) * (1.0 / width)
    inverse = lax.rsqrt(mean_square + EPS)
    rows = lax.broadcasted_iota(jnp.int32, (groups * cap, tokens), 0)
    selector = (rows == flat_ref[...]).astype(jnp.float32).astype(jnp.bfloat16)
    step = 512
    for at in range(0, width, step):
        cols = slice(at, at + step)
        normed = (hidden_ref[:, cols] * inverse * gain_ref[:, cols]).astype(jnp.bfloat16)
        packed = jnp.dot(selector, normed, preferred_element_type=jnp.float32).astype(jnp.bfloat16)
        for group in range(groups):
            packed_refs[group][:, cols] = packed[group * cap : (group + 1) * cap]


def attend(state, query, gain, flat, kv_pieces, groups, cap, after):
    tokens, width = state.shape
    outs = [struct((tokens, width), jnp.float32)] + [struct((cap, width))] * groups
    pieces = len(kv_pieces)
    return call(
        functools.partial(attend_kernel, pieces, groups, cap),
        outs,
        [VMEM] * (4 + pieces) + [ANY] * len(after),
        "attend",
        4 * tokens * pieces * kv_pieces[0].shape[0] * width,
        12 * tokens * width,
    )(state, query, gain, flat, *kv_pieces, *after)


def place(pipes, shift, pipe, size):
    at = pipe - shift
    at = jnp.where(at < 0, at + pipes, at)
    return pl.multiple_of(at * size, size)


def part_kernel(stride, first, pipe_ref, whole, part, sem):
    size = part.shape[0]
    at = pl.multiple_of(pipe_ref[0] * stride + first, size)
    copy = pltpu.make_async_copy(whole.at[pl.ds(at, size)], part, sem)
    copy.start()
    copy.wait()


def cut_part(pipe, whole, stride, first, size):
    return call(
        functools.partial(part_kernel, stride, first),
        struct((size, whole.shape[1])),
        [SMEM, ANY],
        "weight_part",
        1,
        4 * size * whole.shape[1],
        scratch=[pltpu.SemaphoreType.DMA],
        limit=PART_LIMIT,
    )(pipe, whole)


def hold_kernel(pipes, pipe_ref, w_in, w_out, *refs):
    in_held, out_held, out_part, out_rest, sems = refs[-5:]
    size, half = out_part.shape
    at = pl.multiple_of(pipe_ref[0] * size, size)
    copies = [
        pltpu.make_async_copy(source, target, sems.at[i])
        for i, (source, target) in enumerate(
            (
                (w_in, in_held),
                (w_out, out_held),
                (w_out.at[pl.ds(at, size), pl.ds(0, half)], out_part),
                (w_out.at[:, pl.ds(half, half)], out_rest),
            )
        )
    ]
    for copy in copies:
        copy.start()
    for copy in copies:
        copy.wait()


def hold(pipe, w_in, w_out, pipes, after):
    units, width = w_out.shape
    half = width // 2
    return call(
        functools.partial(hold_kernel, pipes),
        [
            struct(w_in.shape),
            struct(w_out.shape),
            struct((units // pipes, half)),
            struct((units, half)),
        ],
        [SMEM, ANY, ANY] + [ANY] * len(after),
        "hold_weights",
        1,
        8 * units * width,
        scratch=[pltpu.SemaphoreType.DMA((4,))],
    )(pipe, w_in, w_out, *after)


def up_kernel(own_in, z_in, w_own, w_pair, out_ref):
    entries = jnp.concatenate([own_in[...], z_in[...]], axis=0)
    weights = jnp.concatenate([w_own[...], w_pair[...]], axis=1)
    raw = jnp.dot(entries, weights, preferred_element_type=jnp.float32)
    out_ref[...] = jnp.maximum(raw, 0.0).astype(jnp.bfloat16)


def up(own, z, w_in):
    rows, width = own.shape
    units = w_in[0].shape[1]
    return call(
        up_kernel,
        struct((2 * rows, 2 * units)),
        [VMEM] * 4,
        "expert_up",
        8 * rows * width * units,
        4 * units * width,
    )(own, z, *w_in)


def up_y_kernel(pipes, halves, *refs):
    pipe = refs[0][0]
    act_ref, own_in, z_in = refs[1:4]
    count = pipes * halves
    y_parts = refs[4 : 4 + count]
    pair_parts = refs[4 + count : 4 + 2 * count]
    out_ref, entries = refs[-2:]
    rows, width = own_in.shape
    units = act_ref.shape[1]
    entries[:rows] = own_in[...]
    entries[rows:] = z_in[...]
    out_ref[:, :units] = act_ref[...]
    depth = width // count
    raw = jnp.zeros(act_ref.shape, jnp.float32)
    for i in range(count):
        half, shift = divmod(i, pipes)
        at = place(pipes, shift, pipe, halves * depth) + half * depth
        part = entries[:, pl.ds(pl.multiple_of(at, depth), depth)]
        weights = jnp.concatenate([y_parts[i][...], pair_parts[i][...]], axis=1)
        raw = raw + jnp.dot(part, weights, preferred_element_type=jnp.float32)
    out_ref[:, units:] = jnp.maximum(raw, 0.0).astype(jnp.bfloat16)


def up_y(pipe, act, own, z, y_parts, pair_parts, pipes, after=()):
    rows, width = own.shape
    units = y_parts[0].shape[1]
    count = len(y_parts)
    return call(
        functools.partial(up_y_kernel, pipes, count // pipes),
        struct((2 * rows, 4 * units)),
        [SMEM] + [VMEM] * (3 + 2 * count) + [ANY] * len(after),
        "expert_up_y",
        8 * rows * width * units,
        4 * units * width,
        scratch=[pltpu.VMEM((2 * rows, width), jnp.bfloat16)],
    )(pipe, act, own, z, *y_parts, *pair_parts, *after)


def multiply(act_ref, weights, first, own_ref, z_ref):
    rows, width = own_ref.shape
    step = 512
    for at in range(0, width, step):
        cols = slice(at, at + step)
        there = slice(first + at, first + at + step)
        block = [r[:, there] for r in weights[:2]] + [r[:, cols] for r in weights[2:]]
        part = jnp.dot(
            act_ref[...], jnp.concatenate(block, axis=0), preferred_element_type=jnp.float32
        ).astype(jnp.bfloat16)
        own_ref[:, cols] = part[:rows]
        z_ref[:, cols] = part[rows:]


def down_first_kernel(pipes, *refs):
    pipe = refs[0][0]
    act_ref, w_own, w_pair = refs[1:4]
    y_parts = refs[4 : 4 + pipes]
    pair_parts = refs[4 + pipes : 4 + 2 * pipes]
    own_ref, z_ref, held = refs[-3:]
    units = w_own.shape[0]
    size = y_parts[0].shape[0]
    for shift in range(pipes):
        at = place(pipes, shift, pipe, size)
        held[pl.ds(at, size)] = y_parts[shift][...]
        held[pl.ds(pl.multiple_of(units + at, size), size)] = pair_parts[shift][...]
    multiply(act_ref, [w_own, w_pair, held], 0, own_ref, z_ref)


def down_last_kernel(act_ref, w_own, w_pair, y_rest, pair_rest, *refs):
    own_ref, z_ref = refs[-2:]
    multiply(act_ref, [w_own, w_pair, y_rest, pair_rest], own_ref.shape[1], own_ref, z_ref)


def down_first(pipe, act, w_out, y_parts, pair_parts):
    rows = act.shape[0] // 2
    units, width = w_out[0].shape
    pipes, half = len(y_parts), width // 2
    return call(
        functools.partial(down_first_kernel, pipes),
        [struct((rows, half))] * 2,
        [SMEM] + [VMEM] * (3 + 2 * pipes),
        "expert_down",
        16 * rows * half * units,
        8 * units * half,
        scratch=[pltpu.VMEM((2 * units, half), jnp.bfloat16)],
    )(pipe, act, *w_out, *y_parts, *pair_parts)


def down_last(act, w_out, rests, after=()):
    rows = act.shape[0] // 2
    units, width = w_out[0].shape
    half = width // 2
    return call(
        down_last_kernel,
        [struct((rows, half))] * 2,
        [VMEM] * 5 + [ANY] * len(after),
        "expert_down_last",
        16 * rows * half * units,
        8 * units * half,
    )(act, *w_out, *rests, *after)


def total_kernel(own_ref, z_ref, out_ref):
    out_ref[...] = (own_ref[...].astype(jnp.float32) + z_ref[...].astype(jnp.float32)).astype(
        jnp.bfloat16
    )


def total(own, z):
    return call(
        total_kernel,
        struct(own.shape),
        [VMEM] * 2,
        "far_total",
        own.size,
        6 * own.size,
    )(own, z)


def finish_kernel(groups, cap, *refs):
    hidden_ref, gate_ref, flat_ref = refs[:3]
    near_refs = refs[3:7]
    back_refs = refs[7:-1]
    out_ref = refs[-1]
    tokens, width = hidden_ref.shape
    half = width // 2
    slots = lax.broadcasted_iota(jnp.int32, (tokens, groups * cap), 1)
    picker = (slots == flat_ref[...]).astype(jnp.float32).astype(jnp.bfloat16)
    step = 512
    for at in range(0, width, step):
        cols = slice(at, at + step)
        side, inner = divmod(at, half)
        part = slice(inner, inner + step)
        own, z = near_refs[2 * side][:, part], near_refs[2 * side + 1][:, part]
        near = (own.astype(jnp.float32) + z.astype(jnp.float32)).astype(jnp.bfloat16)
        backs = [r[:, part] for r in back_refs[side::2]]
        found = jnp.concatenate([near, *backs], axis=0)
        picked = jnp.dot(picker, found, preferred_element_type=jnp.float32)
        out_ref[:, cols] = (hidden_ref[:, cols] + gate_ref[...] * picked).astype(jnp.bfloat16)


def finish(hidden, gate, flat, sums, backs, groups, cap):
    tokens, width = hidden.shape
    operands = [hidden, gate, flat, *sums, *backs]
    return call(
        functools.partial(finish_kernel, groups, cap),
        struct((tokens, width)),
        [VMEM] * len(operands),
        "finish",
        4 * tokens * cap * groups * width,
        16 * tokens * width,
    )(*operands)


def body(state, query, enc_kv, gain, w_in, w_out, expert_id, slot, gate):
    tokens, width = state.shape[2:]
    devices = lax.axis_size("expert")
    pipes = lax.axis_size("pipe")
    groups = devices // WSPLIT
    cap = 3 * tokens // (2 * groups)

    def across(value, bit):
        return lax.ppermute(value, "expert", [(i, i ^ bit) for i in range(devices)])

    def groups_on(value, count):
        shift = count * WSPLIT
        return lax.ppermute(value, "expert", [(i, (i + shift) % devices) for i in range(devices)])

    def along(value):
        perms = [[(i, (i + shift) % pipes) for i in range(pipes)] for shift in range(1, pipes)]
        return [value] + [lax.ppermute(value, "pipe", perm) for perm in perms]

    def paired(parts):
        return [across(value, 1) for value in parts]

    pipe = lax.axis_index("pipe").astype(jnp.int32)
    w_in_pair, w_out_pair = across(w_in, 1), across(w_out, 1)
    pipe = pipe.reshape(1)
    depth = width // pipes
    in_y, in_late = (cut_part(pipe, w_in, depth, at, depth // 2) for at in (0, depth // 2))
    kv = jnp.transpose(enc_kv[0], (1, 0, 2)).reshape(-1, width)
    (kv,) = after_all([kv], [in_y])
    kv_pieces = [kv]
    for shift in range(1, pipes):
        perm = [(i, (i + shift) % pipes) for i in range(pipes)]
        kv_pieces.append(lax.ppermute(kv, "pipe", perm))
    in_y = across(in_y, 2)
    in_late = across(*after_all([in_late], kv_pieces[1:2]), 2)

    group = (lax.axis_index("expert") // WSPLIT).astype(jnp.int32).reshape(1)
    staged = stage(
        group,
        state[0, 0],
        query[0, 0],
        gain.reshape(1, width),
        expert_id[0],
        slot[0],
        gate[0],
        groups,
        cap,
    )
    flat, gates = staged[4:]
    hidden, near, *packed = attend(
        *staged[:4], kv_pieces, groups, cap, after=[w_in_pair, w_out_pair]
    )
    far = [groups_on(block, count) for count, block in enumerate(packed, 1)]
    far = jnp.concatenate(far, axis=0) if len(far) > 1 else far[0]

    w_in_held, w_out_held, out_part, out_rest = hold(pipe, w_in, w_out, pipes, [near])
    in_first = along(*after_all([in_y], [out_part]))
    in_last = after_all([in_late], [in_first[0]])
    out_part, out_rest = after_all([out_part, out_rest], in_last)
    in_last = along(*in_last)
    out_y, rest_y = across(out_part, 2), across(out_rest, 2)

    near_z = across(near, 4)
    far = [far]
    for step in range(CROSS_STEPS):
        far = after_all(far, [] if step else [near_z], CROSS_WEIGHT)
    (far,) = far
    far_z = [across(far, 4)]
    in_sent = in_last[-1]
    in_parts = after_all([*in_first, *in_last], far_z)
    for _ in range(FAR_STEPS):
        far_z = after_all(far_z, [], FAR_WEIGHT)
    (far_z,) = far_z

    in_pair = paired(in_parts[:pipes])
    in_parts = [*in_parts[:pipes], *after_all(in_parts[pipes:], in_pair)]
    in_pair += paired(in_parts[pipes:])

    def experts_up(own, z, after=()):
        act = up(own, z, [w_in_held, w_in_pair])
        return up_y(pipe, act, own, z, in_parts, in_pair, pipes, after)

    far_act = experts_up(far, far_z)
    out_parts = along(*after_all([out_y], [in_sent]))
    out_pair = paired(out_parts[:1])
    out_parts[1:] = after_all(out_parts[1:], [far_act, *out_pair], PART_WEIGHT)
    out_pair += paired(out_parts[1:])
    w_out_here = [w_out_held, w_out_pair]
    far_a, sent_a = down_first(pipe, far_act, w_out_here, out_parts, out_pair)
    near_act = experts_up(near, near_z, [far_a])
    near_a, near_sent_a = down_first(pipe, near_act, w_out_here, out_parts, out_pair)
    sum_a = total(far_a, *after_all([across(sent_a, 4)], [], FIRST_WEIGHT))
    for step in range(REST_STEPS):
        (rest_y,) = after_all([rest_y], [] if step else [near_a, sum_a], REST_WEIGHT)
    rests = [rest_y, across(rest_y, 1)]
    far_b, sent_b = down_last(far_act, w_out_here, rests)
    near_b, near_sent_b = down_last(near_act, w_out_here, rests, [far_b])
    sum_b = total(far_b, across(sent_b, 4))
    backs = [
        groups_on(side[(count - 1) * cap : count * cap], groups - count)
        for count in range(1, groups)
        for side in (sum_a, sum_b)
    ]
    backs[::2] = after_all(backs[::2], [sum_b], SUM_WEIGHT)
    for _ in range(BACK_STEPS):
        backs[::2] = after_all(backs[::2], [], BACK_WEIGHT)
    near_sums = [near_a, across(near_sent_a, 4), near_b, across(near_sent_b, 4)]
    output = finish(hidden, gates, flat, near_sums, backs, groups, cap)
    return output.reshape(1, 1, tokens, width)


def solution(mesh):
    return jax.shard_map(
        body,
        mesh=mesh,
        in_specs=(
            P("expert", "pipe", None, None),
            P("expert", "pipe", None, None),
            P("expert", "pipe", None, None),
            P(),
            P(None, "expert"),
            P("expert", None),
            P("expert", "pipe", None),
            P("expert", "pipe", None),
            P("expert", "pipe", None),
        ),
        out_specs=P("expert", "pipe", None, None),
        check_vma=False,
    )
```

```python
import functools
import math

import jax
import jax.numpy as jnp
from jax import lax
from jax.experimental import pallas as pl
from jax.experimental.pallas import tpu as pltpu
from jax.sharding import PartitionSpec as P

HEADS = 16
HD = 128
WSPLIT = 8
EPS = 1e-06
FAR_WEIGHT = 3_000_000_000
FAR_STEPS = 4
CROSS_STEPS = 1
CROSS_WEIGHT = 3_000_000_000
SUM_WEIGHT = 1_000_000_000
BACK_WEIGHT = 3_000_000_000
VMEM_LIMIT = 32 * 1024 * 1024
PART_LIMIT = 60 * 1024 * 1024

VMEM = pl.BlockSpec(memory_space=pltpu.VMEM)
SMEM = pl.BlockSpec(memory_space=pltpu.SMEM)
ANY = pl.BlockSpec(memory_space=pl.ANY)


def struct(shape, dtype=jnp.bfloat16):
    return jax.ShapeDtypeStruct(shape, dtype)


def call(
    kernel, outs, in_specs, name, flops, moved, scratch=(), out_specs=None, aliases=None, limit=VMEM_LIMIT
):
    return pl.pallas_call(
        kernel,
        out_shape=outs,
        in_specs=in_specs,
        out_specs=out_specs or jax.tree.map(lambda _: VMEM, outs),
        scratch_shapes=list(scratch),
        input_output_aliases=aliases or {},
        compiler_params=pltpu.CompilerParams(vmem_limit_bytes=limit),
        cost_estimate=pl.CostEstimate(flops=flops, bytes_accessed=moved, transcendentals=0),
        name=name,
    )


def as_column(row):
    count = row.shape[1]
    down = lax.broadcasted_iota(jnp.int32, (count, count), 0)
    along = lax.broadcasted_iota(jnp.int32, (count, count), 1)
    return jnp.sum(jnp.where(down == along, row, jnp.zeros_like(row)), axis=1, keepdims=True)


def stage_kernel(groups, cap, *refs):
    group_ref, state_in, query_in, gain_in, expert_ref, slot_ref, gate_ref = refs[:7]
    state_out, query_out, gain_out, flat_row, flat_column, gate_column = refs[7:]
    state_out[...] = state_in[...]
    query_out[...] = query_in[...]
    gain_out[...] = gain_in[...]
    offset = expert_ref[...] - group_ref[0]
    offset = jnp.where(offset < 0, offset + groups, offset)
    slot = slot_ref[...]
    flat = jnp.where(slot >= 0, offset * cap + slot, -1)
    flat_row[...] = flat
    flat_column[...] = as_column(flat)
    gate_column[...] = as_column(gate_ref[...])


def stage(group, state, query, gain, expert_id, slot, gate, groups, cap):
    tokens, width = state.shape
    outs = [
        struct((tokens, width)),
        struct((tokens, width)),
        struct((1, width), jnp.float32),
        struct((1, tokens), jnp.int32),
        struct((tokens, 1), jnp.int32),
        struct((tokens, 1), jnp.float32),
    ]
    return call(
        functools.partial(stage_kernel, groups, cap),
        outs,
        [SMEM] + [VMEM] * 6,
        "stage",
        tokens * tokens,
        8 * tokens * width,
    )(group, state, query, gain, expert_id, slot, gate)


def gate_kernel(*refs):
    pass


def after_all(values, others, weight=1):
    return call(
        gate_kernel,
        [struct(value.shape) for value in values],
        [ANY] * (len(values) + len(others)),
        "hand_on",
        weight,
        1,
        out_specs=[ANY] * len(values),
        aliases={i: i for i in range(len(values))},
    )(*values, *others)


def attend_kernel(pieces, groups, cap, *refs):
    state_ref, query_ref, gain_ref, flat_ref = refs[:4]
    kv_refs = refs[4 : 4 + pieces]
    hidden_ref = refs[-1 - groups]
    packed_refs = refs[-groups:]
    tokens, width = state_ref.shape
    local = kv_refs[0].shape[0] // 2
    scale = 1.0 / math.sqrt(HD)
    squares = jnp.zeros((tokens, HD), jnp.float32)
    for head in range(HEADS):
        cols = slice(head * HD, (head + 1) * HD)
        keys = jnp.concatenate([r[:local, cols] for r in kv_refs], axis=0)
        values = jnp.concatenate([r[local:, cols] for r in kv_refs], axis=0)
        scores = (
            lax.dot_general(
                query_ref[:, cols],
                keys,
                (((1,), (1,)), ((), ())),
                preferred_element_type=jnp.float32,
            )
            * scale
        )
        raised = jnp.exp(scores - jnp.max(scores, axis=1, keepdims=True))
        total = jnp.sum(raised, axis=1, keepdims=True)
        mixed = jnp.dot(raised.astype(jnp.bfloat16), values, preferred_element_type=jnp.float32)
        hidden = state_ref[:, cols].astype(jnp.float32) + mixed / total
        hidden_ref[:, cols] = hidden
        squares = squares + hidden * hidden
    mean_square = jnp.sum(squares, axis=1, keepdims=True) * (1.0 / width)
    inverse = lax.rsqrt(mean_square + EPS)
    rows = lax.broadcasted_iota(jnp.int32, (groups * cap, tokens), 0)
    selector = (rows == flat_ref[...]).astype(jnp.float32).astype(jnp.bfloat16)
    step = 512
    for at in range(0, width, step):
        cols = slice(at, at + step)
        normed = (hidden_ref[:, cols] * inverse * gain_ref[:, cols]).astype(jnp.bfloat16)
        packed = jnp.dot(selector, normed, preferred_element_type=jnp.float32).astype(jnp.bfloat16)
        for group in range(groups):
            packed_refs[group][:, cols] = packed[group * cap : (group + 1) * cap]


def attend(state, query, gain, flat, kv_pieces, groups, cap, after):
    tokens, width = state.shape
    outs = [struct((tokens, width), jnp.float32)] + [struct((cap, width))] * groups
    pieces = len(kv_pieces)
    return call(
        functools.partial(attend_kernel, pieces, groups, cap),
        outs,
        [VMEM] * (4 + pieces) + [ANY] * len(after),
        "attend",
        4 * tokens * pieces * kv_pieces[0].shape[0] * width,
        12 * tokens * width,
    )(state, query, gain, flat, *kv_pieces, *after)


def place(pipes, shift, pipe, size):
    at = pipe - shift
    at = jnp.where(at < 0, at + pipes, at)
    return pl.multiple_of(at * size, size)


def part_kernel(stride, first, pipe_ref, whole, part, sem):
    size = part.shape[0]
    at = pl.multiple_of(pipe_ref[0] * stride + first, size)
    copy = pltpu.make_async_copy(whole.at[pl.ds(at, size)], part, sem)
    copy.start()
    copy.wait()


def cut_part(pipe, whole, stride, first, size):
    return call(
        functools.partial(part_kernel, stride, first),
        struct((size, whole.shape[1])),
        [SMEM, ANY],
        "weight_part",
        1,
        4 * size * whole.shape[1],
        scratch=[pltpu.SemaphoreType.DMA],
        limit=PART_LIMIT,
    )(pipe, whole)


def hold_kernel(pipes, pipe_ref, w_in, w_out, *refs):
    in_held, out_held, out_part, out_rest, sems = refs[-5:]
    size = out_part.shape[0]
    at = pl.multiple_of(pipe_ref[0] * size, size)
    copies = [
        pltpu.make_async_copy(source, target, sems.at[i])
        for i, (source, target) in enumerate(
            (
                (w_in, in_held),
                (w_out, out_held),
                (w_out.at[pl.ds(at, size)], out_part),
                (w_out.at[pipes * size :], out_rest),
            )
        )
    ]
    for copy in copies:
        copy.start()
    for copy in copies:
        copy.wait()


def hold(pipe, w_in, w_out, pipes, after):
    units, width = w_out.shape
    size = units * 7 // 12 // pipes // 16 * 16
    return call(
        functools.partial(hold_kernel, pipes),
        [
            struct(w_in.shape),
            struct(w_out.shape),
            struct((size, width)),
            struct((units - pipes * size, width)),
        ],
        [SMEM, ANY, ANY] + [ANY] * len(after),
        "hold_weights",
        1,
        8 * units * width,
        scratch=[pltpu.SemaphoreType.DMA((4,))],
    )(pipe, w_in, w_out, *after)


def up_kernel(own_in, z_in, w_own, w_pair, out_ref):
    entries = jnp.concatenate([own_in[...], z_in[...]], axis=0)
    weights = jnp.concatenate([w_own[...], w_pair[...]], axis=1)
    raw = jnp.dot(entries, weights, preferred_element_type=jnp.float32)
    out_ref[...] = jnp.maximum(raw, 0.0).astype(jnp.bfloat16)


def up(own, z, w_in):
    rows, width = own.shape
    units = w_in[0].shape[1]
    return call(
        up_kernel,
        struct((2 * rows, 2 * units)),
        [VMEM] * 4,
        "expert_up",
        8 * rows * width * units,
        4 * units * width,
    )(own, z, *w_in)


def up_y_kernel(pipes, halves, *refs):
    pipe = refs[0][0]
    act_ref, own_in, z_in = refs[1:4]
    count = pipes * halves
    y_parts = refs[4 : 4 + count]
    pair_parts = refs[4 + count : 4 + 2 * count]
    out_ref, entries = refs[-2:]
    rows, width = own_in.shape
    units = act_ref.shape[1]
    entries[:rows] = own_in[...]
    entries[rows:] = z_in[...]
    out_ref[:, :units] = act_ref[...]
    depth = width // count
    raw = jnp.zeros(act_ref.shape, jnp.float32)
    for i in range(count):
        half, shift = divmod(i, pipes)
        at = place(pipes, shift, pipe, halves * depth) + half * depth
        part = entries[:, pl.ds(pl.multiple_of(at, depth), depth)]
        weights = jnp.concatenate([y_parts[i][...], pair_parts[i][...]], axis=1)
        raw = raw + jnp.dot(part, weights, preferred_element_type=jnp.float32)
    out_ref[:, units:] = jnp.maximum(raw, 0.0).astype(jnp.bfloat16)


def up_y(pipe, act, own, z, y_parts, pair_parts, pipes, after=()):
    rows, width = own.shape
    units = y_parts[0].shape[1]
    count = len(y_parts)
    return call(
        functools.partial(up_y_kernel, pipes, count // pipes),
        struct((2 * rows, 4 * units)),
        [SMEM] + [VMEM] * (3 + 2 * count) + [ANY] * len(after),
        "expert_up_y",
        8 * rows * width * units,
        4 * units * width,
        scratch=[pltpu.VMEM((2 * rows, width), jnp.bfloat16)],
    )(pipe, act, own, z, *y_parts, *pair_parts, *after)


def down_kernel(pipes, first, *refs):
    pipe = refs[0][0]
    act_ref, w_own, w_pair = refs[1:4]
    y_parts, refs = refs[4 : 4 + pipes], refs[4 + pipes :]
    pair_parts, refs = refs[:pipes], refs[pipes:]
    y_rest, pair_rest = refs[:2]
    own_ref, z_ref, held = refs[-3:]
    rows, width = own_ref.shape
    whole = slice(first, first + width)
    units = w_own.shape[0]
    size = y_parts[0].shape[0]
    for shift in range(pipes):
        at = place(pipes, shift, pipe, size)
        held[pl.ds(at, size)] = y_parts[shift][:, whole]
        held[pl.ds(pl.multiple_of(units + at, 16), size)] = pair_parts[shift][:, whole]
    held[pipes * size : units] = y_rest[:, whole]
    held[units + pipes * size :] = pair_rest[:, whole]
    step = 512
    for at in range(0, width, step):
        cols = slice(at, at + step)
        there = slice(first + at, first + at + step)
        weights = jnp.concatenate([w_own[:, there], w_pair[:, there], held[:, cols]], axis=0)
        part = jnp.dot(act_ref[...], weights, preferred_element_type=jnp.float32)
        part = part.astype(jnp.bfloat16)
        own_ref[:, cols] = part[:rows]
        z_ref[:, cols] = part[rows:]


def down(pipe, act, w_out, y_parts, pair_parts, rests, first, width, after=()):
    rows = act.shape[0] // 2
    units = w_out[0].shape[0]
    pipes = len(y_parts)
    return call(
        functools.partial(down_kernel, pipes, first),
        [struct((rows, width))] * 2,
        [SMEM] + [VMEM] * (5 + 2 * pipes) + [ANY] * len(after),
        "expert_down",
        16 * rows * width * units,
        8 * units * width,
        scratch=[pltpu.VMEM((2 * units, width), jnp.bfloat16)],
    )(pipe, act, *w_out, *y_parts, *pair_parts, *rests, *after)


def total_kernel(held, own_ref, z_ref, *refs):
    refs[held][...] = (own_ref[...].astype(jnp.float32) + z_ref[...].astype(jnp.float32)).astype(
        jnp.bfloat16
    )


def total(own, z, held):
    outs = [struct(own.shape)] + [struct(value.shape) for value in held]
    return call(
        functools.partial(total_kernel, len(held)),
        outs,
        [VMEM] * 2 + [ANY] * len(held),
        "far_total",
        own.size,
        6 * own.size,
        out_specs=[VMEM] + [ANY] * len(held),
        aliases={2 + i: 1 + i for i in range(len(held))},
    )(own, z, *held)


def finish_kernel(groups, cap, *refs):
    hidden_ref, gate_ref, flat_ref = refs[:3]
    own_ref, z_ref = refs[3:5]
    back_refs = refs[5:-1]
    out_ref = refs[-1]
    tokens, width = hidden_ref.shape
    slots = lax.broadcasted_iota(jnp.int32, (tokens, groups * cap), 1)
    picker = (slots == flat_ref[...]).astype(jnp.float32).astype(jnp.bfloat16)
    step = 512
    for at in range(0, width, step):
        cols = slice(at, at + step)
        near = (own_ref[:, cols].astype(jnp.float32) + z_ref[:, cols].astype(jnp.float32)).astype(
            jnp.bfloat16
        )
        side, inner = divmod(at, width // 2)
        backs = [r[:, inner : inner + step] for r in back_refs[side::2]]
        found = jnp.concatenate([near, *backs], axis=0)
        picked = jnp.dot(picker, found, preferred_element_type=jnp.float32)
        out_ref[:, cols] = (hidden_ref[:, cols] + gate_ref[...] * picked).astype(jnp.bfloat16)


def finish(hidden, gate, flat, sums, backs, groups, cap):
    tokens, width = hidden.shape
    operands = [hidden, gate, flat, *sums, *backs]
    return call(
        functools.partial(finish_kernel, groups, cap),
        struct((tokens, width)),
        [VMEM] * len(operands),
        "finish",
        4 * tokens * cap * groups * width,
        16 * tokens * width,
    )(*operands)


def body(state, query, enc_kv, gain, w_in, w_out, expert_id, slot, gate):
    tokens, width = state.shape[2:]
    devices = lax.axis_size("expert")
    pipes = lax.axis_size("pipe")
    groups = devices // WSPLIT
    cap = 3 * tokens // (2 * groups)

    def across(value, bit):
        return lax.ppermute(value, "expert", [(i, i ^ bit) for i in range(devices)])

    def groups_on(value, count):
        shift = count * WSPLIT
        return lax.ppermute(value, "expert", [(i, (i + shift) % devices) for i in range(devices)])

    def along(value):
        perms = [[(i, (i + shift) % pipes) for i in range(pipes)] for shift in range(1, pipes)]
        return [value] + [lax.ppermute(value, "pipe", perm) for perm in perms]

    def paired(parts):
        return [across(value, 1) for value in parts]

    pipe = lax.axis_index("pipe").astype(jnp.int32)
    w_in_pair, w_out_pair = across(w_in, 1), across(w_out, 1)
    pipe = pipe.reshape(1)
    depth = width // pipes
    in_y, in_late = (cut_part(pipe, w_in, depth, at, depth // 2) for at in (0, depth // 2))
    kv = jnp.transpose(enc_kv[0], (1, 0, 2)).reshape(-1, width)
    (kv,) = after_all([kv], [in_y])
    kv_pieces = [kv]
    for shift in range(1, pipes):
        perm = [(i, (i + shift) % pipes) for i in range(pipes)]
        kv_pieces.append(lax.ppermute(kv, "pipe", perm))
    in_y = across(in_y, 2)
    in_late = across(*after_all([in_late], kv_pieces[1:2]), 2)

    group = (lax.axis_index("expert") // WSPLIT).astype(jnp.int32).reshape(1)
    staged = stage(
        group,
        state[0, 0],
        query[0, 0],
        gain.reshape(1, width),
        expert_id[0],
        slot[0],
        gate[0],
        groups,
        cap,
    )
    flat, gates = staged[4:]
    hidden, near, *packed = attend(
        *staged[:4], kv_pieces, groups, cap, after=[w_in_pair, w_out_pair]
    )
    far = [groups_on(block, count) for count, block in enumerate(packed, 1)]
    far = jnp.concatenate(far, axis=0) if len(far) > 1 else far[0]

    w_in_held, w_out_held, out_part, out_rest = hold(pipe, w_in, w_out, pipes, [near])
    in_first = along(*after_all([in_y], [out_part]))
    in_last = after_all([in_late], [in_first[0]])
    out_part, out_rest = after_all([out_part, out_rest], in_last)
    in_last = along(*in_last)
    out_y, rest_y = across(out_part, 2), across(out_rest, 2)

    near_z = across(near, 4)
    far = [far]
    for step in range(CROSS_STEPS):
        far = after_all(far, [] if step else [near_z], CROSS_WEIGHT)
    (far,) = far
    far_z = [across(far, 4)]
    in_sent = in_last[-1]
    in_parts = after_all([*in_first, *in_last], far_z)
    for _ in range(FAR_STEPS):
        far_z = after_all(far_z, [], FAR_WEIGHT)
    (far_z,) = far_z

    in_pair = paired(in_parts)

    def experts_up(own, z, after=()):
        act = up(own, z, [w_in_held, w_in_pair])
        return up_y(pipe, act, own, z, in_parts, in_pair, pipes, after)

    far_act = experts_up(far, far_z)
    out_parts = along(*after_all([out_y], [in_sent]))
    out_pair = paired(out_parts[:1])
    *out_parts[1:], rest_y = after_all([*out_parts[1:], rest_y], [far_act, *out_pair])
    out_pair += paired(out_parts[1:])
    rests = [rest_y, across(rest_y, 1)]

    def experts_down(act, first, size, after=()):
        return down(
            pipe, act, [w_out_held, w_out_pair], out_parts, out_pair, rests, first, size, after
        )

    half = width // 2
    far_a, sent_a = experts_down(far_act, 0, half)
    far_b, sent_b = experts_down(far_act, half, half, [far_a])
    near_act = experts_up(near, near_z, [far_b])
    (sent_b,) = after_all([sent_b], [near_act])
    near_own, near_sent = experts_down(near_act, 0, width)
    (sum_a,) = total(far_a, across(sent_a, 4), [])
    sum_b, near_sent = total(far_b, across(sent_b, 4), [near_sent])
    backs = [
        groups_on(side[(count - 1) * cap : count * cap], groups - count)
        for count in range(1, groups)
        for side in (sum_a, sum_b)
    ]
    backs[::2] = after_all(backs[::2], [], SUM_WEIGHT)
    backs[::2] = after_all(backs[::2], [], BACK_WEIGHT)
    near_sums = [near_own, across(near_sent, 4)]
    output = finish(hidden, gates, flat, near_sums, backs, groups, cap)
    return output.reshape(1, 1, tokens, width)


def solution(mesh):
    return jax.shard_map(
        body,
        mesh=mesh,
        in_specs=(
            P("expert", "pipe", None, None),
            P("expert", "pipe", None, None),
            P("expert", "pipe", None, None),
            P(),
            P(None, "expert"),
            P("expert", None),
            P("expert", "pipe", None),
            P("expert", "pipe", None),
            P("expert", "pipe", None),
        ),
        out_specs=P("expert", "pipe", None, None),
        check_vma=False,
    )
```

```python
import functools
import math

import jax
import jax.numpy as jnp
from jax import lax
from jax.experimental import pallas as pl
from jax.experimental.pallas import tpu as pltpu
from jax.sharding import PartitionSpec as P

HEADS = 16
HD = 128
WSPLIT = 8
EPS = 1e-06
FAR_WEIGHT = 3_000_000_000
FAR_STEPS = 4
CROSS_STEPS = 1
CROSS_WEIGHT = 3_000_000_000
SUM_WEIGHT = 1_000_000_000
BACK_WEIGHT = 3_000_000_000
VMEM_LIMIT = 32 * 1024 * 1024
PART_LIMIT = 60 * 1024 * 1024

VMEM = pl.BlockSpec(memory_space=pltpu.VMEM)
SMEM = pl.BlockSpec(memory_space=pltpu.SMEM)
ANY = pl.BlockSpec(memory_space=pl.ANY)


def struct(shape, dtype=jnp.bfloat16):
    return jax.ShapeDtypeStruct(shape, dtype)


def call(
    kernel, outs, in_specs, name, flops, moved, scratch=(), out_specs=None, aliases=None, limit=VMEM_LIMIT
):
    return pl.pallas_call(
        kernel,
        out_shape=outs,
        in_specs=in_specs,
        out_specs=out_specs or jax.tree.map(lambda _: VMEM, outs),
        scratch_shapes=list(scratch),
        input_output_aliases=aliases or {},
        compiler_params=pltpu.CompilerParams(vmem_limit_bytes=limit),
        cost_estimate=pl.CostEstimate(flops=flops, bytes_accessed=moved, transcendentals=0),
        name=name,
    )


def as_column(row):
    count = row.shape[1]
    down = lax.broadcasted_iota(jnp.int32, (count, count), 0)
    along = lax.broadcasted_iota(jnp.int32, (count, count), 1)
    return jnp.sum(jnp.where(down == along, row, jnp.zeros_like(row)), axis=1, keepdims=True)


def stage_kernel(groups, cap, *refs):
    group_ref, state_in, query_in, gain_in, expert_ref, slot_ref, gate_ref = refs[:7]
    state_out, query_out, gain_out, flat_row, flat_column, gate_column = refs[7:]
    state_out[...] = state_in[...]
    query_out[...] = query_in[...]
    gain_out[...] = gain_in[...]
    offset = expert_ref[...] - group_ref[0]
    offset = jnp.where(offset < 0, offset + groups, offset)
    slot = slot_ref[...]
    flat = jnp.where(slot >= 0, offset * cap + slot, -1)
    flat_row[...] = flat
    flat_column[...] = as_column(flat)
    gate_column[...] = as_column(gate_ref[...])


def stage(group, state, query, gain, expert_id, slot, gate, groups, cap):
    tokens, width = state.shape
    outs = [
        struct((tokens, width)),
        struct((tokens, width)),
        struct((1, width), jnp.float32),
        struct((1, tokens), jnp.int32),
        struct((tokens, 1), jnp.int32),
        struct((tokens, 1), jnp.float32),
    ]
    return call(
        functools.partial(stage_kernel, groups, cap),
        outs,
        [SMEM] + [VMEM] * 6,
        "stage",
        tokens * tokens,
        8 * tokens * width,
    )(group, state, query, gain, expert_id, slot, gate)


def gate_kernel(*refs):
    pass


def after_all(values, others, weight=1):
    return call(
        gate_kernel,
        [struct(value.shape) for value in values],
        [ANY] * (len(values) + len(others)),
        "hand_on",
        weight,
        1,
        out_specs=[ANY] * len(values),
        aliases={i: i for i in range(len(values))},
    )(*values, *others)


def attend_kernel(pieces, groups, cap, *refs):
    state_ref, query_ref, gain_ref, flat_ref = refs[:4]
    kv_refs = refs[4 : 4 + pieces]
    hidden_ref = refs[-1 - groups]
    packed_refs = refs[-groups:]
    tokens, width = state_ref.shape
    local = kv_refs[0].shape[0] // 2
    scale = 1.0 / math.sqrt(HD)
    squares = jnp.zeros((tokens, HD), jnp.float32)
    for head in range(HEADS):
        cols = slice(head * HD, (head + 1) * HD)
        keys = jnp.concatenate([r[:local, cols] for r in kv_refs], axis=0)
        values = jnp.concatenate([r[local:, cols] for r in kv_refs], axis=0)
        scores = (
            lax.dot_general(
                query_ref[:, cols],
                keys,
                (((1,), (1,)), ((), ())),
                preferred_element_type=jnp.float32,
            )
            * scale
        )
        raised = jnp.exp(scores - jnp.max(scores, axis=1, keepdims=True))
        total = jnp.sum(raised, axis=1, keepdims=True)
        mixed = jnp.dot(raised.astype(jnp.bfloat16), values, preferred_element_type=jnp.float32)
        hidden = state_ref[:, cols].astype(jnp.float32) + mixed / total
        hidden_ref[:, cols] = hidden
        squares = squares + hidden * hidden
    mean_square = jnp.sum(squares, axis=1, keepdims=True) * (1.0 / width)
    inverse = lax.rsqrt(mean_square + EPS)
    rows = lax.broadcasted_iota(jnp.int32, (groups * cap, tokens), 0)
    selector = (rows == flat_ref[...]).astype(jnp.float32).astype(jnp.bfloat16)
    step = 512
    for at in range(0, width, step):
        cols = slice(at, at + step)
        normed = (hidden_ref[:, cols] * inverse * gain_ref[:, cols]).astype(jnp.bfloat16)
        packed = jnp.dot(selector, normed, preferred_element_type=jnp.float32).astype(jnp.bfloat16)
        for group in range(groups):
            packed_refs[group][:, cols] = packed[group * cap : (group + 1) * cap]


def attend(state, query, gain, flat, kv_pieces, groups, cap, after):
    tokens, width = state.shape
    outs = [struct((tokens, width), jnp.float32)] + [struct((cap, width))] * groups
    pieces = len(kv_pieces)
    return call(
        functools.partial(attend_kernel, pieces, groups, cap),
        outs,
        [VMEM] * (4 + pieces) + [ANY] * len(after),
        "attend",
        4 * tokens * pieces * kv_pieces[0].shape[0] * width,
        12 * tokens * width,
    )(state, query, gain, flat, *kv_pieces, *after)


def place(pipes, shift, pipe, size):
    at = pipe - shift
    at = jnp.where(at < 0, at + pipes, at)
    return pl.multiple_of(at * size, size)


def part_kernel(stride, first, pipe_ref, whole, part, sem):
    size = part.shape[0]
    at = pl.multiple_of(pipe_ref[0] * stride + first, size)
    copy = pltpu.make_async_copy(whole.at[pl.ds(at, size)], part, sem)
    copy.start()
    copy.wait()


def cut_part(pipe, whole, stride, first, size):
    return call(
        functools.partial(part_kernel, stride, first),
        struct((size, whole.shape[1])),
        [SMEM, ANY],
        "weight_part",
        1,
        4 * size * whole.shape[1],
        scratch=[pltpu.SemaphoreType.DMA],
        limit=PART_LIMIT,
    )(pipe, whole)


def hold_kernel(pipes, pipe_ref, w_in, w_out, *refs):
    in_held, out_held, out_part, out_rest, sems = refs[-5:]
    size = out_part.shape[0]
    at = pl.multiple_of(pipe_ref[0] * size, size)
    copies = [
        pltpu.make_async_copy(source, target, sems.at[i])
        for i, (source, target) in enumerate(
            (
                (w_in, in_held),
                (w_out, out_held),
                (w_out.at[pl.ds(at, size)], out_part),
                (w_out.at[pipes * size :], out_rest),
            )
        )
    ]
    for copy in copies:
        copy.start()
    for copy in copies:
        copy.wait()


def hold(pipe, w_in, w_out, pipes, after):
    units, width = w_out.shape
    size = units * 7 // 12 // pipes // 16 * 16
    return call(
        functools.partial(hold_kernel, pipes),
        [
            struct(w_in.shape),
            struct(w_out.shape),
            struct((size, width)),
            struct((units - pipes * size, width)),
        ],
        [SMEM, ANY, ANY] + [ANY] * len(after),
        "hold_weights",
        1,
        8 * units * width,
        scratch=[pltpu.SemaphoreType.DMA((4,))],
    )(pipe, w_in, w_out, *after)


def up_kernel(own_in, z_in, w_own, w_pair, out_ref):
    entries = jnp.concatenate([own_in[...], z_in[...]], axis=0)
    weights = jnp.concatenate([w_own[...], w_pair[...]], axis=1)
    raw = jnp.dot(entries, weights, preferred_element_type=jnp.float32)
    out_ref[...] = jnp.maximum(raw, 0.0).astype(jnp.bfloat16)


def up(own, z, w_in):
    rows, width = own.shape
    units = w_in[0].shape[1]
    return call(
        up_kernel,
        struct((2 * rows, 2 * units)),
        [VMEM] * 4,
        "expert_up",
        8 * rows * width * units,
        4 * units * width,
    )(own, z, *w_in)


def up_y_kernel(pipes, halves, *refs):
    pipe = refs[0][0]
    act_ref, own_in, z_in = refs[1:4]
    count = pipes * halves
    y_parts = refs[4 : 4 + count]
    pair_parts = refs[4 + count : 4 + 2 * count]
    out_ref, entries = refs[-2:]
    rows, width = own_in.shape
    units = act_ref.shape[1]
    entries[:rows] = own_in[...]
    entries[rows:] = z_in[...]
    out_ref[:, :units] = act_ref[...]
    depth = width // count
    raw = jnp.zeros(act_ref.shape, jnp.float32)
    for i in range(count):
        half, shift = divmod(i, pipes)
        at = place(pipes, shift, pipe, halves * depth) + half * depth
        part = entries[:, pl.ds(pl.multiple_of(at, depth), depth)]
        weights = jnp.concatenate([y_parts[i][...], pair_parts[i][...]], axis=1)
        raw = raw + jnp.dot(part, weights, preferred_element_type=jnp.float32)
    out_ref[:, units:] = jnp.maximum(raw, 0.0).astype(jnp.bfloat16)


def up_y(pipe, act, own, z, y_parts, pair_parts, pipes, after=()):
    rows, width = own.shape
    units = y_parts[0].shape[1]
    count = len(y_parts)
    return call(
        functools.partial(up_y_kernel, pipes, count // pipes),
        struct((2 * rows, 4 * units)),
        [SMEM] + [VMEM] * (3 + 2 * count) + [ANY] * len(after),
        "expert_up_y",
        8 * rows * width * units,
        4 * units * width,
        scratch=[pltpu.VMEM((2 * rows, width), jnp.bfloat16)],
    )(pipe, act, own, z, *y_parts, *pair_parts, *after)


def down_kernel(pipes, first, *refs):
    pipe = refs[0][0]
    act_ref, w_own, w_pair = refs[1:4]
    y_parts, refs = refs[4 : 4 + pipes], refs[4 + pipes :]
    pair_parts, refs = refs[:pipes], refs[pipes:]
    y_rest, pair_rest = refs[:2]
    own_ref, z_ref, held = refs[-3:]
    rows, width = own_ref.shape
    whole = slice(first, first + width)
    units = w_own.shape[0]
    size = y_parts[0].shape[0]
    for shift in range(pipes):
        at = place(pipes, shift, pipe, size)
        held[pl.ds(at, size)] = y_parts[shift][:, whole]
        held[pl.ds(pl.multiple_of(units + at, 16), size)] = pair_parts[shift][:, whole]
    held[pipes * size : units] = y_rest[:, whole]
    held[units + pipes * size :] = pair_rest[:, whole]
    step = 512
    for at in range(0, width, step):
        cols = slice(at, at + step)
        there = slice(first + at, first + at + step)
        weights = jnp.concatenate([w_own[:, there], w_pair[:, there], held[:, cols]], axis=0)
        part = jnp.dot(act_ref[...], weights, preferred_element_type=jnp.float32)
        part = part.astype(jnp.bfloat16)
        own_ref[:, cols] = part[:rows]
        z_ref[:, cols] = part[rows:]


def down(pipe, act, w_out, y_parts, pair_parts, rests, first, width, after=()):
    rows = act.shape[0] // 2
    units = w_out[0].shape[0]
    pipes = len(y_parts)
    return call(
        functools.partial(down_kernel, pipes, first),
        [struct((rows, width))] * 2,
        [SMEM] + [VMEM] * (5 + 2 * pipes) + [ANY] * len(after),
        "expert_down",
        16 * rows * width * units,
        8 * units * width,
        scratch=[pltpu.VMEM((2 * units, width), jnp.bfloat16)],
    )(pipe, act, *w_out, *y_parts, *pair_parts, *rests, *after)


def total_kernel(held, own_ref, z_ref, *refs):
    refs[held][...] = (own_ref[...].astype(jnp.float32) + z_ref[...].astype(jnp.float32)).astype(
        jnp.bfloat16
    )


def total(own, z, held):
    outs = [struct(own.shape)] + [struct(value.shape) for value in held]
    return call(
        functools.partial(total_kernel, len(held)),
        outs,
        [VMEM] * 2 + [ANY] * len(held),
        "far_total",
        own.size,
        6 * own.size,
        out_specs=[VMEM] + [ANY] * len(held),
        aliases={2 + i: 1 + i for i in range(len(held))},
    )(own, z, *held)


def finish_kernel(groups, cap, *refs):
    hidden_ref, gate_ref, flat_ref = refs[:3]
    own_ref, z_ref = refs[3:5]
    back_refs = refs[5:-1]
    out_ref = refs[-1]
    tokens, width = hidden_ref.shape
    slots = lax.broadcasted_iota(jnp.int32, (tokens, groups * cap), 1)
    picker = (slots == flat_ref[...]).astype(jnp.float32).astype(jnp.bfloat16)
    step = 512
    for at in range(0, width, step):
        cols = slice(at, at + step)
        near = (own_ref[:, cols].astype(jnp.float32) + z_ref[:, cols].astype(jnp.float32)).astype(
            jnp.bfloat16
        )
        side, inner = divmod(at, width // 2)
        backs = [r[:, inner : inner + step] for r in back_refs[side::2]]
        found = jnp.concatenate([near, *backs], axis=0)
        picked = jnp.dot(picker, found, preferred_element_type=jnp.float32)
        out_ref[:, cols] = (hidden_ref[:, cols] + gate_ref[...] * picked).astype(jnp.bfloat16)


def finish(hidden, gate, flat, sums, backs, groups, cap):
    tokens, width = hidden.shape
    operands = [hidden, gate, flat, *sums, *backs]
    return call(
        functools.partial(finish_kernel, groups, cap),
        struct((tokens, width)),
        [VMEM] * len(operands),
        "finish",
        4 * tokens * cap * groups * width,
        16 * tokens * width,
    )(*operands)


def body(state, query, enc_kv, gain, w_in, w_out, expert_id, slot, gate):
    tokens, width = state.shape[2:]
    devices = lax.axis_size("expert")
    pipes = lax.axis_size("pipe")
    groups = devices // WSPLIT
    cap = 3 * tokens // (2 * groups)

    def across(value, bit):
        return lax.ppermute(value, "expert", [(i, i ^ bit) for i in range(devices)])

    def groups_on(value, count):
        shift = count * WSPLIT
        return lax.ppermute(value, "expert", [(i, (i + shift) % devices) for i in range(devices)])

    def along(value):
        perms = [[(i, (i + shift) % pipes) for i in range(pipes)] for shift in range(1, pipes)]
        return [value] + [lax.ppermute(value, "pipe", perm) for perm in perms]

    def paired(parts):
        return [across(value, 1) for value in parts]

    pipe = lax.axis_index("pipe").astype(jnp.int32)
    w_in_pair, w_out_pair = across(w_in, 1), across(w_out, 1)
    pipe = pipe.reshape(1)
    depth = width // pipes
    in_y, in_late = (cut_part(pipe, w_in, depth, at, depth // 2) for at in (0, depth // 2))
    kv = jnp.transpose(enc_kv[0], (1, 0, 2)).reshape(-1, width)
    (kv,) = after_all([kv], [in_y])
    kv_pieces = [kv]
    for shift in range(1, pipes):
        perm = [(i, (i + shift) % pipes) for i in range(pipes)]
        kv_pieces.append(lax.ppermute(kv, "pipe", perm))
    in_y = across(in_y, 2)
    in_late = across(*after_all([in_late], kv_pieces[1:2]), 2)

    group = (lax.axis_index("expert") // WSPLIT).astype(jnp.int32).reshape(1)
    staged = stage(
        group,
        state[0, 0],
        query[0, 0],
        gain.reshape(1, width),
        expert_id[0],
        slot[0],
        gate[0],
        groups,
        cap,
    )
    flat, gates = staged[4:]
    hidden, near, *packed = attend(
        *staged[:4], kv_pieces, groups, cap, after=[w_in_pair, w_out_pair]
    )
    far = [groups_on(block, count) for count, block in enumerate(packed, 1)]
    far = jnp.concatenate(far, axis=0) if len(far) > 1 else far[0]

    in_first = along(*after_all([in_y], [near]))
    w_in_held, w_out_held, out_part, out_rest = hold(pipe, w_in, w_out, pipes, in_first[:1])
    in_last = after_all([in_late], [in_first[0], out_part])
    out_part, out_rest = after_all([out_part, out_rest], in_last)
    in_last = along(*in_last)
    out_y, rest_y = across(out_part, 2), across(out_rest, 2)

    near_z = across(near, 4)
    far = [far]
    for step in range(CROSS_STEPS):
        far = after_all(far, [] if step else [near_z], CROSS_WEIGHT)
    (far,) = far
    far_z = [across(far, 4)]
    in_sent = in_last[-1]
    in_parts = after_all([*in_first, *in_last], far_z)
    for _ in range(FAR_STEPS):
        far_z = after_all(far_z, [], FAR_WEIGHT)
    (far_z,) = far_z

    in_pair = paired(in_parts)

    def experts_up(own, z, after=()):
        act = up(own, z, [w_in_held, w_in_pair])
        return up_y(pipe, act, own, z, in_parts, in_pair, pipes, after)

    far_act = experts_up(far, far_z)
    out_parts = along(*after_all([out_y], [in_sent]))
    out_pair = paired(out_parts[:1])
    *out_parts[1:], rest_y = after_all([*out_parts[1:], rest_y], [far_act, *out_pair])
    out_pair += paired(out_parts[1:])
    rests = [rest_y, across(rest_y, 1)]

    def experts_down(act, first, size, after=()):
        return down(
            pipe, act, [w_out_held, w_out_pair], out_parts, out_pair, rests, first, size, after
        )

    half = width // 2
    far_a, sent_a = experts_down(far_act, 0, half)
    far_b, sent_b = experts_down(far_act, half, half, [far_a])
    near_act = experts_up(near, near_z, [far_b])
    (sent_b,) = after_all([sent_b], [near_act])
    near_own, near_sent = experts_down(near_act, 0, width)
    (sum_a,) = total(far_a, across(sent_a, 4), [])
    sum_b, near_sent = total(far_b, across(sent_b, 4), [near_sent])
    backs = [
        groups_on(side[(count - 1) * cap : count * cap], groups - count)
        for count in range(1, groups)
        for side in (sum_a, sum_b)
    ]
    backs[::2] = after_all(backs[::2], [], SUM_WEIGHT)
    backs[::2] = after_all(backs[::2], [], BACK_WEIGHT)
    near_sums = [near_own, across(near_sent, 4)]
    output = finish(hidden, gates, flat, near_sums, backs, groups, cap)
    return output.reshape(1, 1, tokens, width)


def solution(mesh):
    return jax.shard_map(
        body,
        mesh=mesh,
        in_specs=(
            P("expert", "pipe", None, None),
            P("expert", "pipe", None, None),
            P("expert", "pipe", None, None),
            P(),
            P(None, "expert"),
            P("expert", None),
            P("expert", "pipe", None),
            P("expert", "pipe", None),
            P("expert", "pipe", None),
        ),
        out_specs=P("expert", "pipe", None, None),
        check_vma=False,
    )
```
